32 devices in a mesh: exp: 16 (over z, y, x), head: 2 (over core).
Axes of the slice: x: 2, y: 2, z: 4, core: 2. Of those that a mesh axis runs over, the one named last changes fastest.
Arguments:
- block_input: bfloat16 [10240, 1024], P(('exp', 'head')), may hold values from -6 to 6
- dispatch: int32 [8192], P(('exp', 'head')), may hold values from 0 to 319, as said below
- lengths: int32 [16, 5], P('exp'), may hold values from 64 to 256, as said below
- ln1_gain: float32 [1024], replicated, may hold values from 0.5 to 1.5
- ln1_bias: float32 [1024], replicated, may hold values from -2 to 2
- ln2_gain: float32 [1024], replicated, may hold values from 0.5 to 1.5
- ln2_bias: float32 [1024], replicated, may hold values from -2 to 2
- w_qkv: bfloat16 [3, 1024, 1024], P(None, None, 'head'), may hold values from -0.1875 to 0.1875
- w_out: bfloat16 [1024, 1024], P('head'), may hold values from -1.5 to 1.5
- w_up: bfloat16 [16, 1024, 4096], P('exp', None, 'head'), may hold values from -0.1875 to 0.1875
- w_down: bfloat16 [16, 4096, 1024], P('exp', 'head'), may hold values from -0.09375 to 0.09375
- grad_output: bfloat16 [10240, 1024], P(('exp', 'head')), may hold values from -6 to 6
Outputs:
- block_output: bfloat16 [10240, 1024], P(('exp', 'head'))
- grad_input: float32 [10240, 1024], P(('exp', 'head'))
- grad_ln1_gain: float32 [1024], replicated
- grad_ln1_bias: float32 [1024], replicated
- grad_ln2_gain: float32 [1024], replicated
- grad_ln2_bias: float32 [1024], replicated
- grad_w_qkv: float32 [3, 1024, 1024], P(None, None, 'head')
- grad_w_out: float32 [1024, 1024], P('head')
- grad_w_up: float32 [16, 1024, 4096], P('exp', None, 'head')
- grad_w_down: float32 [16, 4096, 1024], P('exp', 'head')
The draws below stay inside these ranges and needn't reach their ends.
Inputs may be any that keep to these rules, and one draw needn't show every extreme that they name: `dispatch`: on each device's 256 tokens the values are distinct; value d sends the token to expert-order device d // 10, and the values one device sends to one destination are that destination's block start plus 0, 1, 2 and so on without gaps. In every draw one destination gets 10 tokens from every device. `lengths`: each row holds one sequence of 256 tokens, neither first nor last, and four sequences of 64 tokens.
All inputs are finite; a program needn't handle non-finite values.
Results may differ from the reference program's by a relative error of at most 0.015.
Values may be sent and summed in bfloat16 or wider, within the bound.
No kernel may reach another device: no remote copies, remote signals or barrier semaphores. Data moves between devices by JAX's collectives and lax.ppermute only.
A program may use at most 128 MiB of HBM per device.

```python
import math
import jax
import jax.numpy as jnp
from jax import lax

D = 1024
HEADS = 16
HEAD_DIM = 64
FF = 4096
SEQ_ROWS = 256
SEQS = 5
EXPERTS = 16
PAIR_CAP = 10
SLOTS = 320
TOTAL_SLOTS = 10240
TOKENS = 8192
N_EXP = 16
N_HEAD = 2


def draw_dispatch(key, part):
    key = jax.random.fold_in(key, 11)
    devices = N_EXP * N_HEAD
    candidates = devices * PAIR_CAP
    key_dest, key_bias, key_source = jax.random.split(key, 3)
    full_dest = jax.random.randint(key_dest, (), 0, devices)
    weights = jax.random.randint(key_bias, (devices,), 0, 2 ** 15)
    index = jnp.arange(candidates, dtype=jnp.int32).reshape(devices, PAIR_CAP)
    dest_ids = jnp.arange(devices, dtype=jnp.int32)

    def one_source(source_key):
        key_score, key_order = jax.random.split(source_key)
        raw = jax.random.randint(key_score, (devices, PAIR_CAP), 0, 2 ** 16)
        score = lax.cummin(raw, axis=1) + weights[:, None]
        score = jnp.where((dest_ids == full_dest)[:, None], 2 ** 17, score)
        keyed = score * candidates + (candidates - 1 - index)
        ignored, chosen = lax.top_k(keyed.reshape(-1), SEQ_ROWS)
        order = jax.random.permutation(key_order, SEQ_ROWS)
        return chosen[order].astype(jnp.int32)
    return jax.vmap(one_source)(jax.random.split(key_source, devices)).reshape(-1)


def draw_lengths(key, part):
    key = jax.random.fold_in(key, 23)
    place = jax.random.randint(key, (N_EXP,), 1, SEQS - 1)
    slot = jnp.arange(SEQS, dtype=jnp.int32)
    short = SEQ_ROWS * (N_HEAD - 1) // (SEQS - 1)
    return jnp.where(slot[None, :] == place[:, None], SEQ_ROWS, short).astype(jnp.int32)


def steps_of(stream_key, extent, cuts, smallest, largest):
    loudness, own = 1.0, jax.random.fold_in(stream_key, 6)
    for position, shards_of in cuts:
        heights = jnp.exp(jax.random.uniform(jax.random.fold_in(own, position), (shards_of,), jnp.float32, smallest / len(cuts), largest / len(cuts)))
        loudness = loudness * jnp.repeat(heights, extent[position] // shards_of).reshape([-1 if axis == position else 1 for axis in range(len(extent))])
    return loudness


def noise(own_key, extent, scale, bound, pieces=(), kind=jnp.bfloat16):
    loudness = steps_of(own_key, extent, pieces, -0.22, 0.18) if pieces else 1.0
    drawn = jax.random.normal(own_key, extent, jnp.float32) * scale * loudness
    return jnp.minimum(jnp.maximum(drawn, -bound), bound).astype(kind)


def setup_inputs(seed: int = 0) -> dict:
    key_list = jax.random.split(jax.random.key(seed), 13)
    block_input = noise(key_list[0], (TOTAL_SLOTS, D), 1.0, 6.0, ((0, 32),))
    dispatch = draw_dispatch(jax.random.fold_in(key_list[12], 71), 0)
    lengths = draw_lengths(jax.random.fold_in(key_list[12], 71), 0)
    ln1_gain = jnp.clip(1.0 + 0.1 * jax.random.normal(key_list[3], (D,), jnp.float32), 0.5, 1.5)
    ln1_bias = noise(key_list[4], (D,), 0.3, 2.0, (), jnp.float32)
    ln2_gain = jnp.clip(1.0 + 0.1 * jax.random.normal(key_list[5], (D,), jnp.float32), 0.5, 1.5)
    ln2_bias = noise(key_list[6], (D,), 0.3, 2.0, (), jnp.float32)
    w_qkv = noise(key_list[7], (3, D, D), D ** -0.5, 0.1875, ((2, 2),))
    w_out = noise(key_list[8], (D, D), (D // 64) ** -0.5, 1.5, ((0, 2),))
    w_up = noise(key_list[9], (EXPERTS, D, FF), D ** -0.5, 0.1875, ((0, 16), (2, 2)))
    w_down = noise(key_list[10], (EXPERTS, FF, D), FF ** -0.5, 0.09375, ((0, 16), (1, 2)))
    grad_output = noise(key_list[11], (TOTAL_SLOTS, D), 1.0, 6.0, ((0, 32),))
    return dict(block_input=block_input, dispatch=dispatch, lengths=lengths, ln1_gain=ln1_gain, ln1_bias=ln1_bias, ln2_gain=ln2_gain, ln2_bias=ln2_bias, w_qkv=w_qkv, w_out=w_out, w_up=w_up, w_down=w_down, grad_output=grad_output)


@jax.custom_vjp
def low(v):
    return lax.optimization_barrier(v.astype(jnp.bfloat16)).astype(jnp.float32)

@jax.custom_vjp
def low_back(v):
    return v

def low_keep(v):
    return (low(v), None)

def low_pass(kept, grad):
    return (grad,)

def back_keep(v):
    return (v, None)

def back_low(kept, grad):
    return (low(grad),)
low.defvjp(low_keep, low_pass)
low_back.defvjp(back_keep, back_low)

def layer_norm(rows, gain, bias):
    mean = lax.optimization_barrier(jnp.mean(rows, axis=1, keepdims=True))
    centred = rows - mean
    variance = lax.optimization_barrier(jnp.mean(centred * centred, axis=1, keepdims=True))
    return centred * lax.rsqrt(variance + 1e-05) * gain + bias

def chip_attention(rows, chip_lengths, w_qkv, w_out):
    span = rows.shape[0]
    qkv = low(low_back(jnp.einsum('rd,tde->tre', rows, w_qkv, precision=lax.Precision.HIGHEST)))
    qkv = qkv.reshape(3, span, HEADS, HEAD_DIM)
    ends = jnp.cumsum(chip_lengths).astype(jnp.int32)
    places = jnp.arange(span).astype(jnp.int32)
    seg = lax.optimization_barrier(jnp.sum((places[:, None] >= ends[None, :]).astype(jnp.int32), axis=1))
    allowed = (seg[:, None] == seg[None, :]) & (places[None, :] <= places[:, None])
    scores = jnp.einsum('qhe,khe->hqk', qkv[0], qkv[1], precision=lax.Precision.HIGHEST) * (1.0 / math.sqrt(HEAD_DIM))
    scores = low_back(jnp.where(allowed[None], scores, -1e+30))
    probs = low(jax.nn.softmax(scores, axis=2))
    context = jnp.einsum('hqk,khe->qhe', probs, qkv[2], precision=lax.Precision.HIGHEST).reshape(span, HEADS * HEAD_DIM)
    context = low(low_back(context))
    return low(low_back(jnp.dot(context, w_out, precision=lax.Precision.HIGHEST)))

def expert_ffn(rows, w_up, w_down):
    pre = low_back(jnp.dot(rows, w_up, precision=lax.Precision.HIGHEST))
    return jnp.dot(low(jax.nn.gelu(pre)), w_down, precision=lax.Precision.HIGHEST)

def forward(block_input, ln1_gain, ln1_bias, ln2_gain, ln2_bias, w_qkv, w_out, w_up, w_down, row_index, lengths, valid):
    h1 = low(low_back(layer_norm(block_input, ln1_gain, ln1_bias)))
    chips = h1[row_index].reshape(N_EXP, N_HEAD * SEQ_ROWS, D)
    attend = jax.checkpoint(lambda pair: chip_attention(pair[0], pair[1], w_qkv, w_out))
    attn = lax.map(attend, (chips, lengths)).reshape(TOKENS, D)
    resid = block_input + jnp.zeros_like(block_input).at[row_index].set(attn)
    h2 = low(layer_norm(resid, ln2_gain, ln2_bias))
    groups = h2.reshape(N_EXP, N_HEAD * SLOTS, D)
    experts = jax.checkpoint(lambda trio: expert_ffn(trio[0], trio[1], trio[2]))
    branch = lax.map(experts, (groups, w_up, w_down)).reshape(TOTAL_SLOTS, D)
    return resid + valid[:, None] * branch

def reference(block_input, dispatch, lengths, ln1_gain, ln1_bias, ln2_gain, ln2_bias, w_qkv, w_out, w_up, w_down, grad_output):
    source = (jnp.arange(TOKENS) // SEQ_ROWS).astype(jnp.int32)
    row_index = (dispatch // PAIR_CAP * SLOTS + source * PAIR_CAP + dispatch % PAIR_CAP).astype(jnp.int32)
    valid = jnp.zeros((TOTAL_SLOTS,), jnp.float32).at[row_index].set(1.0)
    params = tuple((value.astype(jnp.float32) for value in (block_input, ln1_gain, ln1_bias, ln2_gain, ln2_bias, w_qkv, w_out, w_up, w_down)))

    def run(*values):
        return forward(*values, row_index, lengths, valid)
    result, pull = jax.vjp(run, *params)
    grads = pull(grad_output.astype(jnp.float32))
    return (result.astype(jnp.bfloat16), grads[0], grads[1], grads[2], grads[3], grads[4], grads[5], grads[6], grads[7], grads[8])
```

```python
import functools
import math

import jax
import jax.numpy as jnp
from jax import lax
from jax.experimental import pallas as pl
from jax.experimental.pallas import tpu as pltpu
from jax.sharding import PartitionSpec as P

HEAD_DIM = 64
EPS = 1e-05
BF16 = jnp.bfloat16
F32 = jnp.float32
MIB = 1024 * 1024
EMPTY = 1e30


def dot(left, right):
    return lax.dot_general(left, right, (((1,), (0,)), ((), ())), preferred_element_type=F32)


def dot_nt(left, right):
    return lax.dot_general(left, right, (((1,), (1,)), ((), ())), preferred_element_type=F32)


def dot_tn(left, right):
    return lax.dot_general(left, right, (((0,), (0,)), ((), ())), preferred_element_type=F32)


def normalise(rows):
    mean = jnp.mean(rows, axis=1, keepdims=True)
    centred = rows - mean
    inverse = lax.rsqrt(jnp.mean(centred * centred, axis=1, keepdims=True) + EPS)
    return centred * inverse, inverse


def norm_back(upstream, normed, inverse, gain):
    scaled = upstream * gain
    first = jnp.mean(scaled, axis=1, keepdims=True)
    second = jnp.mean(scaled * normed, axis=1, keepdims=True)
    return inverse * (scaled - first - normed * second)


def pack(out_ref, rows, slot_of, cap, fill):
    total, width = out_ref.shape[0], rows.shape[1]
    place = lax.broadcasted_iota(jnp.int32, (total, slot_of.shape[1]), 0)
    first = (place >> 3) * cap
    sub = lax.broadcasted_iota(jnp.int32, (total, 128), 0) & 7
    piece = width // 8

    def placed(target):
        hit = (slot_of == target).astype(F32)
        moved = dot(hit.astype(BF16), rows)
        if fill:
            moved = moved + (1.0 - jnp.sum(hit, axis=1, keepdims=True)) * EMPTY
        return moved

    whole = cap // 8
    for group in range(whole):
        moved = placed(first + (place & 7) + group * 8)
        out_ref[:, group * width : (group + 1) * width] = moved.astype(BF16)
    for left in range(cap % 8):
        moved = placed(first + whole * 8 + left)
        folded = moved[:, :piece]
        for s in range(1, 8):
            folded = jnp.where(sub == s, moved[:, s * piece : (s + 1) * piece], folded)
        start = whole * width + left * piece
        out_ref[:, start : start + piece] = folded.astype(BF16)


def unpack(packed_ref, slot_of, cap, width):
    total = packed_ref.shape[0]
    place = lax.broadcasted_iota(jnp.int32, (slot_of.shape[0], total), 1)
    first = (place >> 3) * cap
    piece = width // 8
    sub = lax.broadcasted_iota(jnp.int32, (total, piece), 0) & 7
    whole = cap // 8
    rows = None
    for group in range(whole):
        hit = (slot_of == first + (place & 7) + group * 8).astype(BF16)
        part = dot(hit, packed_ref[:, group * width : (group + 1) * width])
        rows = part if rows is None else rows + part
    for left in range(cap % 8):
        start = whole * width + left * piece
        folded = packed_ref[:, start : start + piece].astype(F32)
        spread = jnp.concatenate(
            [jnp.where(sub == s, folded, 0.0).astype(BF16) for s in range(8)], axis=1
        )
        hit = (slot_of == first + whole * 8 + left).astype(BF16)
        part = dot(hit, spread)
        rows = part if rows is None else rows + part
    return rows


def slots_down(count):
    return lax.broadcasted_iota(jnp.int32, (count, 1), 0)


def norm1_kernel(x_ref, gain_ref, bias_ref, out_ref, *, cap):
    normed, _ = normalise(x_ref[...].astype(F32))
    rows = (normed * gain_ref[...] + bias_ref[...]).astype(BF16)
    slot_of = lax.broadcasted_iota(jnp.int32, (1, rows.shape[0]), 1)
    pack(out_ref, rows, slot_of, cap, False)


def gather_kernel(packed_ref, dispatch_ref, out_ref, *, cap):
    out_ref[...] = unpack(packed_ref, dispatch_ref[...], cap, out_ref.shape[1]).astype(BF16)


def segments(lengths_ref, places):
    seg = jnp.zeros(places.shape, jnp.int32)
    end = 0
    for index in range(lengths_ref.shape[1]):
        end = end + lengths_ref[0, index]
        seg = seg + (places >= end).astype(jnp.int32)
    return seg


def attend_kernel(
    where_ref,
    lengths_ref,
    own_ref,
    other_ref,
    w_qkv_ref,
    w_out_ref,
    input_ref,
    qkv_ref,
    context_ref,
    logsum_ref,
    kept_ref,
    sent_ref,
    *,
    step,
    reach,
    scale,
):
    half = own_ref.shape[0]
    span = 2 * half
    here = where_ref[0]
    own_start = pl.multiple_of(here * half, half)
    other_start = pl.multiple_of((1 - here) * half, half)
    input_ref[pl.ds(own_start, half), :] = own_ref[...]
    input_ref[pl.ds(other_start, half), :] = other_ref[...]
    for which in range(3):
        qkv_ref[which] = dot(input_ref[...], w_qkv_ref[which]).astype(BF16)
    heads = qkv_ref.shape[2] // HEAD_DIM
    for start in range(0, span, step):
        stop = start + step
        low = max(0, start - reach)
        shape = (step, stop - low)
        query_at = lax.broadcasted_iota(jnp.int32, shape, 0) + start
        key_at = lax.broadcasted_iota(jnp.int32, shape, 1) + low
        allowed = (segments(lengths_ref, query_at) == segments(lengths_ref, key_at)) & (
            key_at <= query_at
        )
        lane = lax.broadcasted_iota(jnp.int32, (step, 2 * HEAD_DIM), 1)
        logsums = jnp.zeros((step, 128), F32)
        logsum_lane = lax.broadcasted_iota(jnp.int32, (step, 128), 1)
        for pair in range(heads // 2):
            columns = slice(pair * 2 * HEAD_DIM, (pair + 1) * 2 * HEAD_DIM)
            query = qkv_ref[0, start:stop, columns]
            keys = qkv_ref[1, low:stop, columns]
            values = qkv_ref[2, low:stop, columns]
            contexts = []
            for inner in range(2):
                mine = (lane < HEAD_DIM) if inner == 0 else (lane >= HEAD_DIM)
                scores = dot_nt(jnp.where(mine, query, jnp.zeros_like(query)), keys) * scale
                scores = jnp.where(allowed, scores, -1e30)
                top = jnp.max(scores, axis=1, keepdims=True)
                expo = jnp.exp(scores - top)
                total = jnp.sum(expo, axis=1, keepdims=True)
                probs = (expo * (1.0 / total)).astype(BF16)
                contexts.append(dot(probs, values))
                logsums = jnp.where(
                    logsum_lane == pair * 2 + inner, top + jnp.log(total), logsums
                )
            context_ref[start:stop, columns] = jnp.where(
                lane < HEAD_DIM, contexts[0], contexts[1]
            ).astype(BF16)
        logsum_ref[:, start:stop] = logsums.T
    sent_ref[...] = dot(context_ref[pl.ds(other_start, half), :], w_out_ref[...]).astype(BF16)
    kept_ref[...] = dot(context_ref[pl.ds(own_start, half), :], w_out_ref[...])


def scatter_kernel(kept_ref, came_ref, dispatch_ref, out_ref, *, cap, fill):
    rows = (kept_ref[...] + came_ref[...].astype(F32)).astype(BF16)
    pack(out_ref, rows, dispatch_ref[...], cap, fill)


def norm2_kernel(
    packed_ref, x_ref, grad_ref, gain_ref, bias_ref, resid_ref, h2_ref, up_ref, valid_ref, *, cap
):
    count, width = x_ref.shape
    moved = unpack(packed_ref, slots_down(count), cap, width)
    valid = (moved[:, :1] < 0.5 * EMPTY).astype(F32)
    resid = x_ref[...].astype(F32) + jnp.where(moved < 0.5 * EMPTY, moved, 0.0)
    resid_ref[...] = resid
    normed, _ = normalise(resid)
    h2_ref[...] = (normed * gain_ref[...] + bias_ref[...]).astype(BF16)
    up_ref[...] = (grad_ref[...].astype(F32) * valid).astype(BF16)
    valid_ref[...] = jnp.broadcast_to(valid, valid_ref.shape)


def gelu_and_slope(pre):
    root = math.sqrt(2.0 / math.pi)
    square = pre * pre
    bent = jnp.tanh(pre * (root + (root * 0.044715) * square))
    half = 0.5 + 0.5 * bent
    slope = half + (0.5 * pre) * (1.0 - bent * bent) * (root + (3.0 * 0.044715 * root) * square)
    return pre * half, slope


def expert_kernel(
    h2_ref,
    h2_other_ref,
    up_ref,
    up_other_ref,
    w_up_ref,
    w_down_ref,
    hidden_ref,
    dpre_ref,
    dh2_kept_ref,
    dh2_sent_ref,
    branch_kept_ref,
    branch_sent_ref,
    rows_ref,
    grads_ref,
    dh2_ref,
    branch_ref,
):
    count = h2_ref.shape[0]

    @pl.when(pl.program_id(0) == 0)
    def _():
        rows_ref[:count] = h2_ref[...]
        rows_ref[count:] = h2_other_ref[...]
        grads_ref[:count] = up_ref[...]
        grads_ref[count:] = up_other_ref[...]
        dh2_ref[...] = jnp.zeros_like(dh2_ref)
        branch_ref[...] = jnp.zeros_like(branch_ref)

    w_up, w_down = w_up_ref[...], w_down_ref[...]
    pre = dot(rows_ref[...], w_up)
    gelu, slope = gelu_and_slope(pre)
    hidden = gelu.astype(BF16)
    hidden_ref[...] = hidden
    dpre = (dot_nt(grads_ref[...], w_down) * slope).astype(BF16)
    dpre_ref[...] = dpre
    dh2_ref[...] += dot_nt(dpre, w_up)
    branch_ref[...] += dot(hidden, w_down)

    @pl.when(pl.program_id(0) == pl.num_programs(0) - 1)
    def _():
        dh2_kept_ref[...] = dh2_ref[:count]
        dh2_sent_ref[...] = dh2_ref[count:].astype(BF16)
        branch_kept_ref[...] = branch_ref[:count].astype(BF16)
        branch_sent_ref[...] = branch_ref[count:].astype(BF16)


def norm2_back_kernel(
    kept_ref, came_ref, resid_ref, grad_ref, gain_ref, dresid_ref, packed_ref, sums_ref, *, cap
):
    dh2 = kept_ref[...] + came_ref[...].astype(F32)
    normed, inverse = normalise(resid_ref[...])
    dresid = grad_ref[...].astype(F32) + norm_back(dh2, normed, inverse, gain_ref[...])
    dresid_ref[...] = dresid
    slot_of = lax.broadcasted_iota(jnp.int32, (1, dh2.shape[0]), 1)
    pack(packed_ref, dresid.astype(BF16), slot_of, cap, False)
    sums_ref[0:1] = jnp.sum(dh2 * normed, axis=0, keepdims=True)
    sums_ref[1:2] = jnp.sum(dh2, axis=0, keepdims=True)


def attend_back_kernel(
    where_ref,
    lengths_ref,
    own_ref,
    other_ref,
    input_ref,
    qkv_ref,
    context_ref,
    logsum_ref,
    w_qkv_ref,
    w_out_ref,
    kept_ref,
    sent_ref,
    grad_qkv_ref,
    grad_out_ref,
    dattn_ref,
    dcontext_ref,
    inner_ref,
    dquery_ref,
    dqkv_ref,
    *,
    step,
    reach,
    scale,
):
    half = own_ref.shape[0]
    span = 2 * half
    here = where_ref[0]
    own_start = pl.multiple_of(here * half, half)
    other_start = pl.multiple_of((1 - here) * half, half)
    dattn_ref[pl.ds(own_start, half), :] = own_ref[...]
    dattn_ref[pl.ds(other_start, half), :] = other_ref[...]
    dcontext = dot_nt(dattn_ref[...], w_out_ref[...]).astype(BF16)
    dcontext_ref[...] = dcontext
    grad_out_ref[...] = dot_tn(context_ref[...], dattn_ref[...]).astype(BF16)
    heads = qkv_ref.shape[2] // HEAD_DIM
    columns_all = qkv_ref.shape[2]
    product = dcontext.astype(F32) * context_ref[...].astype(F32)
    coarse = product.astype(BF16)
    fine = (product - coarse.astype(F32)).astype(BF16)
    of_head = (
        lax.broadcasted_iota(jnp.int32, (16, columns_all), 1) // HEAD_DIM
        == lax.broadcasted_iota(jnp.int32, (16, columns_all), 0)
    ).astype(BF16)
    inner_ref[...] = dot_nt(of_head, coarse) + dot_nt(of_head, fine)
    dquery_ref[...] = jnp.zeros_like(dquery_ref)
    for start in range(0, span, step):
        stop = start + step
        high = min(span, stop + reach)
        shape = (step, high - start)
        key_at = lax.broadcasted_iota(jnp.int32, shape, 0) + start
        query_at = lax.broadcasted_iota(jnp.int32, shape, 1) + start
        allowed = (segments(lengths_ref, query_at) == segments(lengths_ref, key_at)) & (
            key_at <= query_at
        )
        lane_k = lax.broadcasted_iota(jnp.int32, (step, 2 * HEAD_DIM), 1)
        lane_q = lax.broadcasted_iota(jnp.int32, (high - start, 2 * HEAD_DIM), 1)
        for pair in range(heads // 2):
            columns = slice(pair * 2 * HEAD_DIM, (pair + 1) * 2 * HEAD_DIM)
            query = qkv_ref[0, start:high, columns]
            keys = qkv_ref[1, start:stop, columns]
            values = qkv_ref[2, start:stop, columns]
            dcon = dcontext_ref[start:high, columns]
            dkeys, dvalues, dqueries = [], [], []
            for inner in range(2):
                head = pair * 2 + inner
                mine_k = (lane_k < HEAD_DIM) if inner == 0 else (lane_k >= HEAD_DIM)
                keys_h = jnp.where(mine_k, keys, jnp.zeros_like(keys))
                values_h = jnp.where(mine_k, values, jnp.zeros_like(values))
                scores = dot_nt(keys_h, query) * scale
                probs = jnp.exp(
                    jnp.where(allowed, scores - logsum_ref[head : head + 1, start:high], -1e30)
                )
                dprobs = dot_nt(values_h, dcon)
                dscores = (probs * (dprobs - inner_ref[head : head + 1, start:high])).astype(BF16)
                dvalues.append(dot(probs.astype(BF16), dcon))
                dkeys.append(dot(dscores, query))
                dqueries.append(dot_tn(dscores, keys))
            dqkv_ref[1, start:stop, columns] = (
                jnp.where(lane_k < HEAD_DIM, dkeys[0], dkeys[1]) * scale
            ).astype(BF16)
            dqkv_ref[2, start:stop, columns] = jnp.where(
                lane_k < HEAD_DIM, dvalues[0], dvalues[1]
            ).astype(BF16)
            dquery_ref[start:high, columns] += jnp.where(
                lane_q < HEAD_DIM, dqueries[0], dqueries[1]
            )
    dqkv_ref[0] = (dquery_ref[...] * scale).astype(BF16)

    def back_rows(start):
        total = dot_nt(dqkv_ref[0, pl.ds(start, half), :], w_qkv_ref[0])
        total = total + dot_nt(dqkv_ref[1, pl.ds(start, half), :], w_qkv_ref[1])
        return total + dot_nt(dqkv_ref[2, pl.ds(start, half), :], w_qkv_ref[2])

    sent_ref[...] = back_rows(other_start).astype(BF16)
    kept_ref[...] = back_rows(own_start)
    for which in range(3):
        grad_qkv_ref[which] = dot_tn(input_ref[...], dqkv_ref[which]).astype(BF16)


def norm1_back_kernel(packed_ref, x_ref, dresid_ref, gain_ref, out_ref, sums_ref, *, cap):
    count, width = x_ref.shape
    dh1 = unpack(packed_ref, slots_down(count), cap, width)
    normed, inverse = normalise(x_ref[...].astype(F32))
    out_ref[...] = dresid_ref[...] + norm_back(dh1, normed, inverse, gain_ref[...])
    sums_ref[0:1] = jnp.sum(dh1 * normed, axis=0, keepdims=True)
    sums_ref[1:2] = jnp.sum(dh1, axis=0, keepdims=True)


VMEM = pl.BlockSpec(memory_space=pltpu.VMEM)
SMEM = pl.BlockSpec(memory_space=pltpu.SMEM)


def call(kernel, name, outs, args, flops, scalars=0, scratch=(), limit=40):
    shapes = [jax.ShapeDtypeStruct(shape, kind) for shape, kind in outs]
    size = sum(math.prod(a.shape) * a.dtype.itemsize for a in (*args, *shapes))
    result = pl.pallas_call(
        kernel,
        name=name,
        out_shape=shapes,
        in_specs=[SMEM] * scalars + [VMEM] * (len(args) - scalars),
        out_specs=[VMEM] * len(shapes),
        scratch_shapes=list(scratch),
        cost_estimate=pl.CostEstimate(flops=flops, bytes_accessed=size, transcendentals=0),
        compiler_params=pltpu.CompilerParams(vmem_limit_bytes=limit * MIB),
    )(*args)
    return result


def expert(h2, h2_other, upstream, upstream_other, w_up, w_down):
    count, width = h2.shape
    units = w_up.shape[1]
    tile = min(512, units)
    shapes = [
        ((2 * count, units), BF16),
        ((2 * count, units), BF16),
        ((count, width), F32),
        ((count, width), BF16),
        ((count, width), BF16),
        ((count, width), BF16),
    ]
    rows = pl.BlockSpec((count, width), lambda j: (0, 0))
    by_unit = pl.BlockSpec((2 * count, tile), lambda j: (0, j))
    return pl.pallas_call(
        expert_kernel,
        name="expert",
        grid=(units // tile,),
        out_shape=[jax.ShapeDtypeStruct(shape, kind) for shape, kind in shapes],
        in_specs=[rows] * 4
        + [
            pl.BlockSpec((width, tile), lambda j: (0, j)),
            pl.BlockSpec((tile, width), lambda j: (j, 0)),
        ],
        out_specs=[by_unit, by_unit, rows, rows, rows, rows],
        scratch_shapes=[
            pltpu.VMEM((2 * count, width), BF16),
            pltpu.VMEM((2 * count, width), BF16),
            pltpu.VMEM((2 * count, width), F32),
            pltpu.VMEM((2 * count, width), F32),
        ],
        cost_estimate=pl.CostEstimate(
            flops=16 * count * width * units, bytes_accessed=16 * MIB, transcendentals=0
        ),
        compiler_params=pltpu.CompilerParams(vmem_limit_bytes=48 * MIB),
    )(h2, h2_other, upstream, upstream_other, w_up, w_down)


def flip(value, axis, bit):
    size = lax.axis_size(axis)
    return lax.ppermute(value, axis, [(i, i ^ bit) for i in range(size)])


def add_low(left, right):
    return (left.astype(F32) + right.astype(F32)).astype(BF16)


def halve(value, place, bit, dim):
    size = value.shape[dim] // 2
    side = (place // bit) % 2
    sent = lax.dynamic_slice_in_dim(value, (1 - side) * size, size, dim)
    kept = lax.dynamic_slice_in_dim(value, side * size, size, dim)
    return add_low(kept, flip(sent, "exp", bit))


def join(value, place, bit, dim):
    side = (place // bit) % 2
    came = flip(value, "exp", bit)
    return jnp.where(
        side == 0,
        jnp.concatenate([value, came], dim),
        jnp.concatenate([came, value], dim),
    )


def sum_over_exp(value, place, bits, dim):
    for bit in bits:
        value = halve(value, place, bit, dim)
    for bit in reversed(bits):
        value = join(value, place, bit, dim)
    return value


def on_device(
    block_input,
    dispatch,
    lengths,
    ln1_gain,
    ln1_bias,
    ln2_gain,
    ln2_bias,
    w_qkv,
    w_out,
    w_up,
    w_down,
    grad_output,
):
    slots, width = block_input.shape
    seq_rows = dispatch.shape[0]
    n_exp = lax.axis_size("exp")
    devices = n_exp * lax.axis_size("head")
    cap = slots // devices
    span = 2 * seq_rows
    columns = w_qkv.shape[2]
    scale = 1.0 / math.sqrt(HEAD_DIM)
    where = lax.axis_index("head").astype(jnp.int32).reshape(1)
    place = lax.axis_index("exp")
    step = 128
    reach = 3 * seq_rows // 4
    packed = ((devices * 8, cap * 128), BF16)
    moving = 2 * devices * 8 * max(slots, seq_rows) * width * 3
    gain1, bias1 = ln1_gain.reshape(1, width), ln1_bias.reshape(1, width)
    gain2, bias2 = ln2_gain.reshape(1, width), ln2_bias.reshape(1, width)
    down, along = dispatch.reshape(seq_rows, 1), dispatch.reshape(1, seq_rows)

    def exchange(value):
        value = value.reshape(devices, 8, cap * 128)
        value = lax.all_to_all(value, ("exp", "head"), split_axis=0, concat_axis=0, tiled=True)
        return value.reshape(devices * 8, cap * 128)

    def cross(value):
        return flip(value, "head", 1)

    (h1,) = call(
        functools.partial(norm1_kernel, cap=cap), "norm1", [packed],
        [block_input, gain1, bias1], moving,
    )
    arrived = exchange(h1)
    (own,) = call(
        functools.partial(gather_kernel, cap=cap), "gather1", [((seq_rows, width), BF16)],
        [arrived, down], moving,
    )
    other = cross(own)
    inputs, qkv, context, logsum, attn_kept, attn_sent = call(
        functools.partial(attend_kernel, step=step, reach=reach, scale=scale),
        "attend",
        [
            ((span, width), BF16),
            ((3, span, columns), BF16),
            ((span, columns), BF16),
            ((128, span), F32),
            ((seq_rows, width), F32),
            ((seq_rows, width), BF16),
        ],
        [where, lengths, own, other, w_qkv, w_out],
        2 * span * width * columns * 4 + 16 * span * span * columns,
        scalars=2,
    )
    (sent,) = call(
        functools.partial(scatter_kernel, cap=cap, fill=True), "scatter1", [packed],
        [attn_kept, cross(attn_sent), along], moving,
    )
    attn_back = exchange(sent)
    resid, h2, upstream, valid = call(
        functools.partial(norm2_kernel, cap=cap),
        "norm2",
        [((slots, width), F32), ((slots, width), BF16), ((slots, width), BF16), ((slots, 128), F32)],
        [attn_back, block_input, grad_output, gain2, bias2],
        moving,
    )
    h2_other, upstream_other = cross(h2), cross(upstream)
    hidden, dpre, dh2_kept, dh2_sent, branch_kept, branch_sent = expert(
        h2, h2_other, upstream, upstream_other, w_up[0], w_down[0]
    )
    dresid, sent, sums2 = call(
        functools.partial(norm2_back_kernel, cap=cap),
        "norm2_back",
        [((slots, width), F32), packed, ((2, width), F32)],
        [dh2_kept, cross(dh2_sent), resid, grad_output, gain2],
        moving,
    )
    arrived = exchange(sent)
    rows_all = jnp.concatenate([h2, h2_other], 0)
    grads_all = jnp.concatenate([upstream, upstream_other], 0)
    grad_down = dot_tn(hidden, grads_all)[None]
    grad_up = dot_tn(rows_all, dpre)[None]
    branch = branch_kept.astype(F32) + cross(branch_sent).astype(F32)
    result = (resid + valid[:, :1] * branch).astype(BF16)
    (own,) = call(
        functools.partial(gather_kernel, cap=cap), "gather2", [((seq_rows, width), BF16)],
        [arrived, down], moving,
    )
    other = cross(own)
    du_kept, du_sent, grad_qkv, grad_out = call(
        functools.partial(attend_back_kernel, step=step, reach=reach, scale=scale),
        "attend_back",
        [
            ((seq_rows, width), F32),
            ((seq_rows, width), BF16),
            ((3, width, columns), BF16),
            ((columns, width), BF16),
        ],
        [where, lengths, own, other, inputs, qkv, context, logsum, w_qkv, w_out],
        2 * span * width * columns * 8 + 40 * span * span * columns,
        scalars=2,
        scratch=[
            pltpu.VMEM((span, width), BF16),
            pltpu.VMEM((span, columns), BF16),
            pltpu.VMEM((16, span), F32),
            pltpu.VMEM((span, columns), F32),
            pltpu.VMEM((3, span, columns), BF16),
        ],
    )
    (sent,) = call(
        functools.partial(scatter_kernel, cap=cap, fill=False), "scatter2", [packed],
        [du_kept, cross(du_sent), along], moving,
    )
    arrived = exchange(sent)
    input_grad, sums1 = call(
        functools.partial(norm1_back_kernel, cap=cap),
        "norm1_back",
        [((slots, width), F32), ((2, width), F32)],
        [arrived, block_input, dresid, gain1],
        moving,
    )
    bits = [1 << i for i in range(n_exp.bit_length() - 1)]
    swapped = [bits[1], bits[0], *bits[2:]]
    middle = width // 2
    upper = sum_over_exp(grad_qkv[:, :middle], place, bits, 1)
    lower = sum_over_exp(grad_qkv[:, middle:], place, swapped, 1)
    grad_qkv = jnp.concatenate([upper, lower], 1).astype(F32)
    middle = columns // 2
    upper = sum_over_exp(grad_out[:middle], place, bits, 0)
    lower = sum_over_exp(grad_out[middle:], place, swapped, 0)
    grad_out = jnp.concatenate([upper, lower], 0).astype(F32)
    sums = jnp.concatenate([sums1, sums2], 0)
    sums = sums + cross(sums)
    for bit in bits:
        sums = sums + flip(sums, "exp", bit)
    return (
        result,
        input_grad,
        sums[0],
        sums[1],
        sums[2],
        sums[3],
        grad_qkv,
        grad_out,
        grad_up,
        grad_down,
    )


def solution(mesh):
    placed = (
        P(("exp", "head"), None),
        P(("exp", "head")),
        P("exp", None),
        P(),
        P(),
        P(),
        P(),
        P(None, None, "head"),
        P("head", None),
        P("exp", None, "head"),
        P("exp", "head", None),
        P(("exp", "head"), None),
    )
    return jax.shard_map(
        on_device,
        mesh=mesh,
        in_specs=placed,
        out_specs=(
            P(("exp", "head"), None),
            P(("exp", "head"), None),
            P(),
            P(),
            P(),
            P(),
            P(None, None, "head"),
            P("head", None),
            P("exp", None, "head"),
            P("exp", "head", None),
        ),
        check_vma=False,
    )
```

```python
import functools
import math

import jax
import jax.numpy as jnp
from jax import lax
from jax.experimental import pallas as pl
from jax.experimental.pallas import tpu as pltpu
from jax.sharding import PartitionSpec as P

HEAD_DIM = 64
EPS = 1e-05
BF16 = jnp.bfloat16
F32 = jnp.float32
MIB = 1024 * 1024
EMPTY = 1e30


def dot(left, right):
    return lax.dot_general(left, right, (((1,), (0,)), ((), ())), preferred_element_type=F32)


def dot_nt(left, right):
    return lax.dot_general(left, right, (((1,), (1,)), ((), ())), preferred_element_type=F32)


def dot_tn(left, right):
    return lax.dot_general(left, right, (((0,), (0,)), ((), ())), preferred_element_type=F32)


def normalise(rows):
    mean = jnp.mean(rows, axis=1, keepdims=True)
    centred = rows - mean
    inverse = lax.rsqrt(jnp.mean(centred * centred, axis=1, keepdims=True) + EPS)
    return centred * inverse, inverse


def norm_back(upstream, normed, inverse, gain):
    scaled = upstream * gain
    first = jnp.mean(scaled, axis=1, keepdims=True)
    second = jnp.mean(scaled * normed, axis=1, keepdims=True)
    return inverse * (scaled - first - normed * second)


def pack(out_ref, rows, slot_of, cap, fill):
    total, width = out_ref.shape[0], rows.shape[1]
    place = lax.broadcasted_iota(jnp.int32, (total, slot_of.shape[1]), 0)
    first = (place >> 3) * cap
    sub = lax.broadcasted_iota(jnp.int32, (total, 128), 0) & 7
    piece = width // 8

    def placed(target):
        hit = (slot_of == target).astype(F32)
        moved = dot(hit.astype(BF16), rows)
        if fill:
            moved = moved + (1.0 - jnp.sum(hit, axis=1, keepdims=True)) * EMPTY
        return moved

    whole = cap // 8
    for group in range(whole):
        moved = placed(first + (place & 7) + group * 8)
        out_ref[:, group * width : (group + 1) * width] = moved.astype(BF16)
    for left in range(cap % 8):
        moved = placed(first + whole * 8 + left)
        folded = moved[:, :piece]
        for s in range(1, 8):
            folded = jnp.where(sub == s, moved[:, s * piece : (s + 1) * piece], folded)
        start = whole * width + left * piece
        out_ref[:, start : start + piece] = folded.astype(BF16)


def unpack(packed_ref, slot_of, cap, width):
    total = packed_ref.shape[0]
    place = lax.broadcasted_iota(jnp.int32, (slot_of.shape[0], total), 1)
    first = (place >> 3) * cap
    piece = width // 8
    sub = lax.broadcasted_iota(jnp.int32, (total, piece), 0) & 7
    whole = cap // 8
    rows = None
    for group in range(whole):
        hit = (slot_of == first + (place & 7) + group * 8).astype(BF16)
        part = dot(hit, packed_ref[:, group * width : (group + 1) * width])
        rows = part if rows is None else rows + part
    for left in range(cap % 8):
        start = whole * width + left * piece
        folded = packed_ref[:, start : start + piece].astype(F32)
        spread = jnp.concatenate(
            [jnp.where(sub == s, folded, 0.0).astype(BF16) for s in range(8)], axis=1
        )
        hit = (slot_of == first + whole * 8 + left).astype(BF16)
        part = dot(hit, spread)
        rows = part if rows is None else rows + part
    return rows


def slots_down(count):
    return lax.broadcasted_iota(jnp.int32, (count, 1), 0)


def norm1_kernel(x_ref, gain_ref, bias_ref, out_ref, *, cap):
    normed, _ = normalise(x_ref[...].astype(F32))
    rows = (normed * gain_ref[...] + bias_ref[...]).astype(BF16)
    slot_of = lax.broadcasted_iota(jnp.int32, (1, rows.shape[0]), 1)
    pack(out_ref, rows, slot_of, cap, False)


def gather_kernel(packed_ref, dispatch_ref, out_ref, *, cap):
    out_ref[...] = unpack(packed_ref, dispatch_ref[...], cap, out_ref.shape[1]).astype(BF16)


def started(source, target, sem):
    copy = pltpu.make_async_copy(source, target, sem)
    copy.start()
    return copy


def segments(lengths_ref, places):
    seg = jnp.zeros(places.shape, jnp.int32)
    end = 0
    for index in range(lengths_ref.shape[1]):
        end = end + lengths_ref[0, index]
        seg = seg + (places >= end).astype(jnp.int32)
    return seg


def attend_kernel(
    where_ref,
    lengths_ref,
    own_ref,
    other_ref,
    w_qkv_far,
    w_out_far,
    own_far,
    input_far,
    qkv_far,
    context_far,
    logsum_far,
    kept_ref,
    sent_ref,
    w_qkv_ref,
    w_out_ref,
    input_ref,
    qkv_ref,
    context_ref,
    logsum_ref,
    sems,
    *,
    step,
    reach,
    scale,
):
    weights = [
        started(w_qkv_far.at[which], w_qkv_ref.at[which], sems.at[which]) for which in range(3)
    ]
    last_weight = started(w_out_far, w_out_ref, sems.at[3])
    leaving = [started(own_ref, own_far, sems.at[4])]
    half = own_ref.shape[0]
    span = 2 * half
    here = where_ref[0]
    own_start = pl.multiple_of(here * half, half)
    other_start = pl.multiple_of((1 - here) * half, half)
    input_ref[pl.ds(own_start, half), :] = own_ref[...]
    input_ref[pl.ds(other_start, half), :] = other_ref[...]
    leaving.append(started(input_ref, input_far, sems.at[5]))
    for which in range(3):
        weights[which].wait()
        qkv_ref[which] = dot(input_ref[...], w_qkv_ref[which]).astype(BF16)
    leaving.append(started(qkv_ref, qkv_far, sems.at[6]))
    heads = qkv_ref.shape[2] // HEAD_DIM
    for start in range(0, span, step):
        stop = start + step
        low = max(0, start - reach)
        shape = (step, stop - low)
        query_at = lax.broadcasted_iota(jnp.int32, shape, 0) + start
        key_at = lax.broadcasted_iota(jnp.int32, shape, 1) + low
        allowed = (segments(lengths_ref, query_at) == segments(lengths_ref, key_at)) & (
            key_at <= query_at
        )
        lane = lax.broadcasted_iota(jnp.int32, (step, 2 * HEAD_DIM), 1)
        logsums = jnp.zeros((step, 128), F32)
        logsum_lane = lax.broadcasted_iota(jnp.int32, (step, 128), 1)
        for pair in range(heads // 2):
            columns = slice(pair * 2 * HEAD_DIM, (pair + 1) * 2 * HEAD_DIM)
            query = qkv_ref[0, start:stop, columns]
            keys = qkv_ref[1, low:stop, columns]
            values = qkv_ref[2, low:stop, columns]
            contexts = []
            for inner in range(2):
                mine = (lane < HEAD_DIM) if inner == 0 else (lane >= HEAD_DIM)
                scores = dot_nt(jnp.where(mine, query, jnp.zeros_like(query)), keys) * scale
                scores = jnp.where(allowed, scores, -1e30)
                top = jnp.max(scores, axis=1, keepdims=True)
                expo = jnp.exp(scores - top)
                total = jnp.sum(expo, axis=1, keepdims=True)
                probs = (expo * (1.0 / total)).astype(BF16)
                contexts.append(dot(probs, values))
                logsums = jnp.where(
                    logsum_lane == pair * 2 + inner, top + jnp.log(total), logsums
                )
            context_ref[start:stop, columns] = jnp.where(
                lane < HEAD_DIM, contexts[0], contexts[1]
            ).astype(BF16)
        logsum_ref[:, start:stop] = logsums.T
    leaving.append(started(context_ref, context_far, sems.at[7]))
    leaving.append(started(logsum_ref, logsum_far, sems.at[8]))
    last_weight.wait()
    sent_ref[...] = dot(context_ref[pl.ds(other_start, half), :], w_out_ref[...]).astype(BF16)
    kept_ref[...] = dot(context_ref[pl.ds(own_start, half), :], w_out_ref[...])
    for copy in leaving:
        copy.wait()


def scatter_kernel(kept_ref, came_ref, dispatch_ref, out_ref, *, cap, fill):
    rows = (kept_ref[...] + came_ref[...].astype(F32)).astype(BF16)
    pack(out_ref, rows, dispatch_ref[...], cap, fill)


def norm2_kernel(
    packed_ref, x_ref, grad_ref, gain_ref, bias_ref, resid_ref, h2_ref, up_ref, valid_ref, *, cap
):
    count, width = x_ref.shape
    moved = unpack(packed_ref, slots_down(count), cap, width)
    valid = (moved[:, :1] < 0.5 * EMPTY).astype(F32)
    resid = x_ref[...].astype(F32) + jnp.where(moved < 0.5 * EMPTY, moved, 0.0)
    resid_ref[...] = resid
    normed, _ = normalise(resid)
    h2_ref[...] = (normed * gain_ref[...] + bias_ref[...]).astype(BF16)
    up_ref[...] = (grad_ref[...].astype(F32) * valid).astype(BF16)
    valid_ref[...] = jnp.broadcast_to(valid, valid_ref.shape)


def gelu_and_slope(pre):
    root = math.sqrt(2.0 / math.pi)
    square = pre * pre
    bent = jnp.tanh(pre * (root + (root * 0.044715) * square))
    half = 0.5 + 0.5 * bent
    slope = half + (0.5 * pre) * (1.0 - bent * bent) * (root + (3.0 * 0.044715 * root) * square)
    return pre * half, slope


def expert_kernel(
    h2_ref,
    h2_other_ref,
    up_ref,
    up_other_ref,
    w_up_ref,
    w_down_ref,
    hidden_ref,
    dpre_ref,
    dh2_kept_ref,
    dh2_sent_ref,
    branch_kept_ref,
    branch_sent_ref,
    rows_ref,
    grads_ref,
    dh2_ref,
    branch_ref,
):
    count = h2_ref.shape[0]

    @pl.when(pl.program_id(0) == 0)
    def _():
        rows_ref[:count] = h2_ref[...]
        rows_ref[count:] = h2_other_ref[...]
        grads_ref[:count] = up_ref[...]
        grads_ref[count:] = up_other_ref[...]
        dh2_ref[...] = jnp.zeros_like(dh2_ref)
        branch_ref[...] = jnp.zeros_like(branch_ref)

    w_up, w_down = w_up_ref[...], w_down_ref[...]
    pre = dot(rows_ref[...], w_up)
    gelu, slope = gelu_and_slope(pre)
    hidden = gelu.astype(BF16)
    hidden_ref[...] = hidden
    dpre = (dot_nt(grads_ref[...], w_down) * slope).astype(BF16)
    dpre_ref[...] = dpre
    dh2_ref[...] += dot_nt(dpre, w_up)
    branch_ref[...] += dot(hidden, w_down)

    @pl.when(pl.program_id(0) == pl.num_programs(0) - 1)
    def _():
        dh2_kept_ref[...] = dh2_ref[:count]
        dh2_sent_ref[...] = dh2_ref[count:].astype(BF16)
        branch_kept_ref[...] = branch_ref[:count].astype(BF16)
        branch_sent_ref[...] = branch_ref[count:].astype(BF16)


def store_sums(sums_ref, upstream, normed):
    for which, total in enumerate((upstream * normed, upstream)):
        total = jnp.sum(total, axis=0, keepdims=True)
        pieces = total.shape[1] // 128
        for at in range(pieces):
            row = which * pieces + at
            sums_ref[row : row + 1] = total[:, at * 128 : (at + 1) * 128]


def norm2_back_kernel(
    kept_ref, came_ref, resid_ref, grad_ref, gain_ref, dresid_ref, packed_ref, sums_ref, *, cap
):
    dh2 = kept_ref[...] + came_ref[...].astype(F32)
    normed, inverse = normalise(resid_ref[...])
    dresid = grad_ref[...].astype(F32) + norm_back(dh2, normed, inverse, gain_ref[...])
    dresid_ref[...] = dresid
    slot_of = lax.broadcasted_iota(jnp.int32, (1, dh2.shape[0]), 1)
    pack(packed_ref, dresid.astype(BF16), slot_of, cap, False)
    store_sums(sums_ref, dh2, normed)


def out_grad_kernel(where_ref, own_ref, other_ref, context_far, dattn_ref, *rest):
    piece_fars, (context_ref, grad_ref, piece_ref, sems) = rest[:4], rest[4:]
    arriving = started(context_far, context_ref, sems.at[4])
    half = own_ref.shape[0]
    here = where_ref[0]
    dattn_ref[pl.ds(pl.multiple_of(here * half, half), half), :] = own_ref[...]
    dattn_ref[pl.ds(pl.multiple_of((1 - here) * half, half), half), :] = other_ref[...]
    arriving.wait()
    grad_ref[...] = dot_tn(context_ref[...], dattn_ref[...])
    width = grad_ref.shape[1]
    quarter = grad_ref.shape[0] // 4
    owners = piece_ref.shape[1]
    rows = quarter // owners
    leaving = []
    for step in (1, 2, 3, 0):
        first = (where_ref[1] ^ step) * quarter
        for owner in range(owners):
            start = pl.multiple_of(first + owner * rows, rows)
            block = grad_ref[pl.ds(start, rows), :]
            piece_ref[step, owner] = jnp.concatenate(
                [block[:, at : at + 128] for at in range(0, width, 128)], axis=0
            ).astype(BF16)
        leaving.append(started(piece_ref.at[step], piece_fars[step], sems.at[step]))
    for copy in leaving:
        copy.wait()


def attend_back_kernel(
    where_ref,
    lengths_ref,
    dattn_ref,
    qkv_far,
    context_far,
    logsum_far,
    w_qkv_far,
    w_out_far,
    kept_ref,
    sent_ref,
    *rest,
    step,
    reach,
    scale,
):
    dvalue_fars, dkq_fars = rest[:4], rest[4:8]
    dcontext_ref, inner_ref, dquery_ref, dqkv_ref = rest[8:12]
    qkv_ref, context_ref, logsum_ref, w_qkv_ref, w_out_ref, sems = rest[12:]
    arriving = [
        started(source, target, sems.at[at])
        for at, (source, target) in enumerate(
            (
                (w_out_far, w_out_ref),
                (context_far, context_ref),
                (qkv_far, qkv_ref),
                (logsum_far, logsum_ref),
                (w_qkv_far, w_qkv_ref),
            )
        )
    ]
    half = kept_ref.shape[0]
    span = 2 * half
    here = where_ref[0]
    own_start = pl.multiple_of(here * half, half)
    other_start = pl.multiple_of((1 - here) * half, half)
    arriving[0].wait()
    dcontext = dot_nt(dattn_ref[...], w_out_ref[...]).astype(BF16)
    dcontext_ref[...] = dcontext
    arriving[1].wait()
    arriving[2].wait()
    arriving[3].wait()
    heads = qkv_ref.shape[2] // HEAD_DIM
    columns_all = qkv_ref.shape[2]
    product = dcontext.astype(F32) * context_ref[...].astype(F32)
    coarse = product.astype(BF16)
    fine = (product - coarse.astype(F32)).astype(BF16)
    of_head = (
        lax.broadcasted_iota(jnp.int32, (16, columns_all), 1) // HEAD_DIM
        == lax.broadcasted_iota(jnp.int32, (16, columns_all), 0)
    ).astype(BF16)
    inner_ref[...] = dot_nt(of_head, coarse) + dot_nt(of_head, fine)
    dquery_ref[...] = jnp.zeros_like(dquery_ref)
    for start in range(0, span, step):
        stop = start + step
        high = min(span, stop + reach)
        shape = (step, high - start)
        key_at = lax.broadcasted_iota(jnp.int32, shape, 0) + start
        query_at = lax.broadcasted_iota(jnp.int32, shape, 1) + start
        allowed = (segments(lengths_ref, query_at) == segments(lengths_ref, key_at)) & (
            key_at <= query_at
        )
        lane_k = lax.broadcasted_iota(jnp.int32, (step, 2 * HEAD_DIM), 1)
        lane_q = lax.broadcasted_iota(jnp.int32, (high - start, 2 * HEAD_DIM), 1)
        for pair in range(heads // 2):
            columns = slice(pair * 2 * HEAD_DIM, (pair + 1) * 2 * HEAD_DIM)
            query = qkv_ref[0, start:high, columns]
            keys = qkv_ref[1, start:stop, columns]
            values = qkv_ref[2, start:stop, columns]
            dcon = dcontext_ref[start:high, columns]
            dkeys, dvalues, dqueries = [], [], []
            for inner in range(2):
                head = pair * 2 + inner
                mine_k = (lane_k < HEAD_DIM) if inner == 0 else (lane_k >= HEAD_DIM)
                keys_h = jnp.where(mine_k, keys, jnp.zeros_like(keys))
                values_h = jnp.where(mine_k, values, jnp.zeros_like(values))
                scores = dot_nt(keys_h, query) * scale
                probs = jnp.exp(
                    jnp.where(allowed, scores - logsum_ref[head : head + 1, start:high], -1e30)
                )
                dprobs = dot_nt(values_h, dcon)
                dscores = (probs * (dprobs - inner_ref[head : head + 1, start:high])).astype(BF16)
                dvalues.append(dot(probs.astype(BF16), dcon))
                dkeys.append(dot(dscores, query))
                dqueries.append(dot_tn(dscores, keys))
            dqkv_ref[1, start:stop, columns] = (
                jnp.where(lane_k < HEAD_DIM, dkeys[0], dkeys[1]) * scale
            ).astype(BF16)
            dqkv_ref[2, start:stop, columns] = jnp.where(
                lane_k < HEAD_DIM, dvalues[0], dvalues[1]
            ).astype(BF16)
            dquery_ref[start:high, columns] += jnp.where(
                lane_q < HEAD_DIM, dqueries[0], dqueries[1]
            )
    dqkv_ref[0] = (dquery_ref[...] * scale).astype(BF16)

    quarter = columns_all // 4
    leaving = []
    for kind, at in ((2, 1), (2, 2), (2, 3), (1, 1), (0, 1), (1, 2), (0, 2), (1, 3), (0, 3), (2, 0), (1, 0), (0, 0)):
        first = pl.multiple_of((where_ref[1] ^ at) * quarter, quarter)
        target = dvalue_fars[at] if kind == 2 else dkq_fars[at].at[1 - kind]
        leaving.append(
            started(dqkv_ref.at[kind, :, pl.ds(first, quarter)], target, sems.at[5 + kind * 4 + at])
        )
    arriving[4].wait()

    def back_rows(start):
        total = dot_nt(dqkv_ref[0, pl.ds(start, half), :], w_qkv_ref[0])
        total = total + dot_nt(dqkv_ref[1, pl.ds(start, half), :], w_qkv_ref[1])
        return total + dot_nt(dqkv_ref[2, pl.ds(start, half), :], w_qkv_ref[2])

    sent_ref[...] = back_rows(other_start).astype(BF16)
    kept_ref[...] = back_rows(own_start)
    for copy in leaving:
        copy.wait()


def token_grad(where_ref, grad_refs, index, input_ref, own_refs, other_refs):
    half = own_refs[0].shape[0]
    own_start = pl.multiple_of(where_ref[0] * half, half)
    other_start = pl.multiple_of((1 - where_ref[0]) * half, half)

    def rows(ref, start, count):
        return ref[pl.ds(start, count), :] if index is None else ref[index, pl.ds(start, count), :]

    total = dot_tn(rows(grad_refs[0], 0, 2 * half), input_ref[...])
    for grad_ref, own_ref, other_ref in zip(grad_refs[1:], own_refs, other_refs):
        total = total + dot_tn(rows(grad_ref, own_start, half), own_ref[...])
        total = total + dot_tn(rows(grad_ref, other_start, half), other_ref[...])
    return total.T


def value_grad_kernel(where_ref, *refs):
    grad_refs, input_ref, own_refs, other_refs = refs[0:4], refs[4], refs[5:8], refs[8:11]
    out_refs, piece_refs, total_ref = refs[11:15], refs[15:19], refs[19]
    total_ref[...] = token_grad(where_ref, grad_refs, None, input_ref, own_refs, other_refs)
    rest, rows = piece_refs[0].shape[0], piece_refs[0].shape[1] // 2
    for step, piece_ref in enumerate(piece_refs):
        for at in range(rest):
            owner = (where_ref[2] ^ step) + 4 * at
            piece_ref[at, :rows] = sum(ref[owner].astype(F32) for ref in out_refs).astype(BF16)
            start = pl.multiple_of(owner * rows, rows)
            piece_ref[at, rows:] = total_ref[pl.ds(start, rows), :].astype(BF16)


def key_query_grad_kernel(where_ref, *refs):
    grad_refs, input_ref, own_refs, other_refs = refs[0:4], refs[4], refs[5:8], refs[8:11]
    piece_refs, total_ref = refs[11:15], refs[15]
    rest, rows = piece_refs[0].shape[0], piece_refs[0].shape[1] // 2
    for index in range(2):
        total_ref[...] = token_grad(where_ref, grad_refs, index, input_ref, own_refs, other_refs)
        for step, piece_ref in enumerate(piece_refs):
            for at in range(rest):
                owner = (where_ref[2] ^ step) + 4 * at
                start = pl.multiple_of(owner * rows, rows)
                piece_ref[at, index * rows : (index + 1) * rows] = total_ref[
                    pl.ds(start, rows), :
                ].astype(BF16)


def add_kernel(where_ref, *refs, digit):
    for step, out_ref in enumerate(refs[4:]):
        for at in range(out_ref.shape[0]):
            owner = (where_ref[digit] ^ step) + 4 * at
            out_ref[at] = sum(ref[owner].astype(F32) for ref in refs[:4]).astype(BF16)


def last_add_kernel(*refs):
    refs[4][...] = sum(ref[0].astype(F32) for ref in refs[:4]).astype(BF16)


def split_store(out_ref, start, value):
    rows = value.shape[0]
    coarse = value.astype(BF16)
    out_ref[start : start + rows] = coarse
    out_ref[start + rows : start + 2 * rows] = (value - coarse.astype(F32)).astype(BF16)


def last_add_sums_kernel(*refs):
    out_ref = refs[8]
    rows = refs[0].shape[1]
    out_ref[:rows] = sum(ref[0].astype(F32) for ref in refs[:4]).astype(BF16)
    sums = jnp.concatenate([refs[4][...] + refs[5][...], refs[6][...] + refs[7][...]], axis=0)
    split_store(out_ref, rows, sums)


def split_sum(refs, start, stop):
    rows = (stop - start) // 2
    return sum(
        ref[start : start + rows].astype(F32) + ref[start + rows : stop].astype(F32)
        for ref in refs
    )


def stack_kernel(*refs, sums):
    out_ref = refs[4]
    rows = refs[0].shape[0] - sums
    for at, ref in enumerate(refs[:4]):
        out_ref[at * rows : (at + 1) * rows] = ref[:rows]
    if sums:
        split_store(out_ref, 4 * rows, split_sum(refs[:4], rows, rows + sums))


def place_rows(where_ref, digits, at):
    owner = 0
    for digit in range(1, digits):
        owner = owner + ((where_ref[1 + digit] ^ (at % 4)) << (2 * (digit - 1)))
        at = at // 4
    return owner


def each_piece(where_ref, refs, digits, rows, use):
    owners = 4 ** (digits - 1)
    for step in range(4):
        column = where_ref[1] ^ step
        for at in range(owners):
            owner = place_rows(where_ref, digits, at)
            first = at * 2 * rows

            def load(low, high, first=first, step=step):
                if step < 3:
                    return refs[step][first + low : first + high]
                middle = refs[3].shape[0]
                start, stop = first + low, first + high
                if stop <= middle:
                    return refs[3][start:stop]
                if start >= middle:
                    return refs[4][start - middle : stop - middle]
                return jnp.concatenate([refs[3][start:middle], refs[4][: stop - middle]], axis=0)

            use(column, owner, load)


def finish_out_value_kernel(where_ref, *refs, digits):
    qkv_ref, out_ref = refs[5:]
    width = qkv_ref.shape[1]
    rows = width // 4 ** (digits - 1)
    few = rows * 128 // width

    def use(column, owner, load):
        start = pl.multiple_of(column * 128 + owner * few, few)
        out_ref[pl.ds(start, few), :] = jnp.concatenate(
            [load(at, at + few).astype(F32) for at in range(0, rows, few)], axis=1
        )
        lanes = pl.ds(pl.multiple_of(column * 128, 128), 128)
        qkv_ref[0, pl.ds(pl.multiple_of(owner * rows, rows), rows), lanes] = load(
            rows, 2 * rows
        ).astype(F32)

    each_piece(where_ref, refs[:5], digits, rows, use)


def finish_key_query_kernel(where_ref, *refs, digits, sums):
    qkv_ref, sums_ref = refs[6:]
    width = qkv_ref.shape[1]
    rows = width // 4 ** (digits - 1)

    def use(column, owner, load):
        lanes = pl.ds(pl.multiple_of(column * 128, 128), 128)
        down = pl.ds(pl.multiple_of(owner * rows, rows), rows)
        qkv_ref[1, down, lanes] = load(0, rows).astype(F32)
        qkv_ref[0, down, lanes] = load(rows, 2 * rows).astype(F32)

    each_piece(where_ref, refs[:5], digits, rows, use)
    total = refs[0].shape[0]
    half = refs[4].shape[0]
    sums_ref[...] = split_sum(refs[:3], total - sums, total) + split_sum(
        refs[4:5], half - sums, half
    )


def expert_grad_kernel(rows_ref, grads_ref, hidden_ref, dpre_ref, up_ref, down_ref, turned_ref):
    @pl.when(pl.program_id(0) == 0)
    def _():
        turned_ref[...] = rows_ref[...].T

    up_ref[...] = dot(turned_ref[...], dpre_ref[...])
    down_ref[...] = dot_tn(hidden_ref[...], grads_ref[...])


def norm1_back_kernel(packed_ref, x_ref, dresid_ref, gain_ref, out_ref, sums_ref, *, cap):
    count, width = x_ref.shape
    dh1 = unpack(packed_ref, slots_down(count), cap, width)
    normed, inverse = normalise(x_ref[...].astype(F32))
    out_ref[...] = dresid_ref[...] + norm_back(dh1, normed, inverse, gain_ref[...])
    store_sums(sums_ref, dh1, normed)


VMEM = pl.BlockSpec(memory_space=pltpu.VMEM)
SMEM = pl.BlockSpec(memory_space=pltpu.SMEM)


def after(value, *others):
    return lax.optimization_barrier((value, *others))[0]


def far(value):
    return pltpu.with_memory_space_constraint(value, pltpu.HBM)


def call(kernel, name, outs, args, flops, scalars=0, scratch=(), limit=16, away=(), out_away=(), raw=(), out_raw=()):
    shapes = [
        pltpu.HBM(shape, kind)
        if at in out_away or at in out_raw
        else jax.ShapeDtypeStruct(shape, kind)
        for at, (shape, kind) in enumerate(outs)
    ]

    def spec(at, away, raw):
        if at in raw:
            return pl.BlockSpec(memory_space=pltpu.HBM)
        return pl.BlockSpec() if at in away else VMEM

    size = sum(math.prod(a.shape) * a.dtype.itemsize for a in (*args, *shapes))
    return pl.pallas_call(
        kernel,
        name=name,
        out_shape=shapes,
        in_specs=[
            SMEM if at < scalars else spec(at, away, raw) for at in range(len(args))
        ],
        out_specs=[spec(at, out_away, out_raw) for at in range(len(outs))],
        scratch_shapes=list(scratch),
        cost_estimate=pl.CostEstimate(flops=flops, bytes_accessed=size, transcendentals=0),
        compiler_params=pltpu.CompilerParams(vmem_limit_bytes=limit * MIB),
    )(*[far(value) if at in away or at in raw else value for at, value in enumerate(args)])


def expert(h2, h2_other, upstream, upstream_other, w_up, w_down):
    count, width = h2.shape
    units = w_up.shape[1]
    tile = min(512, units)
    shapes = [
        ((2 * count, units), BF16),
        ((2 * count, units), BF16),
        ((count, width), F32),
        ((count, width), BF16),
        ((count, width), BF16),
        ((count, width), BF16),
        ((2 * count, width), BF16),
        ((2 * count, width), BF16),
    ]
    stay = (2, 3)
    both = pl.BlockSpec((2 * count, width), lambda j: (0, 0))
    rows = pl.BlockSpec((count, width), lambda j: (0, 0))
    by_unit = pl.BlockSpec((2 * count, tile), lambda j: (0, j))
    return pl.pallas_call(
        expert_kernel,
        name="expert",
        grid=(units // tile,),
        out_shape=[
            jax.ShapeDtypeStruct(shape, kind) if at in stay else pltpu.HBM(shape, kind)
            for at, (shape, kind) in enumerate(shapes)
        ],
        in_specs=[rows] * 4
        + [
            pl.BlockSpec((width, tile), lambda j: (0, j)),
            pl.BlockSpec((tile, width), lambda j: (j, 0)),
        ],
        out_specs=[by_unit, by_unit, rows, rows, rows, rows, both, both],
        scratch_shapes=[
            pltpu.VMEM((2 * count, width), F32),
            pltpu.VMEM((2 * count, width), F32),
        ],
        cost_estimate=pl.CostEstimate(
            flops=16 * count * width * units, bytes_accessed=16 * MIB, transcendentals=0
        ),
        compiler_params=pltpu.CompilerParams(vmem_limit_bytes=40 * MIB),
    )(h2, h2_other, upstream, upstream_other, far(w_up), far(w_down))


def expert_grads(rows, grads, hidden, dpre):
    count, width = rows.shape
    units = hidden.shape[1]
    tile = min(512, units)
    whole = pl.BlockSpec((count, width), lambda j: (0, 0))
    by_unit = pl.BlockSpec((count, tile), lambda j: (0, j))
    return pl.pallas_call(
        expert_grad_kernel,
        name="expert_grads",
        grid=(units // tile,),
        out_shape=[pltpu.HBM((width, units), F32), pltpu.HBM((units, width), F32)],
        in_specs=[whole] * 2 + [by_unit] * 2,
        out_specs=[
            pl.BlockSpec((width, tile), lambda j: (0, j)),
            pl.BlockSpec((tile, width), lambda j: (j, 0)),
        ],
        scratch_shapes=[pltpu.VMEM((width, count), BF16)],
        cost_estimate=pl.CostEstimate(
            flops=4 * count * width * units, bytes_accessed=24 * MIB, transcendentals=0
        ),
        compiler_params=pltpu.CompilerParams(vmem_limit_bytes=40 * MIB),
    )(far(rows), far(grads), far(hidden), far(dpre))


def flip(value, axis, bit):
    size = lax.axis_size(axis)
    return lax.ppermute(value, axis, [(i, i ^ bit) for i in range(size)])


def to_others(values, digit):
    return [
        flip(values[m] if isinstance(values, (list, tuple)) else values, "exp", m << (2 * digit))
        for m in range(1, 4)
    ]


def after_all(values, *others):
    return list(lax.optimization_barrier((*values, *others))[: len(values)])


def add_up(parts, where, digit, digits, sums=None):
    owners, rows, columns = parts[0].shape
    if digit + 1 < digits:
        return call(
            functools.partial(add_kernel, digit=digit + 2), "add",
            [((owners // 4, rows, columns), BF16)] * 4, [where, *parts], 0, scalars=1,
            away=(1,), out_away=(0,),
        )
    if sums is None:
        return call(
            last_add_kernel, "last_add", [((rows, columns), BF16)], parts, 0, away=(0,),
        )
    rows += 4 * sums[0].shape[0]
    return call(
        last_add_sums_kernel, "last_add_sums", [((rows, columns), BF16)], [*parts, *sums], 0,
        away=(0,),
    )


def stack(parts, sums):
    rows, columns = parts[0].shape
    shape = (4 * (rows - sums) + sums, columns)
    return call(
        functools.partial(stack_kernel, sums=sums), "stack", [(shape, BF16)], parts, 0,
    )[0]


def sum_and_spread(first, second, where, digits, sums, extra):
    for digit in range(1, digits):
        first_came, second_came = to_others(first, digit), to_others(second, digit)
        first = add_up([first[0], *first_came], where, digit, digits)
        second_came = after_all(second_came, first[0])
        second = add_up([second[0], *second_came], where, digit, digits, sums)
    first, second = first[0], second[0]
    for digit in reversed(range(1, digits)):
        first_came, second_came = to_others(first, digit), to_others(second, digit)
        first = stack([first, *after_all(first_came, second)], 0)
        second = stack([second, *after_all(second_came, first)], extra)
    results = []
    for total in (first, second):
        by_x, by_y = flip(total, "exp", 1), flip(total, "exp", 2)
        middle = total.shape[0] // 2
        if results:
            by_x, by_y = after_all([by_x, by_y], forward)
        forward = by_y[:middle]
        results.append([total, by_x, by_y, flip(forward, "exp", 1), flip(by_x[middle:], "exp", 2)])
    return results


def on_device(
    block_input,
    dispatch,
    lengths,
    ln1_gain,
    ln1_bias,
    ln2_gain,
    ln2_bias,
    w_qkv,
    w_out,
    w_up,
    w_down,
    grad_output,
):
    slots, width = block_input.shape
    seq_rows = dispatch.shape[0]
    n_exp = lax.axis_size("exp")
    devices = n_exp * lax.axis_size("head")
    cap = slots // devices
    span = 2 * seq_rows
    columns = w_qkv.shape[2]
    scale = 1.0 / math.sqrt(HEAD_DIM)
    digits = (n_exp.bit_length() - 1) // 2
    place = lax.axis_index("exp")
    where = jnp.stack(
        [lax.axis_index("head"), *[(place >> (2 * digit)) & 3 for digit in range(digits)]]
    ).astype(jnp.int32)
    step = 128
    reach = 3 * seq_rows // 4
    packed = ((devices * 8, cap * 128), BF16)
    moving = 2 * devices * 8 * max(slots, seq_rows) * width * 3
    gain1, bias1 = ln1_gain.reshape(1, width), ln1_bias.reshape(1, width)
    gain2, bias2 = ln2_gain.reshape(1, width), ln2_bias.reshape(1, width)
    down, along = dispatch.reshape(seq_rows, 1), dispatch.reshape(1, seq_rows)

    def exchange(value):
        value = value.reshape(devices, 8, cap * 128)
        value = lax.all_to_all(value, ("exp", "head"), split_axis=0, concat_axis=0, tiled=True)
        return value.reshape(devices * 8, cap * 128)

    def cross(value):
        return flip(value, "head", 1)

    (h1,) = call(
        functools.partial(norm1_kernel, cap=cap), "norm1", [packed],
        [block_input, gain1, bias1], moving, away=(0, 1, 2),
    )
    arrived = exchange(h1)
    (own,) = call(
        functools.partial(gather_kernel, cap=cap), "gather1", [((seq_rows, width), BF16)],
        [arrived, down], moving,
    )
    other = cross(own)
    own_copy, inputs, qkv, context, logsum, attn_kept, attn_sent = call(
        functools.partial(attend_kernel, step=step, reach=reach, scale=scale),
        "attend",
        [
            ((seq_rows, width), BF16),
            ((span, width), BF16),
            ((3, span, columns), BF16),
            ((span, columns), BF16),
            ((128, span), F32),
            ((seq_rows, width), F32),
            ((seq_rows, width), BF16),
        ],
        [where, lengths, own, other, w_qkv, w_out],
        2 * span * width * columns * 4 + 16 * span * span * columns,
        scalars=2,
        limit=24,
        raw=(4, 5),
        out_raw=range(5),
        scratch=[
            pltpu.VMEM((3, width, columns), BF16),
            pltpu.VMEM((columns, width), BF16),
            pltpu.VMEM((span, width), BF16),
            pltpu.VMEM((3, span, columns), BF16),
            pltpu.VMEM((span, columns), BF16),
            pltpu.VMEM((128, span), F32),
            pltpu.SemaphoreType.DMA((9,)),
        ],
    )
    (sent,) = call(
        functools.partial(scatter_kernel, cap=cap, fill=True), "scatter1", [packed],
        [attn_kept, cross(attn_sent), along], moving,
    )
    attn_back = exchange(sent)
    near_own = after(own_copy, sent)
    by_x, by_y = flip(near_own, "exp", 1), flip(near_own, "exp", 2)
    by_xy = flip(after(own_copy, attn_back), "exp", 3)
    attn_back = after(attn_back, by_x, by_y)
    resid, h2, upstream, valid = call(
        functools.partial(norm2_kernel, cap=cap),
        "norm2",
        [((slots, width), F32), ((slots, width), BF16), ((slots, width), BF16), ((slots, 128), F32)],
        [attn_back, block_input, grad_output, gain2, bias2],
        moving,
    )
    h2_other, upstream_other = cross(h2), cross(upstream)
    hidden, dpre, dh2_kept, dh2_sent, branch_kept, branch_sent, rows_all, grads_all = expert(
        h2, h2_other, upstream, upstream_other, w_up[0], w_down[0]
    )
    dh2_sent = after(dh2_sent, by_xy)
    dresid, sent, sums2 = call(
        functools.partial(norm2_back_kernel, cap=cap),
        "norm2_back",
        [((slots, width), F32), packed, ((width // 64, 128), F32)],
        [dh2_kept, cross(dh2_sent), resid, grad_output, gain2],
        moving,
    )
    arrived = exchange(sent)
    plane_own = [after(rows, sent) for rows in (by_x, by_y, by_xy)]
    plane_other = [cross(rows) for rows in plane_own]
    hidden = after(hidden, sent)
    grad_up, grad_down = expert_grads(rows_all, grads_all, hidden, dpre)
    arrived, grad_up, grad_down, *plane_other = lax.optimization_barrier(
        (arrived, grad_up, grad_down, *plane_other)
    )
    branch = branch_kept.astype(F32) + cross(branch_sent).astype(F32)
    result = (resid + valid[:, :1] * branch).astype(BF16)
    (own,) = call(
        functools.partial(gather_kernel, cap=cap), "gather2", [((seq_rows, width), BF16)],
        [arrived, down], moving,
    )
    other = cross(own)
    piece = 4 * width // n_exp
    dattn, *out_pieces = call(
        out_grad_kernel,
        "out_grad",
        [((span, width), BF16), *[((n_exp // 4, piece, 128), BF16)] * 4],
        [where, own, other, context],
        2 * span * width * columns,
        scalars=1,
        scratch=[
            pltpu.VMEM((span, columns), BF16),
            pltpu.VMEM((columns, width), F32),
            pltpu.VMEM((4, n_exp // 4, piece, 128), BF16),
            pltpu.SemaphoreType.DMA((5,)),
        ],
        raw=(3,),
        out_raw=range(1, 5),
    )
    out_parts = [out_pieces[0], *to_others(out_pieces, 0)]
    du_kept, du_sent, *parts = call(
        functools.partial(attend_back_kernel, step=step, reach=reach, scale=scale),
        "attend_back",
        [
            ((seq_rows, width), F32),
            ((seq_rows, width), BF16),
            *[((span, 128), BF16)] * 4,
            *[((2, span, 128), BF16)] * 4,
        ],
        [where, lengths, dattn, qkv, context, logsum, w_qkv, w_out],
        2 * span * width * columns * 4 + 40 * span * span * columns,
        scalars=2,
        limit=24,
        raw=range(3, 8),
        out_raw=range(2, 10),
        scratch=[
            pltpu.VMEM((span, columns), BF16),
            pltpu.VMEM((16, span), F32),
            pltpu.VMEM((span, columns), F32),
            pltpu.VMEM((3, span, columns), BF16),
            pltpu.VMEM((3, span, columns), BF16),
            pltpu.VMEM((span, columns), BF16),
            pltpu.VMEM((128, span), F32),
            pltpu.VMEM((3, width, columns), BF16),
            pltpu.VMEM((columns, width), BF16),
            pltpu.SemaphoreType.DMA((17,)),
        ],
    )
    du_sent = after(du_sent, *out_parts[1:])
    value_parts = [parts[0], *to_others(parts[:4], 0)]
    key_query_parts = [parts[4], *to_others(after_all(parts[4:], *value_parts[1:]), 0)]
    (sent,) = call(
        functools.partial(scatter_kernel, cap=cap, fill=False), "scatter2", [packed],
        [du_kept, cross(du_sent), along], moving,
    )
    arrived = exchange(sent)
    input_grad, sums1 = call(
        functools.partial(norm1_back_kernel, cap=cap),
        "norm1_back",
        [((slots, width), F32), ((width // 64, 128), F32)],
        [arrived, block_input, dresid, gain1],
        moving,
        away=(1, 2, 3),
        out_away=(0,),
    )
    tokens = [inputs, *plane_own, *plane_other]
    split = [((n_exp // 16, 2 * piece, 128), BF16)] * 4
    product = 8 * span * width * 128
    out_value = call(
        value_grad_kernel, "value_grad", split, [where, *value_parts, *tokens, *out_parts],
        product, scalars=1, scratch=[pltpu.VMEM((width, 128), F32)], away=(1, *range(5, 13)),
        out_away=(0,),
    )
    key_query_parts[1:] = after_all(key_query_parts[1:], out_value[1])
    key_query = call(
        key_query_grad_kernel, "key_query_grad", split, [where, *key_query_parts, *tokens],
        2 * product, scalars=1, scratch=[pltpu.VMEM((width, 128), F32)], away=(1, *range(5, 12)),
        out_away=(0,),
    )
    sums = [sums1, cross(sums1), sums2, cross(sums2)]
    extra = 4 * sums1.shape[0]
    out_value, key_query = sum_and_spread(out_value, key_query, where, digits, sums, extra)
    whole_qkv = pltpu.HBM((3, width, columns), F32)
    grad_qkv, grad_out = pl.pallas_call(
        functools.partial(finish_out_value_kernel, digits=digits),
        name="finish_out_value",
        grid=(1,),
        out_shape=[whole_qkv, pltpu.HBM((columns, width), F32)],
        in_specs=[SMEM] + [VMEM] * 5,
        out_specs=[
            pl.BlockSpec((1, width, columns), lambda i: (2, 0, 0)),
            pl.BlockSpec((columns, width), lambda i: (0, 0)),
        ],
        cost_estimate=pl.CostEstimate(flops=0, bytes_accessed=6 * MIB, transcendentals=0),
        compiler_params=pltpu.CompilerParams(vmem_limit_bytes=40 * MIB),
    )(where, *out_value)
    grad_qkv, sums = pl.pallas_call(
        functools.partial(finish_key_query_kernel, digits=digits, sums=extra),
        name="finish_key_query",
        grid=(1,),
        out_shape=[whole_qkv, jax.ShapeDtypeStruct((extra // 2, 128), F32)],
        in_specs=[SMEM] + [VMEM] * 5 + [pl.BlockSpec(memory_space=pltpu.HBM)],
        out_specs=[
            pl.BlockSpec((2, width, columns), lambda i: (0, 0, 0)),
            pl.BlockSpec((extra // 2, 128), lambda i: (0, 0)),
        ],
        input_output_aliases={6: 0},
        cost_estimate=pl.CostEstimate(flops=0, bytes_accessed=6 * MIB, transcendentals=0),
        compiler_params=pltpu.CompilerParams(vmem_limit_bytes=40 * MIB),
    )(where, *key_query, grad_qkv)
    sums = sums.reshape(4, width)
    return (
        result,
        input_grad,
        sums[0],
        sums[1],
        sums[2],
        sums[3],
        grad_qkv,
        grad_out,
        grad_up[None],
        grad_down[None],
    )


def solution(mesh):
    placed = (
        P(("exp", "head"), None),
        P(("exp", "head")),
        P("exp", None),
        P(),
        P(),
        P(),
        P(),
        P(None, None, "head"),
        P("head", None),
        P("exp", None, "head"),
        P("exp", "head", None),
        P(("exp", "head"), None),
    )
    return jax.shard_map(
        on_device,
        mesh=mesh,
        in_specs=placed,
        out_specs=(
            P(("exp", "head"), None),
            P(("exp", "head"), None),
            P(),
            P(),
            P(),
            P(),
            P(None, None, "head"),
            P("head", None),
            P("exp", None, "head"),
            P("exp", "head", None),
        ),
        check_vma=False,
    )
```

```python
import functools
import math

import jax
import jax.numpy as jnp
from jax import lax
from jax.experimental import pallas as pl
from jax.experimental.pallas import tpu as pltpu
from jax.sharding import PartitionSpec as P

HEAD_DIM = 64
EPS = 1e-05
BF16 = jnp.bfloat16
F32 = jnp.float32
MIB = 1024 * 1024
EMPTY = 1e30


def dot(left, right):
    return lax.dot_general(left, right, (((1,), (0,)), ((), ())), preferred_element_type=F32)


def dot_nt(left, right):
    return lax.dot_general(left, right, (((1,), (1,)), ((), ())), preferred_element_type=F32)


def dot_tn(left, right):
    return lax.dot_general(left, right, (((0,), (0,)), ((), ())), preferred_element_type=F32)


def normalise(rows):
    mean = jnp.mean(rows, axis=1, keepdims=True)
    centred = rows - mean
    inverse = lax.rsqrt(jnp.mean(centred * centred, axis=1, keepdims=True) + EPS)
    return centred * inverse, inverse


def norm_back(upstream, normed, inverse, gain):
    scaled = upstream * gain
    first = jnp.mean(scaled, axis=1, keepdims=True)
    second = jnp.mean(scaled * normed, axis=1, keepdims=True)
    return inverse * (scaled - first - normed * second)


def pack(out_ref, rows, slot_of, cap, fill):
    total, width = out_ref.shape[0], rows.shape[1]
    place = lax.broadcasted_iota(jnp.int32, (total, slot_of.shape[1]), 0)
    first = (place >> 3) * cap
    sub = lax.broadcasted_iota(jnp.int32, (total, 128), 0) & 7
    piece = width // 8

    def placed(target):
        hit = (slot_of == target).astype(F32)
        moved = dot(hit.astype(BF16), rows)
        if fill:
            moved = moved + (1.0 - jnp.sum(hit, axis=1, keepdims=True)) * EMPTY
        return moved

    whole = cap // 8
    for group in range(whole):
        moved = placed(first + (place & 7) + group * 8)
        out_ref[:, group * width : (group + 1) * width] = moved.astype(BF16)
    for left in range(cap % 8):
        moved = placed(first + whole * 8 + left)
        folded = moved[:, :piece]
        for s in range(1, 8):
            folded = jnp.where(sub == s, moved[:, s * piece : (s + 1) * piece], folded)
        start = whole * width + left * piece
        out_ref[:, start : start + piece] = folded.astype(BF16)


def unpack(packed_ref, slot_of, cap, width):
    total = packed_ref.shape[0]
    place = lax.broadcasted_iota(jnp.int32, (slot_of.shape[0], total), 1)
    first = (place >> 3) * cap
    piece = width // 8
    sub = lax.broadcasted_iota(jnp.int32, (total, piece), 0) & 7
    whole = cap // 8
    rows = None
    for group in range(whole):
        hit = (slot_of == first + (place & 7) + group * 8).astype(BF16)
        part = dot(hit, packed_ref[:, group * width : (group + 1) * width])
        rows = part if rows is None else rows + part
    for left in range(cap % 8):
        start = whole * width + left * piece
        folded = packed_ref[:, start : start + piece].astype(F32)
        spread = jnp.concatenate(
            [jnp.where(sub == s, folded, 0.0).astype(BF16) for s in range(8)], axis=1
        )
        hit = (slot_of == first + whole * 8 + left).astype(BF16)
        part = dot(hit, spread)
        rows = part if rows is None else rows + part
    return rows


def slots_down(count):
    return lax.broadcasted_iota(jnp.int32, (count, 1), 0)


def norm1_kernel(x_ref, gain_ref, bias_ref, out_ref, *, cap):
    normed, _ = normalise(x_ref[...].astype(F32))
    rows = (normed * gain_ref[...] + bias_ref[...]).astype(BF16)
    slot_of = lax.broadcasted_iota(jnp.int32, (1, rows.shape[0]), 1)
    pack(out_ref, rows, slot_of, cap, False)


def gather_kernel(packed_ref, dispatch_ref, out_ref, *, cap):
    out_ref[...] = unpack(packed_ref, dispatch_ref[...], cap, out_ref.shape[1]).astype(BF16)


def two_heads(rows):
    lane = lax.broadcasted_iota(jnp.int32, rows.shape, 1)
    clear = jnp.zeros_like(rows)
    return jnp.concatenate(
        [jnp.where(lane < HEAD_DIM, rows, clear), jnp.where(lane < HEAD_DIM, clear, rows)], axis=0
    )


def started(source, target, sem):
    copy = pltpu.make_async_copy(source, target, sem)
    copy.start()
    return copy


def segments(lengths_ref, places):
    seg = jnp.zeros(places.shape, jnp.int32)
    end = 0
    for index in range(lengths_ref.shape[1]):
        end = end + lengths_ref[0, index]
        seg = seg + (places >= end).astype(jnp.int32)
    return seg


def attend_kernel(
    where_ref,
    lengths_ref,
    own_ref,
    other_ref,
    w_qkv_far,
    w_out_far,
    own_far,
    input_far,
    qkv_far,
    context_far,
    logsum_far,
    kept_ref,
    sent_ref,
    w_qkv_ref,
    w_out_ref,
    input_ref,
    qkv_ref,
    context_ref,
    logsum_ref,
    sems,
    *,
    step,
    reach,
    scale,
):
    weights = [
        started(w_qkv_far.at[which], w_qkv_ref.at[which], sems.at[which]) for which in range(3)
    ]
    last_weight = started(w_out_far, w_out_ref, sems.at[3])
    leaving = [started(own_ref, own_far, sems.at[4])]
    half = own_ref.shape[0]
    span = 2 * half
    here = where_ref[0]
    own_start = pl.multiple_of(here * half, half)
    other_start = pl.multiple_of((1 - here) * half, half)
    input_ref[pl.ds(own_start, half), :] = own_ref[...]
    input_ref[pl.ds(other_start, half), :] = other_ref[...]
    leaving.append(started(input_ref, input_far, sems.at[5]))
    for which in range(3):
        weights[which].wait()
        qkv_ref[which] = dot(input_ref[...], w_qkv_ref[which]).astype(BF16)
    leaving.append(started(qkv_ref, qkv_far, sems.at[6]))
    heads = qkv_ref.shape[2] // HEAD_DIM
    for start in range(0, span, step):
        stop = start + step
        low = max(0, start - reach)
        shape = (step, stop - low)
        query_at = lax.broadcasted_iota(jnp.int32, shape, 0) + start
        key_at = lax.broadcasted_iota(jnp.int32, shape, 1) + low
        allowed = (segments(lengths_ref, query_at) == segments(lengths_ref, key_at)) & (
            key_at <= query_at
        )
        allowed = jnp.concatenate([allowed.astype(F32)] * heads, axis=0) > 0.5
        lane = lax.broadcasted_iota(jnp.int32, (step, 2 * HEAD_DIM), 1)
        pairs = [
            slice(at, at + 2 * HEAD_DIM) for at in range(0, heads * HEAD_DIM, 2 * HEAD_DIM)
        ]
        scores = jnp.concatenate(
            [
                dot_nt(two_heads(qkv_ref[0, start:stop, columns]), qkv_ref[1, low:stop, columns])
                for columns in pairs
            ],
            axis=0,
        )
        scores = jnp.where(allowed, scores * scale, -1e30)
        top = jnp.max(scores, axis=1, keepdims=True)
        expo = jnp.exp(scores - top)
        total = jnp.sum(expo, axis=1, keepdims=True)
        probs = (expo * (1.0 / total)).astype(BF16)
        logsum = top + jnp.log(total)
        logsums = jnp.zeros((step, 128), F32)
        logsum_lane = lax.broadcasted_iota(jnp.int32, (step, 128), 1)
        for head in range(heads):
            mine = logsum[head * step : (head + 1) * step]
            logsums = jnp.where(logsum_lane == head, mine, logsums)
        for at, columns in enumerate(pairs):
            both = dot(
                probs[2 * at * step : 2 * (at + 1) * step], qkv_ref[2, low:stop, columns]
            )
            context_ref[start:stop, columns] = jnp.where(
                lane < HEAD_DIM, both[:step], both[step:]
            ).astype(BF16)
        logsum_ref[:, start:stop] = logsums.T
    leaving.append(started(context_ref, context_far, sems.at[7]))
    leaving.append(started(logsum_ref, logsum_far, sems.at[8]))
    last_weight.wait()
    sent_ref[...] = dot(context_ref[pl.ds(other_start, half), :], w_out_ref[...]).astype(BF16)
    kept_ref[...] = dot(context_ref[pl.ds(own_start, half), :], w_out_ref[...])
    for copy in leaving:
        copy.wait()


def scatter_kernel(kept_ref, came_ref, dispatch_ref, out_ref, *, cap, fill):
    rows = (kept_ref[...] + came_ref[...].astype(F32)).astype(BF16)
    pack(out_ref, rows, dispatch_ref[...], cap, fill)


def norm2_kernel(
    packed_ref, x_ref, grad_ref, gain_ref, bias_ref, resid_ref, h2_ref, up_ref, valid_ref, *, cap
):
    count, width = x_ref.shape
    moved = unpack(packed_ref, slots_down(count), cap, width)
    valid = (moved[:, :1] < 0.5 * EMPTY).astype(F32)
    resid = x_ref[...].astype(F32) + jnp.where(moved < 0.5 * EMPTY, moved, 0.0)
    resid_ref[...] = resid
    normed, _ = normalise(resid)
    h2_ref[...] = (normed * gain_ref[...] + bias_ref[...]).astype(BF16)
    up_ref[...] = (grad_ref[...].astype(F32) * valid).astype(BF16)
    valid_ref[...] = jnp.broadcast_to(valid, valid_ref.shape)


def gelu_and_slope(pre):
    root = math.sqrt(2.0 / math.pi)
    square = pre * pre
    bent = jnp.tanh(pre * (root + (root * 0.044715) * square))
    half = 0.5 + 0.5 * bent
    slope = half + (0.5 * pre) * (1.0 - bent * bent) * (root + (3.0 * 0.044715 * root) * square)
    return pre * half, slope


def expert_kernel(
    h2_ref,
    h2_other_ref,
    up_ref,
    up_other_ref,
    w_up_ref,
    w_down_ref,
    hidden_ref,
    dpre_ref,
    dh2_kept_ref,
    dh2_sent_ref,
    branch_kept_ref,
    branch_sent_ref,
    rows_ref,
    grads_ref,
    dh2_ref,
    branch_ref,
):
    count = h2_ref.shape[0]

    @pl.when(pl.program_id(0) == 0)
    def _():
        rows_ref[:count] = h2_ref[...]
        rows_ref[count:] = h2_other_ref[...]
        grads_ref[:count] = up_ref[...]
        grads_ref[count:] = up_other_ref[...]
        dh2_ref[...] = jnp.zeros_like(dh2_ref)
        branch_ref[...] = jnp.zeros_like(branch_ref)

    w_up, w_down = w_up_ref[...], w_down_ref[...]
    pre = dot(rows_ref[...], w_up)
    gelu, slope = gelu_and_slope(pre)
    hidden = gelu.astype(BF16)
    hidden_ref[...] = hidden
    dpre = (dot_nt(grads_ref[...], w_down) * slope).astype(BF16)
    dpre_ref[...] = dpre
    dh2_ref[...] += dot_nt(dpre, w_up)
    branch_ref[...] += dot(hidden, w_down)

    @pl.when(pl.program_id(0) == pl.num_programs(0) - 1)
    def _():
        dh2_kept_ref[...] = dh2_ref[:count]
        dh2_sent_ref[...] = dh2_ref[count:].astype(BF16)
        branch_kept_ref[...] = branch_ref[:count].astype(BF16)
        branch_sent_ref[...] = branch_ref[count:].astype(BF16)


def store_sums(sums_ref, upstream, normed):
    for which, total in enumerate((upstream * normed, upstream)):
        total = jnp.sum(total, axis=0, keepdims=True)
        pieces = total.shape[1] // 128
        for at in range(pieces):
            row = which * pieces + at
            sums_ref[row : row + 1] = total[:, at * 128 : (at + 1) * 128]


def norm2_back_kernel(
    kept_ref, came_ref, resid_ref, grad_ref, gain_ref, dresid_ref, packed_ref, sums_ref, *, cap
):
    dh2 = kept_ref[...] + came_ref[...].astype(F32)
    normed, inverse = normalise(resid_ref[...])
    dresid = grad_ref[...].astype(F32) + norm_back(dh2, normed, inverse, gain_ref[...])
    dresid_ref[...] = dresid
    slot_of = lax.broadcasted_iota(jnp.int32, (1, dh2.shape[0]), 1)
    pack(packed_ref, dresid.astype(BF16), slot_of, cap, False)
    store_sums(sums_ref, dh2, normed)


def out_grad_kernel(where_ref, own_ref, other_ref, context_far, dattn_ref, *rest):
    piece_fars, (context_ref, grad_ref, piece_ref, sems) = rest[:4], rest[4:]
    arriving = started(context_far, context_ref, sems.at[4])
    half = own_ref.shape[0]
    here = where_ref[0]
    dattn_ref[pl.ds(pl.multiple_of(here * half, half), half), :] = own_ref[...]
    dattn_ref[pl.ds(pl.multiple_of((1 - here) * half, half), half), :] = other_ref[...]
    arriving.wait()
    grad_ref[...] = dot_tn(context_ref[...], dattn_ref[...])
    width = grad_ref.shape[1]
    quarter = grad_ref.shape[0] // 4
    owners = piece_ref.shape[1]
    rows = quarter // owners
    leaving = []
    for step in (1, 2, 3, 0):
        first = (where_ref[1] ^ step) * quarter
        for owner in range(owners):
            start = pl.multiple_of(first + owner * rows, rows)
            block = grad_ref[pl.ds(start, rows), :]
            piece_ref[step, owner] = jnp.concatenate(
                [block[:, at : at + 128] for at in range(0, width, 128)], axis=0
            ).astype(BF16)
        leaving.append(started(piece_ref.at[step], piece_fars[step], sems.at[step]))
    for copy in leaving:
        copy.wait()


def attend_back_kernel(
    where_ref,
    lengths_ref,
    dattn_ref,
    qkv_far,
    context_far,
    logsum_far,
    w_qkv_far,
    w_out_far,
    kept_ref,
    sent_ref,
    *rest,
    step,
    reach,
    scale,
):
    dvalue_fars, dkq_fars = rest[:4], rest[4:8]
    dcontext_ref, inner_ref, dquery_ref, dqkv_ref = rest[8:12]
    qkv_ref, context_ref, logsum_ref, w_qkv_ref, w_out_ref, sems = rest[12:]
    arriving = [
        started(source, target, sems.at[at])
        for at, (source, target) in enumerate(
            (
                (w_out_far, w_out_ref),
                (context_far, context_ref),
                (qkv_far, qkv_ref),
                (logsum_far, logsum_ref),
                (w_qkv_far, w_qkv_ref),
            )
        )
    ]
    half = kept_ref.shape[0]
    span = 2 * half
    here = where_ref[0]
    own_start = pl.multiple_of(here * half, half)
    other_start = pl.multiple_of((1 - here) * half, half)
    arriving[0].wait()
    dcontext = dot_nt(dattn_ref[...], w_out_ref[...]).astype(BF16)
    dcontext_ref[...] = dcontext
    arriving[1].wait()
    arriving[2].wait()
    arriving[3].wait()
    heads = qkv_ref.shape[2] // HEAD_DIM
    columns_all = qkv_ref.shape[2]
    product = dcontext.astype(F32) * context_ref[...].astype(F32)
    coarse = product.astype(BF16)
    fine = (product - coarse.astype(F32)).astype(BF16)
    of_head = (
        lax.broadcasted_iota(jnp.int32, (16, columns_all), 1) // HEAD_DIM
        == lax.broadcasted_iota(jnp.int32, (16, columns_all), 0)
    ).astype(BF16)
    inner_ref[...] = dot_nt(of_head, coarse) + dot_nt(of_head, fine)
    dquery_ref[...] = jnp.zeros_like(dquery_ref)
    for start in range(0, span, step):
        stop = start + step
        high = min(span, stop + reach)
        shape = (step, high - start)
        key_at = lax.broadcasted_iota(jnp.int32, shape, 0) + start
        query_at = lax.broadcasted_iota(jnp.int32, shape, 1) + start
        allowed = (segments(lengths_ref, query_at) == segments(lengths_ref, key_at)) & (
            key_at <= query_at
        )
        allowed = jnp.concatenate([allowed.astype(F32)] * heads, axis=0) > 0.5
        lane = lax.broadcasted_iota(jnp.int32, (step, 2 * HEAD_DIM), 1)
        pairs = [
            slice(at, at + 2 * HEAD_DIM) for at in range(0, heads * HEAD_DIM, 2 * HEAD_DIM)
        ]
        keys = [two_heads(qkv_ref[1, start:stop, columns]) for columns in pairs]

        def by_head(ref, start=start, high=high):
            return jnp.concatenate(
                [
                    jnp.broadcast_to(ref[head : head + 1, start:high], (step, high - start))
                    for head in range(heads)
                ],
                axis=0,
            )

        scores = jnp.concatenate(
            [
                dot_nt(keys[at], qkv_ref[0, start:high, columns])
                for at, columns in enumerate(pairs)
            ],
            axis=0,
        )
        probs = jnp.exp(jnp.where(allowed, scores * scale - by_head(logsum_ref), -1e30))
        dprobs = jnp.concatenate(
            [
                dot_nt(two_heads(qkv_ref[2, start:stop, columns]), dcontext_ref[start:high, columns])
                for columns in pairs
            ],
            axis=0,
        )
        dscores = (probs * (dprobs - by_head(inner_ref))).astype(BF16)
        probs = probs.astype(BF16)
        for at, columns in enumerate(pairs):
            mine = slice(2 * at * step, 2 * (at + 1) * step)
            dvalues = dot(probs[mine], dcontext_ref[start:high, columns])
            dkeys = dot(dscores[mine], qkv_ref[0, start:high, columns])
            dquery_ref[start:high, columns] += dot_tn(dscores[mine], keys[at])
            dqkv_ref[1, start:stop, columns] = (
                jnp.where(lane < HEAD_DIM, dkeys[:step], dkeys[step:]) * scale
            ).astype(BF16)
            dqkv_ref[2, start:stop, columns] = jnp.where(
                lane < HEAD_DIM, dvalues[:step], dvalues[step:]
            ).astype(BF16)
    dqkv_ref[0] = (dquery_ref[...] * scale).astype(BF16)

    quarter = columns_all // 4
    leaving = []
    for kind, at in ((2, 1), (2, 2), (2, 3), (1, 1), (0, 1), (1, 2), (0, 2), (1, 3), (0, 3), (2, 0), (1, 0), (0, 0)):
        first = pl.multiple_of((where_ref[1] ^ at) * quarter, quarter)
        target = dvalue_fars[at] if kind == 2 else dkq_fars[at].at[1 - kind]
        leaving.append(
            started(dqkv_ref.at[kind, :, pl.ds(first, quarter)], target, sems.at[5 + kind * 4 + at])
        )
    arriving[4].wait()

    def back_rows(start):
        total = dot_nt(dqkv_ref[0, pl.ds(start, half), :], w_qkv_ref[0])
        total = total + dot_nt(dqkv_ref[1, pl.ds(start, half), :], w_qkv_ref[1])
        return total + dot_nt(dqkv_ref[2, pl.ds(start, half), :], w_qkv_ref[2])

    sent_ref[...] = back_rows(other_start).astype(BF16)
    kept_ref[...] = back_rows(own_start)
    for copy in leaving:
        copy.wait()


def token_grad(where_ref, grad_refs, index, input_ref, own_refs, other_refs):
    half = own_refs[0].shape[0]
    own_start = pl.multiple_of(where_ref[0] * half, half)
    other_start = pl.multiple_of((1 - where_ref[0]) * half, half)

    def rows(ref, start, count):
        return ref[pl.ds(start, count), :] if index is None else ref[index, pl.ds(start, count), :]

    total = dot_tn(rows(grad_refs[0], 0, 2 * half), input_ref[...])
    for grad_ref, own_ref, other_ref in zip(grad_refs[1:], own_refs, other_refs):
        total = total + dot_tn(rows(grad_ref, own_start, half), own_ref[...])
        total = total + dot_tn(rows(grad_ref, other_start, half), other_ref[...])
    return total.T


def store_halves(where_ref, bit, half_refs, load, at):
    rows = at.stop - at.start
    for side, half_ref in enumerate(half_refs):
        mine = ((where_ref[2] >> bit) & 1) ^ side
        for index in range(half_ref.shape[0]):
            half_ref[index, at] = load(2 * index + mine, rows).astype(BF16)


def value_grad_kernel(where_ref, *refs):
    grad_refs, input_ref, own_refs, other_refs = refs[0:4], refs[4], refs[5:8], refs[8:11]
    out_refs, half_refs, total_ref = refs[11:15], refs[15:17], refs[17]
    total_ref[...] = token_grad(where_ref, grad_refs, None, input_ref, own_refs, other_refs)
    rows = half_refs[0].shape[1] // 2
    store_halves(
        where_ref, 0, half_refs,
        lambda owner, rows: sum(ref[owner].astype(F32) for ref in out_refs), slice(0, rows),
    )
    store_halves(
        where_ref, 0, half_refs,
        lambda owner, rows: total_ref[pl.ds(pl.multiple_of(owner * rows, rows), rows), :],
        slice(rows, 2 * rows),
    )


def key_query_grad_kernel(where_ref, *refs):
    grad_refs, input_ref, own_refs, other_refs = refs[0:4], refs[4], refs[5:8], refs[8:11]
    half_refs, total_ref = refs[11:13], refs[13]
    rows = half_refs[0].shape[1] // 2
    for index in range(2):
        total_ref[...] = token_grad(where_ref, grad_refs, index, input_ref, own_refs, other_refs)
        store_halves(
            where_ref, 0, half_refs,
            lambda owner, rows: total_ref[pl.ds(pl.multiple_of(owner * rows, rows), rows), :],
            slice(index * rows, (index + 1) * rows),
        )


def add_kernel(where_ref, kept_ref, came_ref, *half_refs, bit):
    store_halves(
        where_ref, bit, half_refs,
        lambda owner, rows: kept_ref[owner].astype(F32) + came_ref[owner].astype(F32),
        slice(0, kept_ref.shape[1]),
    )


def last_add_kernel(kept_ref, came_ref, out_ref):
    out_ref[...] = (kept_ref[0].astype(F32) + came_ref[0].astype(F32)).astype(BF16)


def split_store(out_ref, start, value):
    rows = value.shape[0]
    coarse = value.astype(BF16)
    out_ref[start : start + rows] = coarse
    out_ref[start + rows : start + 2 * rows] = (value - coarse.astype(F32)).astype(BF16)


def last_add_sums_kernel(kept_ref, came_ref, *refs):
    out_ref = refs[4]
    rows = kept_ref.shape[1]
    out_ref[:rows] = (kept_ref[0].astype(F32) + came_ref[0].astype(F32)).astype(BF16)
    sums = jnp.concatenate([refs[0][...] + refs[1][...], refs[2][...] + refs[3][...]], axis=0)
    split_store(out_ref, rows, sums)


def split_sum(refs, start, stop):
    rows = (stop - start) // 2
    return sum(
        ref[start : start + rows].astype(F32) + ref[start + rows : stop].astype(F32)
        for ref in refs
    )


def stack_kernel(own_ref, came_ref, out_ref, *, sums):
    rows = own_ref.shape[0] - sums
    out_ref[:rows] = own_ref[:rows]
    out_ref[rows : 2 * rows] = came_ref[:rows]
    if sums:
        split_store(out_ref, 2 * rows, split_sum((own_ref, came_ref), rows, rows + sums))


def place_rows(where_ref, digits, at):
    bits = 2 * (digits - 1)
    return where_ref[2] ^ sum(((at >> bit) & 1) << (bits - 1 - bit) for bit in range(bits))


def each_piece(where_ref, refs, digits, rows, use):
    owners = 4 ** (digits - 1)
    for step in range(4):
        column = where_ref[1] ^ step
        for at in range(owners):
            owner = place_rows(where_ref, digits, at)
            first = at * 2 * rows

            def load(low, high, first=first, step=step):
                if step < 3:
                    return refs[step][first + low : first + high]
                middle = refs[3].shape[0]
                start, stop = first + low, first + high
                if stop <= middle:
                    return refs[3][start:stop]
                if start >= middle:
                    return refs[4][start - middle : stop - middle]
                return jnp.concatenate([refs[3][start:middle], refs[4][: stop - middle]], axis=0)

            use(column, owner, load)


def finish_out_value_kernel(where_ref, *refs, digits):
    qkv_ref, out_ref = refs[5:]
    width = qkv_ref.shape[1]
    rows = width // 4 ** (digits - 1)
    few = rows * 128 // width

    def use(column, owner, load):
        start = pl.multiple_of(column * 128 + owner * few, few)
        out_ref[pl.ds(start, few), :] = jnp.concatenate(
            [load(at, at + few).astype(F32) for at in range(0, rows, few)], axis=1
        )
        lanes = pl.ds(pl.multiple_of(column * 128, 128), 128)
        qkv_ref[0, pl.ds(pl.multiple_of(owner * rows, rows), rows), lanes] = load(
            rows, 2 * rows
        ).astype(F32)

    each_piece(where_ref, refs[:5], digits, rows, use)


def finish_key_query_kernel(where_ref, *refs, digits, sums):
    qkv_ref, sums_ref = refs[6:]
    width = qkv_ref.shape[1]
    rows = width // 4 ** (digits - 1)

    def use(column, owner, load):
        lanes = pl.ds(pl.multiple_of(column * 128, 128), 128)
        down = pl.ds(pl.multiple_of(owner * rows, rows), rows)
        qkv_ref[1, down, lanes] = load(0, rows).astype(F32)
        qkv_ref[0, down, lanes] = load(rows, 2 * rows).astype(F32)

    each_piece(where_ref, refs[:5], digits, rows, use)
    total = refs[0].shape[0]
    half = refs[4].shape[0]
    sums_ref[...] = split_sum(refs[:3], total - sums, total) + split_sum(
        refs[4:5], half - sums, half
    )


def expert_grad_kernel(rows_ref, grads_ref, hidden_ref, dpre_ref, up_ref, down_ref, turned_ref):
    @pl.when(pl.program_id(0) == 0)
    def _():
        turned_ref[...] = rows_ref[...].T

    up_ref[...] = dot(turned_ref[...], dpre_ref[...])
    down_ref[...] = dot_tn(hidden_ref[...], grads_ref[...])


def norm1_back_kernel(packed_ref, x_ref, dresid_ref, gain_ref, out_ref, sums_ref, *, cap):
    count, width = x_ref.shape
    dh1 = unpack(packed_ref, slots_down(count), cap, width)
    normed, inverse = normalise(x_ref[...].astype(F32))
    out_ref[...] = dresid_ref[...] + norm_back(dh1, normed, inverse, gain_ref[...])
    store_sums(sums_ref, dh1, normed)


VMEM = pl.BlockSpec(memory_space=pltpu.VMEM)
SMEM = pl.BlockSpec(memory_space=pltpu.SMEM)


def after(value, *others):
    return lax.optimization_barrier((value, *others))[0]


def far(value):
    return pltpu.with_memory_space_constraint(value, pltpu.HBM)


def call(kernel, name, outs, args, flops, scalars=0, scratch=(), limit=16, away=(), out_away=(), raw=(), out_raw=()):
    shapes = [
        pltpu.HBM(shape, kind)
        if at in out_away or at in out_raw
        else jax.ShapeDtypeStruct(shape, kind)
        for at, (shape, kind) in enumerate(outs)
    ]

    def spec(at, away, raw):
        if at in raw:
            return pl.BlockSpec(memory_space=pltpu.HBM)
        return pl.BlockSpec() if at in away else VMEM

    size = sum(math.prod(a.shape) * a.dtype.itemsize for a in (*args, *shapes))
    return pl.pallas_call(
        kernel,
        name=name,
        out_shape=shapes,
        in_specs=[
            SMEM if at < scalars else spec(at, away, raw) for at in range(len(args))
        ],
        out_specs=[spec(at, out_away, out_raw) for at in range(len(outs))],
        scratch_shapes=list(scratch),
        cost_estimate=pl.CostEstimate(flops=flops, bytes_accessed=size, transcendentals=0),
        compiler_params=pltpu.CompilerParams(vmem_limit_bytes=limit * MIB),
    )(*[far(value) if at in away or at in raw else value for at, value in enumerate(args)])


def expert(h2, h2_other, upstream, upstream_other, w_up, w_down):
    count, width = h2.shape
    units = w_up.shape[1]
    tile = min(512, units)
    shapes = [
        ((2 * count, units), BF16),
        ((2 * count, units), BF16),
        ((count, width), F32),
        ((count, width), BF16),
        ((count, width), BF16),
        ((count, width), BF16),
        ((2 * count, width), BF16),
        ((2 * count, width), BF16),
    ]
    stay = (2, 3)
    both = pl.BlockSpec((2 * count, width), lambda j: (0, 0))
    rows = pl.BlockSpec((count, width), lambda j: (0, 0))
    by_unit = pl.BlockSpec((2 * count, tile), lambda j: (0, j))
    return pl.pallas_call(
        expert_kernel,
        name="expert",
        grid=(units // tile,),
        out_shape=[
            jax.ShapeDtypeStruct(shape, kind) if at in stay else pltpu.HBM(shape, kind)
            for at, (shape, kind) in enumerate(shapes)
        ],
        in_specs=[rows] * 4
        + [
            pl.BlockSpec((width, tile), lambda j: (0, j)),
            pl.BlockSpec((tile, width), lambda j: (j, 0)),
        ],
        out_specs=[by_unit, by_unit, rows, rows, rows, rows, both, both],
        scratch_shapes=[
            pltpu.VMEM((2 * count, width), F32),
            pltpu.VMEM((2 * count, width), F32),
        ],
        cost_estimate=pl.CostEstimate(
            flops=16 * count * width * units, bytes_accessed=16 * MIB, transcendentals=0
        ),
        compiler_params=pltpu.CompilerParams(vmem_limit_bytes=40 * MIB),
    )(h2, h2_other, upstream, upstream_other, far(w_up), far(w_down))


def expert_grads(rows, grads, hidden, dpre):
    count, width = rows.shape
    units = hidden.shape[1]
    tile = min(512, units)
    whole = pl.BlockSpec((count, width), lambda j: (0, 0))
    by_unit = pl.BlockSpec((count, tile), lambda j: (0, j))
    return pl.pallas_call(
        expert_grad_kernel,
        name="expert_grads",
        grid=(units // tile,),
        out_shape=[pltpu.HBM((width, units), F32), pltpu.HBM((units, width), F32)],
        in_specs=[whole] * 2 + [by_unit] * 2,
        out_specs=[
            pl.BlockSpec((width, tile), lambda j: (0, j)),
            pl.BlockSpec((tile, width), lambda j: (j, 0)),
        ],
        scratch_shapes=[pltpu.VMEM((width, count), BF16)],
        cost_estimate=pl.CostEstimate(
            flops=4 * count * width * units, bytes_accessed=24 * MIB, transcendentals=0
        ),
        compiler_params=pltpu.CompilerParams(vmem_limit_bytes=40 * MIB),
    )(far(rows), far(grads), far(hidden), far(dpre))


def flip(value, axis, bit):
    size = lax.axis_size(axis)
    return lax.ppermute(value, axis, [(i, i ^ bit) for i in range(size)])


def to_others(values, digit):
    return [
        flip(values[m] if isinstance(values, (list, tuple)) else values, "exp", m << (2 * digit))
        for m in range(1, 4)
    ]


def after_all(values, *others):
    return list(lax.optimization_barrier((*values, *others))[: len(values)])


def sum_and_spread(first, second, where, digits, sums, extra, finish):
    bits = 2 * (digits - 1)

    def across(value, bit):
        return flip(value, "exp", 4 << bit)

    def add(halves, came, bit, sums=None):
        owners, rows, columns = came.shape
        if bit + 1 < bits:
            return call(
                functools.partial(add_kernel, bit=bit + 1), "add",
                [((owners // 2, rows, columns), BF16)] * 2, [where, halves[0], came], 0, scalars=1,
                away=(1,), out_away=(0,),
            )
        if sums is None:
            return call(
                last_add_kernel, "last_add", [((rows, columns), BF16)], [halves[0], came], 0,
                away=(0,),
            )
        return call(
            last_add_sums_kernel, "last_add_sums", [((rows + extra, columns), BF16)],
            [halves[0], came, *sums], 0, away=(0,),
        )

    def stack(own, came, sums):
        rows, columns = own.shape
        return call(
            functools.partial(stack_kernel, sums=sums), "stack",
            [((2 * rows - sums, columns), BF16)], [own, came], 0,
        )[0]

    def steps(halves, sums, extra):
        for bit in range(bits):
            came = yield halves[1], [across(halves[1], bit)]
            halves = add(halves, came[0], bit, sums)
        total = halves[0]
        for bit in reversed(range(bits)):
            came = yield total, [across(total, bit)]
            total = stack(total, came[0], extra)
        by_x, by_y = yield total, [flip(total, "exp", 1), flip(total, "exp", 2)]
        middle = total.shape[0] // 2
        sent = [by_y[:middle], by_x[middle:]]
        halves = yield sent[0], [flip(sent[0], "exp", 1), flip(sent[1], "exp", 2)]
        yield None, [total, by_x, by_y, *halves]

    lines, states, last = [steps(first, None, 0), None], [None, None], None
    states[0] = next(lines[0])
    for at, line in enumerate([0] + [0, 1] * (2 * bits + 1) + [1]):
        if at == 1:
            pieces = second(last)
            lines[1], last = steps(pieces, sums, extra), pieces[1]
            states[1] = next(lines[1])
        came = states[line][1]
        states[line] = lines[line].send(came if last is None else after_all(came, last))
        last = states[line][0]
        if line == 0 and last is None:
            finished = finish(states[0][1])
            last = finished[1]
    return finished, states[1][1]


def on_device(
    block_input,
    dispatch,
    lengths,
    ln1_gain,
    ln1_bias,
    ln2_gain,
    ln2_bias,
    w_qkv,
    w_out,
    w_up,
    w_down,
    grad_output,
):
    slots, width = block_input.shape
    seq_rows = dispatch.shape[0]
    n_exp = lax.axis_size("exp")
    devices = n_exp * lax.axis_size("head")
    cap = slots // devices
    span = 2 * seq_rows
    columns = w_qkv.shape[2]
    scale = 1.0 / math.sqrt(HEAD_DIM)
    digits = (n_exp.bit_length() - 1) // 2
    place = lax.axis_index("exp")
    where = jnp.stack(
        [lax.axis_index("head"), place & 3, place >> 2]
    ).astype(jnp.int32)
    step = 128
    reach = 3 * seq_rows // 4
    packed = ((devices * 8, cap * 128), BF16)
    moving = 2 * devices * 8 * max(slots, seq_rows) * width * 3
    gain1, bias1 = ln1_gain.reshape(1, width), ln1_bias.reshape(1, width)
    gain2, bias2 = ln2_gain.reshape(1, width), ln2_bias.reshape(1, width)
    down, along = dispatch.reshape(seq_rows, 1), dispatch.reshape(1, seq_rows)

    def exchange(value):
        value = value.reshape(devices, 8, cap * 128)
        value = lax.all_to_all(value, ("exp", "head"), split_axis=0, concat_axis=0, tiled=True)
        return value.reshape(devices * 8, cap * 128)

    def cross(value):
        return flip(value, "head", 1)

    (h1,) = call(
        functools.partial(norm1_kernel, cap=cap), "norm1", [packed],
        [block_input, gain1, bias1], moving, away=(0, 1, 2),
    )
    arrived = exchange(h1)
    (own,) = call(
        functools.partial(gather_kernel, cap=cap), "gather1", [((seq_rows, width), BF16)],
        [arrived, down], moving,
    )
    other = cross(own)
    own_copy, inputs, qkv, context, logsum, attn_kept, attn_sent = call(
        functools.partial(attend_kernel, step=step, reach=reach, scale=scale),
        "attend",
        [
            ((seq_rows, width), BF16),
            ((span, width), BF16),
            ((3, span, columns), BF16),
            ((span, columns), BF16),
            ((128, span), F32),
            ((seq_rows, width), F32),
            ((seq_rows, width), BF16),
        ],
        [where, lengths, own, other, w_qkv, w_out],
        2 * span * width * columns * 4 + 16 * span * span * columns,
        scalars=2,
        limit=24,
        raw=(4, 5),
        out_raw=range(5),
        scratch=[
            pltpu.VMEM((3, width, columns), BF16),
            pltpu.VMEM((columns, width), BF16),
            pltpu.VMEM((span, width), BF16),
            pltpu.VMEM((3, span, columns), BF16),
            pltpu.VMEM((span, columns), BF16),
            pltpu.VMEM((128, span), F32),
            pltpu.SemaphoreType.DMA((9,)),
        ],
    )
    (sent,) = call(
        functools.partial(scatter_kernel, cap=cap, fill=True), "scatter1", [packed],
        [attn_kept, cross(attn_sent), along], moving,
    )
    attn_back = exchange(sent)
    near_own = after(own_copy, sent)
    by_x, by_y = flip(near_own, "exp", 1), flip(near_own, "exp", 2)
    by_xy = flip(after(own_copy, attn_back), "exp", 3)
    attn_back = after(attn_back, by_x, by_y)
    resid, h2, upstream, valid = call(
        functools.partial(norm2_kernel, cap=cap),
        "norm2",
        [((slots, width), F32), ((slots, width), BF16), ((slots, width), BF16), ((slots, 128), F32)],
        [attn_back, block_input, grad_output, gain2, bias2],
        moving,
    )
    h2_other, upstream_other = cross(h2), cross(upstream)
    hidden, dpre, dh2_kept, dh2_sent, branch_kept, branch_sent, rows_all, grads_all = expert(
        h2, h2_other, upstream, upstream_other, w_up[0], w_down[0]
    )
    dh2_sent = after(dh2_sent, by_xy)
    dresid, sent, sums2 = call(
        functools.partial(norm2_back_kernel, cap=cap),
        "norm2_back",
        [((slots, width), F32), packed, ((width // 64, 128), F32)],
        [dh2_kept, cross(dh2_sent), resid, grad_output, gain2],
        moving,
    )
    arrived = exchange(sent)
    plane_own = [after(rows, sent) for rows in (by_x, by_y, by_xy)]
    plane_other = [cross(rows) for rows in plane_own]
    hidden = after(hidden, sent)
    grad_up, grad_down = expert_grads(rows_all, grads_all, hidden, dpre)
    arrived, grad_up, grad_down, *plane_other = lax.optimization_barrier(
        (arrived, grad_up, grad_down, *plane_other)
    )
    branch = branch_kept.astype(F32) + cross(branch_sent).astype(F32)
    result = (resid + valid[:, :1] * branch).astype(BF16)
    (own,) = call(
        functools.partial(gather_kernel, cap=cap), "gather2", [((seq_rows, width), BF16)],
        [arrived, down], moving,
    )
    other = cross(own)
    piece = 4 * width // n_exp
    dattn, *out_pieces = call(
        out_grad_kernel,
        "out_grad",
        [((span, width), BF16), *[((n_exp // 4, piece, 128), BF16)] * 4],
        [where, own, other, context],
        2 * span * width * columns,
        scalars=1,
        scratch=[
            pltpu.VMEM((span, columns), BF16),
            pltpu.VMEM((columns, width), F32),
            pltpu.VMEM((4, n_exp // 4, piece, 128), BF16),
            pltpu.SemaphoreType.DMA((5,)),
        ],
        raw=(3,),
        out_raw=range(1, 5),
    )
    out_parts = [out_pieces[0], *to_others(out_pieces, 0)]
    du_kept, du_sent, *parts = call(
        functools.partial(attend_back_kernel, step=step, reach=reach, scale=scale),
        "attend_back",
        [
            ((seq_rows, width), F32),
            ((seq_rows, width), BF16),
            *[((span, 128), BF16)] * 4,
            *[((2, span, 128), BF16)] * 4,
        ],
        [where, lengths, dattn, qkv, context, logsum, w_qkv, w_out],
        2 * span * width * columns * 4 + 40 * span * span * columns,
        scalars=2,
        limit=24,
        raw=range(3, 8),
        out_raw=range(2, 10),
        scratch=[
            pltpu.VMEM((span, columns), BF16),
            pltpu.VMEM((16, span), F32),
            pltpu.VMEM((span, columns), F32),
            pltpu.VMEM((3, span, columns), BF16),
            pltpu.VMEM((3, span, columns), BF16),
            pltpu.VMEM((span, columns), BF16),
            pltpu.VMEM((128, span), F32),
            pltpu.VMEM((3, width, columns), BF16),
            pltpu.VMEM((columns, width), BF16),
            pltpu.SemaphoreType.DMA((17,)),
        ],
    )
    du_sent, *parts = after_all([du_sent, *parts], *out_parts[1:])
    value_parts = [parts[0], *to_others(parts[:4], 0)]
    key_query_parts = [parts[4], *to_others(after_all(parts[4:], *value_parts[1:]), 0)]
    (sent,) = call(
        functools.partial(scatter_kernel, cap=cap, fill=False), "scatter2", [packed],
        [du_kept, cross(du_sent), along], moving,
    )
    arrived = exchange(after(sent, *value_parts[1:]))
    input_grad, sums1 = call(
        functools.partial(norm1_back_kernel, cap=cap),
        "norm1_back",
        [((slots, width), F32), ((width // 64, 128), F32)],
        [arrived, block_input, dresid, gain1],
        moving,
        away=(1, 2, 3),
        out_away=(0,),
    )
    tokens = [inputs, *plane_own, *plane_other]
    split = [((n_exp // 8, 2 * piece, 128), BF16)] * 2
    product = 8 * span * width * 128
    out_value = call(
        value_grad_kernel, "value_grad", split, [where, *value_parts, *tokens, *out_parts],
        product, scalars=1, scratch=[pltpu.VMEM((width, 128), F32)], away=(1, *range(5, 13)),
        out_away=(0,),
    )

    def key_query(last):
        came = after_all(key_query_parts[1:], last)
        return call(
            key_query_grad_kernel, "key_query_grad", split,
            [where, key_query_parts[0], *came, *tokens], 2 * product, scalars=1,
            scratch=[pltpu.VMEM((width, 128), F32)], away=(1, *range(5, 12)), out_away=(0,),
        )

    sums = [sums1, cross(sums1), sums2, cross(sums2)]
    extra = 4 * sums1.shape[0]
    whole_qkv = pltpu.HBM((3, width, columns), F32)
    finish = pl.pallas_call(
        functools.partial(finish_out_value_kernel, digits=digits),
        name="finish_out_value",
        grid=(1,),
        out_shape=[whole_qkv, pltpu.HBM((columns, width), F32)],
        in_specs=[SMEM] + [VMEM] * 5,
        out_specs=[
            pl.BlockSpec((1, width, columns), lambda i: (2, 0, 0)),
            pl.BlockSpec((columns, width), lambda i: (0, 0)),
        ],
        cost_estimate=pl.CostEstimate(flops=0, bytes_accessed=6 * MIB, transcendentals=0),
        compiler_params=pltpu.CompilerParams(vmem_limit_bytes=40 * MIB),
    )
    (grad_qkv, grad_out), key_query = sum_and_spread(
        out_value, key_query, where, digits, sums, extra, lambda parts: finish(where, *parts)
    )
    grad_qkv, sums = pl.pallas_call(
        functools.partial(finish_key_query_kernel, digits=digits, sums=extra),
        name="finish_key_query",
        grid=(1,),
        out_shape=[whole_qkv, jax.ShapeDtypeStruct((extra // 2, 128), F32)],
        in_specs=[SMEM] + [VMEM] * 5 + [pl.BlockSpec(memory_space=pltpu.HBM)],
        out_specs=[
            pl.BlockSpec((2, width, columns), lambda i: (0, 0, 0)),
            pl.BlockSpec((extra // 2, 128), lambda i: (0, 0)),
        ],
        input_output_aliases={6: 0},
        cost_estimate=pl.CostEstimate(flops=0, bytes_accessed=6 * MIB, transcendentals=0),
        compiler_params=pltpu.CompilerParams(vmem_limit_bytes=40 * MIB),
    )(where, *key_query, grad_qkv)
    sums = sums.reshape(4, width)
    return (
        result,
        input_grad,
        sums[0],
        sums[1],
        sums[2],
        sums[3],
        grad_qkv,
        grad_out,
        grad_up[None],
        grad_down[None],
    )


def solution(mesh):
    placed = (
        P(("exp", "head"), None),
        P(("exp", "head")),
        P("exp", None),
        P(),
        P(),
        P(),
        P(),
        P(None, None, "head"),
        P("head", None),
        P("exp", None, "head"),
        P("exp", "head", None),
        P(("exp", "head"), None),
    )
    return jax.shard_map(
        on_device,
        mesh=mesh,
        in_specs=placed,
        out_specs=(
            P(("exp", "head"), None),
            P(("exp", "head"), None),
            P(),
            P(),
            P(),
            P(),
            P(None, None, "head"),
            P("head", None),
            P("exp", None, "head"),
            P("exp", "head", None),
        ),
        check_vma=False,
    )
```

```python
import functools
import math

import jax
import jax.numpy as jnp
from jax import lax
from jax.experimental import pallas as pl
from jax.experimental.pallas import tpu as pltpu
from jax.sharding import PartitionSpec as P

HEAD_DIM = 64
EPS = 1e-05
BF16 = jnp.bfloat16
F32 = jnp.float32
MIB = 1024 * 1024
EMPTY = 1e30


def dot(left, right):
    return lax.dot_general(left, right, (((1,), (0,)), ((), ())), preferred_element_type=F32)


def dot_nt(left, right):
    return lax.dot_general(left, right, (((1,), (1,)), ((), ())), preferred_element_type=F32)


def dot_tn(left, right):
    return lax.dot_general(left, right, (((0,), (0,)), ((), ())), preferred_element_type=F32)


def normalise(rows):
    mean = jnp.mean(rows, axis=1, keepdims=True)
    centred = rows - mean
    inverse = lax.rsqrt(jnp.mean(centred * centred, axis=1, keepdims=True) + EPS)
    return centred * inverse, inverse


def norm_back(upstream, normed, inverse, gain):
    scaled = upstream * gain
    first = jnp.mean(scaled, axis=1, keepdims=True)
    second = jnp.mean(scaled * normed, axis=1, keepdims=True)
    return inverse * (scaled - first - normed * second)


def pack(out_ref, rows, slot_of, cap, fill):
    total, width = out_ref.shape[0], rows.shape[1]
    place = lax.broadcasted_iota(jnp.int32, (total, slot_of.shape[1]), 0)
    first = (place >> 3) * cap
    sub = lax.broadcasted_iota(jnp.int32, (total, 128), 0) & 7
    piece = width // 8

    def placed(target):
        hit = (slot_of == target).astype(F32)
        moved = dot(hit.astype(BF16), rows)
        if fill:
            moved = moved + (1.0 - jnp.sum(hit, axis=1, keepdims=True)) * EMPTY
        return moved

    whole = cap // 8
    for group in range(whole):
        moved = placed(first + (place & 7) + group * 8)
        out_ref[:, group * width : (group + 1) * width] = moved.astype(BF16)
    for left in range(cap % 8):
        moved = placed(first + whole * 8 + left)
        folded = moved[:, :piece]
        for s in range(1, 8):
            folded = jnp.where(sub == s, moved[:, s * piece : (s + 1) * piece], folded)
        start = whole * width + left * piece
        out_ref[:, start : start + piece] = folded.astype(BF16)


def unpack(packed_ref, slot_of, cap, width):
    total = packed_ref.shape[0]
    place = lax.broadcasted_iota(jnp.int32, (slot_of.shape[0], total), 1)
    first = (place >> 3) * cap
    piece = width // 8
    sub = lax.broadcasted_iota(jnp.int32, (total, piece), 0) & 7
    whole = cap // 8
    rows = None
    for group in range(whole):
        hit = (slot_of == first + (place & 7) + group * 8).astype(BF16)
        part = dot(hit, packed_ref[:, group * width : (group + 1) * width])
        rows = part if rows is None else rows + part
    for left in range(cap % 8):
        start = whole * width + left * piece
        folded = packed_ref[:, start : start + piece].astype(F32)
        spread = jnp.concatenate(
            [jnp.where(sub == s, folded, 0.0).astype(BF16) for s in range(8)], axis=1
        )
        hit = (slot_of == first + whole * 8 + left).astype(BF16)
        part = dot(hit, spread)
        rows = part if rows is None else rows + part
    return rows


def slots_down(count):
    return lax.broadcasted_iota(jnp.int32, (count, 1), 0)


def norm1_kernel(x_ref, gain_ref, bias_ref, out_ref, *, cap):
    normed, _ = normalise(x_ref[...].astype(F32))
    rows = (normed * gain_ref[...] + bias_ref[...]).astype(BF16)
    slot_of = lax.broadcasted_iota(jnp.int32, (1, rows.shape[0]), 1)
    pack(out_ref, rows, slot_of, cap, False)


def gather_kernel(packed_ref, dispatch_ref, out_ref, *, cap):
    out_ref[...] = unpack(packed_ref, dispatch_ref[...], cap, out_ref.shape[1]).astype(BF16)


def two_heads(rows):
    lane = lax.broadcasted_iota(jnp.int32, rows.shape, 1)
    clear = jnp.zeros_like(rows)
    return jnp.concatenate(
        [jnp.where(lane < HEAD_DIM, rows, clear), jnp.where(lane < HEAD_DIM, clear, rows)], axis=0
    )


def started(source, target, sem):
    copy = pltpu.make_async_copy(source, target, sem)
    copy.start()
    return copy


def segments(lengths_ref, places):
    seg = jnp.zeros(places.shape, jnp.int32)
    end = 0
    for index in range(lengths_ref.shape[1]):
        end = end + lengths_ref[0, index]
        seg = seg + (places >= end).astype(jnp.int32)
    return seg


def attend_kernel(
    where_ref,
    lengths_ref,
    own_ref,
    other_ref,
    w_qkv_far,
    w_out_far,
    own_far,
    input_far,
    qkv_far,
    context_far,
    logsum_far,
    kept_ref,
    sent_ref,
    w_qkv_ref,
    w_out_ref,
    input_ref,
    qkv_ref,
    context_ref,
    logsum_ref,
    sems,
    *,
    step,
    reach,
    scale,
):
    weights = [
        started(w_qkv_far.at[which], w_qkv_ref.at[which], sems.at[which]) for which in range(3)
    ]
    last_weight = started(w_out_far, w_out_ref, sems.at[3])
    leaving = [started(own_ref, own_far, sems.at[4])]
    half = own_ref.shape[0]
    span = 2 * half
    here = where_ref[0]
    own_start = pl.multiple_of(here * half, half)
    other_start = pl.multiple_of((1 - here) * half, half)
    input_ref[pl.ds(own_start, half), :] = own_ref[...]
    input_ref[pl.ds(other_start, half), :] = other_ref[...]
    leaving.append(started(input_ref, input_far, sems.at[5]))
    for which in range(3):
        weights[which].wait()
        qkv_ref[which] = dot(input_ref[...], w_qkv_ref[which]).astype(BF16)
    leaving.append(started(qkv_ref, qkv_far, sems.at[6]))
    heads = qkv_ref.shape[2] // HEAD_DIM
    for start in range(0, span, step):
        stop = start + step
        low = max(0, start - reach)
        shape = (step, stop - low)
        query_at = lax.broadcasted_iota(jnp.int32, shape, 0) + start
        key_at = lax.broadcasted_iota(jnp.int32, shape, 1) + low
        allowed = (segments(lengths_ref, query_at) == segments(lengths_ref, key_at)) & (
            key_at <= query_at
        )
        allowed = jnp.concatenate([allowed.astype(F32)] * heads, axis=0) > 0.5
        lane = lax.broadcasted_iota(jnp.int32, (step, 2 * HEAD_DIM), 1)
        pairs = [
            slice(at, at + 2 * HEAD_DIM) for at in range(0, heads * HEAD_DIM, 2 * HEAD_DIM)
        ]
        scores = jnp.concatenate(
            [
                dot_nt(two_heads(qkv_ref[0, start:stop, columns]), qkv_ref[1, low:stop, columns])
                for columns in pairs
            ],
            axis=0,
        )
        scores = jnp.where(allowed, scores * scale, -1e30)
        top = jnp.max(scores, axis=1, keepdims=True)
        expo = jnp.exp(scores - top)
        total = jnp.sum(expo, axis=1, keepdims=True)
        probs = (expo * (1.0 / total)).astype(BF16)
        logsum = top + jnp.log(total)
        logsums = jnp.zeros((step, 128), F32)
        logsum_lane = lax.broadcasted_iota(jnp.int32, (step, 128), 1)
        for head in range(heads):
            mine = logsum[head * step : (head + 1) * step]
            logsums = jnp.where(logsum_lane == head, mine, logsums)
        for at, columns in enumerate(pairs):
            both = dot(
                probs[2 * at * step : 2 * (at + 1) * step], qkv_ref[2, low:stop, columns]
            )
            context_ref[start:stop, columns] = jnp.where(
                lane < HEAD_DIM, both[:step], both[step:]
            ).astype(BF16)
        logsum_ref[:, start:stop] = logsums.T
    leaving.append(started(context_ref, context_far, sems.at[7]))
    leaving.append(started(logsum_ref, logsum_far, sems.at[8]))
    last_weight.wait()
    sent_ref[...] = dot(context_ref[pl.ds(other_start, half), :], w_out_ref[...]).astype(BF16)
    kept_ref[...] = dot(context_ref[pl.ds(own_start, half), :], w_out_ref[...])
    for copy in leaving:
        copy.wait()


def scatter_kernel(kept_ref, came_ref, dispatch_ref, out_ref, *, cap, fill):
    rows = (kept_ref[...] + came_ref[...].astype(F32)).astype(BF16)
    pack(out_ref, rows, dispatch_ref[...], cap, fill)


def norm2_kernel(
    packed_ref, x_ref, grad_ref, gain_ref, bias_ref, resid_ref, h2_ref, up_ref, valid_ref, *, cap
):
    count, width = x_ref.shape
    moved = unpack(packed_ref, slots_down(count), cap, width)
    valid = (moved[:, :1] < 0.5 * EMPTY).astype(F32)
    resid = x_ref[...].astype(F32) + jnp.where(moved < 0.5 * EMPTY, moved, 0.0)
    resid_ref[...] = resid
    normed, _ = normalise(resid)
    h2_ref[...] = (normed * gain_ref[...] + bias_ref[...]).astype(BF16)
    up_ref[...] = (grad_ref[...].astype(F32) * valid).astype(BF16)
    valid_ref[...] = jnp.broadcast_to(valid, valid_ref.shape)


def gelu_and_slope(pre):
    root = math.sqrt(2.0 / math.pi)
    square = pre * pre
    bent = jnp.tanh(pre * (root + (root * 0.044715) * square))
    half = 0.5 + 0.5 * bent
    slope = half + (0.5 * pre) * (1.0 - bent * bent) * (root + (3.0 * 0.044715 * root) * square)
    return pre * half, slope


def expert_kernel(
    h2_ref,
    h2_other_ref,
    up_ref,
    up_other_ref,
    w_up_ref,
    w_down_ref,
    hidden_ref,
    dpre_ref,
    dh2_kept_ref,
    dh2_sent_ref,
    rows_ref,
    grads_ref,
    dh2_ref,
):
    count = h2_ref.shape[0]

    @pl.when(pl.program_id(0) == 0)
    def _():
        rows_ref[:count] = h2_ref[...]
        rows_ref[count:] = h2_other_ref[...]
        grads_ref[:count] = up_ref[...]
        grads_ref[count:] = up_other_ref[...]
        dh2_ref[...] = jnp.zeros_like(dh2_ref)

    w_up, w_down = w_up_ref[...], w_down_ref[...]
    pre = dot(rows_ref[...], w_up)
    gelu, slope = gelu_and_slope(pre)
    hidden = gelu.astype(BF16)
    hidden_ref[...] = hidden
    dpre = (dot_nt(grads_ref[...], w_down) * slope).astype(BF16)
    dpre_ref[...] = dpre
    dh2_ref[...] += dot_nt(dpre, w_up)

    @pl.when(pl.program_id(0) == pl.num_programs(0) - 1)
    def _():
        dh2_kept_ref[...] = dh2_ref[:count]
        dh2_sent_ref[...] = dh2_ref[count:].astype(BF16)


def store_sums(sums_ref, upstream, normed):
    for which, total in enumerate((upstream * normed, upstream)):
        total = jnp.sum(total, axis=0, keepdims=True)
        pieces = total.shape[1] // 128
        for at in range(pieces):
            row = which * pieces + at
            sums_ref[row : row + 1] = total[:, at * 128 : (at + 1) * 128]


def norm2_back_kernel(
    kept_ref,
    came_ref,
    resid_ref,
    grad_ref,
    gain_ref,
    dresid_far,
    packed_ref,
    sums_ref,
    dresid_ref,
    sem,
    *,
    cap,
):
    dh2 = kept_ref[...] + came_ref[...].astype(F32)
    normed, inverse = normalise(resid_ref[...])
    dresid = grad_ref[...].astype(F32) + norm_back(dh2, normed, inverse, gain_ref[...])
    dresid_ref[...] = dresid
    leaving = started(dresid_ref, dresid_far, sem)
    slot_of = lax.broadcasted_iota(jnp.int32, (1, dh2.shape[0]), 1)
    pack(packed_ref, dresid.astype(BF16), slot_of, cap, False)
    store_sums(sums_ref, dh2, normed)
    leaving.wait()


def out_grad_kernel(where_ref, own_ref, other_ref, context_far, dattn_ref, *rest):
    piece_fars, (context_ref, grad_ref, piece_ref, sems) = rest[:4], rest[4:]
    arriving = started(context_far, context_ref, sems.at[4])
    half = own_ref.shape[0]
    here = where_ref[0]
    dattn_ref[pl.ds(pl.multiple_of(here * half, half), half), :] = own_ref[...]
    dattn_ref[pl.ds(pl.multiple_of((1 - here) * half, half), half), :] = other_ref[...]
    arriving.wait()
    grad_ref[...] = dot_tn(context_ref[...], dattn_ref[...])
    width = grad_ref.shape[1]
    quarter = grad_ref.shape[0] // 4
    owners = piece_ref.shape[1]
    rows = quarter // owners
    leaving = []
    for step in (1, 2, 3, 0):
        first = (where_ref[1] ^ step) * quarter
        for owner in range(owners):
            start = pl.multiple_of(first + owner * rows, rows)
            block = grad_ref[pl.ds(start, rows), :]
            piece_ref[step, owner] = jnp.concatenate(
                [block[:, at : at + 128] for at in range(0, width, 128)], axis=0
            ).astype(BF16)
        leaving.append(started(piece_ref.at[step], piece_fars[step], sems.at[step]))
    for copy in leaving:
        copy.wait()


def attend_back_kernel(
    where_ref,
    lengths_ref,
    dattn_ref,
    qkv_far,
    context_far,
    logsum_far,
    w_qkv_far,
    w_out_far,
    kept_ref,
    sent_ref,
    *rest,
    step,
    reach,
    scale,
):
    dvalue_fars, dkq_fars = rest[:4], rest[4:8]
    dcontext_ref, inner_ref, dquery_ref, dqkv_ref = rest[8:12]
    qkv_ref, context_ref, logsum_ref, w_qkv_ref, w_out_ref, sems = rest[12:]
    arriving = [
        started(source, target, sems.at[at])
        for at, (source, target) in enumerate(
            (
                (w_out_far, w_out_ref),
                (context_far, context_ref),
                (qkv_far, qkv_ref),
                (logsum_far, logsum_ref),
                (w_qkv_far, w_qkv_ref),
            )
        )
    ]
    half = kept_ref.shape[0]
    span = 2 * half
    here = where_ref[0]
    own_start = pl.multiple_of(here * half, half)
    other_start = pl.multiple_of((1 - here) * half, half)
    arriving[0].wait()
    dcontext = dot_nt(dattn_ref[...], w_out_ref[...]).astype(BF16)
    dcontext_ref[...] = dcontext
    arriving[1].wait()
    arriving[2].wait()
    arriving[3].wait()
    heads = qkv_ref.shape[2] // HEAD_DIM
    columns_all = qkv_ref.shape[2]
    product = dcontext.astype(F32) * context_ref[...].astype(F32)
    coarse = product.astype(BF16)
    fine = (product - coarse.astype(F32)).astype(BF16)
    of_head = (
        lax.broadcasted_iota(jnp.int32, (16, columns_all), 1) // HEAD_DIM
        == lax.broadcasted_iota(jnp.int32, (16, columns_all), 0)
    ).astype(BF16)
    inner_ref[...] = dot_nt(of_head, coarse) + dot_nt(of_head, fine)
    dquery_ref[...] = jnp.zeros_like(dquery_ref)
    for start in range(0, span, step):
        stop = start + step
        high = min(span, stop + reach)
        shape = (step, high - start)
        key_at = lax.broadcasted_iota(jnp.int32, shape, 0) + start
        query_at = lax.broadcasted_iota(jnp.int32, shape, 1) + start
        allowed = (segments(lengths_ref, query_at) == segments(lengths_ref, key_at)) & (
            key_at <= query_at
        )
        allowed = jnp.concatenate([allowed.astype(F32)] * heads, axis=0) > 0.5
        lane = lax.broadcasted_iota(jnp.int32, (step, 2 * HEAD_DIM), 1)
        pairs = [
            slice(at, at + 2 * HEAD_DIM) for at in range(0, heads * HEAD_DIM, 2 * HEAD_DIM)
        ]
        keys = [two_heads(qkv_ref[1, start:stop, columns]) for columns in pairs]

        def by_head(ref, start=start, high=high):
            return jnp.concatenate(
                [
                    jnp.broadcast_to(ref[head : head + 1, start:high], (step, high - start))
                    for head in range(heads)
                ],
                axis=0,
            )

        scores = jnp.concatenate(
            [
                dot_nt(keys[at], qkv_ref[0, start:high, columns])
                for at, columns in enumerate(pairs)
            ],
            axis=0,
        )
        probs = jnp.exp(jnp.where(allowed, scores * scale - by_head(logsum_ref), -1e30))
        dprobs = jnp.concatenate(
            [
                dot_nt(two_heads(qkv_ref[2, start:stop, columns]), dcontext_ref[start:high, columns])
                for columns in pairs
            ],
            axis=0,
        )
        dscores = (probs * (dprobs - by_head(inner_ref))).astype(BF16)
        probs = probs.astype(BF16)
        for at, columns in enumerate(pairs):
            mine = slice(2 * at * step, 2 * (at + 1) * step)
            dvalues = dot(probs[mine], dcontext_ref[start:high, columns])
            dkeys = dot(dscores[mine], qkv_ref[0, start:high, columns])
            dquery_ref[start:high, columns] += dot_tn(dscores[mine], keys[at])
            dqkv_ref[1, start:stop, columns] = (
                jnp.where(lane < HEAD_DIM, dkeys[:step], dkeys[step:]) * scale
            ).astype(BF16)
            dqkv_ref[2, start:stop, columns] = jnp.where(
                lane < HEAD_DIM, dvalues[:step], dvalues[step:]
            ).astype(BF16)
    dqkv_ref[0] = (dquery_ref[...] * scale).astype(BF16)

    quarter = columns_all // 4
    leaving = []
    for kind, at in ((2, 1), (2, 2), (2, 3), (1, 1), (0, 1), (1, 2), (0, 2), (1, 3), (0, 3), (2, 0), (1, 0), (0, 0)):
        first = pl.multiple_of((where_ref[1] ^ at) * quarter, quarter)
        target = dvalue_fars[at] if kind == 2 else dkq_fars[at].at[1 - kind]
        leaving.append(
            started(dqkv_ref.at[kind, :, pl.ds(first, quarter)], target, sems.at[5 + kind * 4 + at])
        )
    arriving[4].wait()

    def back_rows(start):
        total = dot_nt(dqkv_ref[0, pl.ds(start, half), :], w_qkv_ref[0])
        total = total + dot_nt(dqkv_ref[1, pl.ds(start, half), :], w_qkv_ref[1])
        return total + dot_nt(dqkv_ref[2, pl.ds(start, half), :], w_qkv_ref[2])

    sent_ref[...] = back_rows(other_start).astype(BF16)
    kept_ref[...] = back_rows(own_start)
    for copy in leaving:
        copy.wait()


def token_grad(where_ref, grad_refs, index, input_ref, own_refs, other_refs):
    half = own_refs[0].shape[0]
    own_start = pl.multiple_of(where_ref[0] * half, half)
    other_start = pl.multiple_of((1 - where_ref[0]) * half, half)

    def rows(ref, start, count):
        return ref[pl.ds(start, count), :] if index is None else ref[index, pl.ds(start, count), :]

    total = dot_tn(rows(grad_refs[0], 0, 2 * half), input_ref[...])
    for grad_ref, own_ref, other_ref in zip(grad_refs[1:], own_refs, other_refs):
        total = total + dot_tn(rows(grad_ref, own_start, half), own_ref[...])
        total = total + dot_tn(rows(grad_ref, other_start, half), other_ref[...])
    return total.T


def store_halves(where_ref, bit, half_refs, load, at):
    rows = at.stop - at.start
    for side, half_ref in enumerate(half_refs):
        mine = ((where_ref[2] >> bit) & 1) ^ side
        for index in range(half_ref.shape[0]):
            half_ref[index, at] = load(2 * index + mine, rows).astype(BF16)


def value_grad_kernel(where_ref, *refs):
    grad_refs, input_ref, own_refs, other_refs = refs[0:4], refs[4], refs[5:8], refs[8:11]
    out_refs, half_refs, total_ref = refs[11:15], refs[15:17], refs[17]
    total_ref[...] = token_grad(where_ref, grad_refs, None, input_ref, own_refs, other_refs)
    rows = half_refs[0].shape[1] // 2
    store_halves(
        where_ref, 0, half_refs,
        lambda owner, rows: sum(ref[owner].astype(F32) for ref in out_refs), slice(0, rows),
    )
    store_halves(
        where_ref, 0, half_refs,
        lambda owner, rows: total_ref[pl.ds(pl.multiple_of(owner * rows, rows), rows), :],
        slice(rows, 2 * rows),
    )


def key_query_grad_kernel(where_ref, *refs):
    grad_refs, input_ref, own_refs, other_refs = refs[0:4], refs[4], refs[5:8], refs[8:11]
    half_refs, total_ref = refs[11:13], refs[13]
    rows = half_refs[0].shape[1] // 2
    for index in range(2):
        total_ref[...] = token_grad(where_ref, grad_refs, index, input_ref, own_refs, other_refs)
        store_halves(
            where_ref, 0, half_refs,
            lambda owner, rows: total_ref[pl.ds(pl.multiple_of(owner * rows, rows), rows), :],
            slice(index * rows, (index + 1) * rows),
        )


def add_kernel(where_ref, kept_ref, came_ref, *half_refs, bit):
    store_halves(
        where_ref, bit, half_refs,
        lambda owner, rows: kept_ref[owner].astype(F32) + came_ref[owner].astype(F32),
        slice(0, kept_ref.shape[1]),
    )


def last_add_kernel(kept_ref, came_ref, out_ref):
    out_ref[...] = (kept_ref[0].astype(F32) + came_ref[0].astype(F32)).astype(BF16)


def split_store(out_ref, start, value):
    rows = value.shape[0]
    coarse = value.astype(BF16)
    out_ref[start : start + rows] = coarse
    out_ref[start + rows : start + 2 * rows] = (value - coarse.astype(F32)).astype(BF16)


def last_add_sums_kernel(kept_ref, came_ref, *refs):
    out_ref = refs[4]
    rows = kept_ref.shape[1]
    out_ref[:rows] = (kept_ref[0].astype(F32) + came_ref[0].astype(F32)).astype(BF16)
    sums = jnp.concatenate([refs[0][...] + refs[1][...], refs[2][...] + refs[3][...]], axis=0)
    split_store(out_ref, rows, sums)


def split_sum(refs, start, stop):
    rows = (stop - start) // 2
    return sum(
        ref[start : start + rows].astype(F32) + ref[start + rows : stop].astype(F32)
        for ref in refs
    )


def stack_kernel(own_ref, came_ref, out_ref, *, sums):
    rows = own_ref.shape[0] - sums
    out_ref[:rows] = own_ref[:rows]
    out_ref[rows : 2 * rows] = came_ref[:rows]
    if sums:
        split_store(out_ref, 2 * rows, split_sum((own_ref, came_ref), rows, rows + sums))


def place_rows(where_ref, digits, at):
    bits = 2 * (digits - 1)
    return where_ref[2] ^ sum(((at >> bit) & 1) << (bits - 1 - bit) for bit in range(bits))


def each_piece(where_ref, refs, digits, rows, use):
    owners = 4 ** (digits - 1)
    for step in range(4):
        column = where_ref[1] ^ step
        for at in range(owners):
            owner = place_rows(where_ref, digits, at)
            first = at * 2 * rows

            def load(low, high, first=first, step=step):
                if step < 3:
                    return refs[step][first + low : first + high]
                middle = refs[3].shape[0]
                start, stop = first + low, first + high
                if stop <= middle:
                    return refs[3][start:stop]
                if start >= middle:
                    return refs[4][start - middle : stop - middle]
                return jnp.concatenate([refs[3][start:middle], refs[4][: stop - middle]], axis=0)

            use(column, owner, load)


def finish_out_value_kernel(where_ref, *refs, digits):
    qkv_ref, out_ref = refs[5:]
    width = qkv_ref.shape[1]
    rows = width // 4 ** (digits - 1)
    few = rows * 128 // width

    def use(column, owner, load):
        start = pl.multiple_of(column * 128 + owner * few, few)
        out_ref[pl.ds(start, few), :] = jnp.concatenate(
            [load(at, at + few).astype(F32) for at in range(0, rows, few)], axis=1
        )
        lanes = pl.ds(pl.multiple_of(column * 128, 128), 128)
        qkv_ref[0, pl.ds(pl.multiple_of(owner * rows, rows), rows), lanes] = load(
            rows, 2 * rows
        ).astype(F32)

    each_piece(where_ref, refs[:5], digits, rows, use)


def finish_key_query_kernel(where_ref, *refs, digits, sums):
    qkv_ref, sums_ref = refs[6:]
    width = qkv_ref.shape[1]
    rows = width // 4 ** (digits - 1)

    def use(column, owner, load):
        lanes = pl.ds(pl.multiple_of(column * 128, 128), 128)
        down = pl.ds(pl.multiple_of(owner * rows, rows), rows)
        qkv_ref[1, down, lanes] = load(0, rows).astype(F32)
        qkv_ref[0, down, lanes] = load(rows, 2 * rows).astype(F32)

    each_piece(where_ref, refs[:5], digits, rows, use)
    total = refs[0].shape[0]
    half = refs[4].shape[0]
    sums_ref[...] = split_sum(refs[:3], total - sums, total) + split_sum(
        refs[4:5], half - sums, half
    )


def expert_grad_kernel(rows_ref, grads_ref, hidden_ref, dpre_ref, up_ref, down_ref, turned_ref):
    @pl.when(pl.program_id(0) == 0)
    def _():
        turned_ref[...] = rows_ref[...].T

    up_ref[...] = dot(turned_ref[...], dpre_ref[...])
    down_ref[...] = dot_tn(hidden_ref[...], grads_ref[...])


def branch_kernel(hidden_ref, w_down_ref, kept_ref, sent_ref, branch_ref):
    @pl.when(pl.program_id(0) == 0)
    def _():
        branch_ref[...] = jnp.zeros_like(branch_ref)

    branch_ref[...] += dot(hidden_ref[...], w_down_ref[...])

    @pl.when(pl.program_id(0) == pl.num_programs(0) - 1)
    def _():
        count = kept_ref.shape[0]
        kept_ref[...] = branch_ref[:count].astype(BF16)
        sent_ref[...] = branch_ref[count:].astype(BF16)


def norm1_back_kernel(packed_ref, x_ref, dresid_ref, gain_ref, out_ref, sums_ref, *, cap):
    count, width = x_ref.shape
    dh1 = unpack(packed_ref, slots_down(count), cap, width)
    normed, inverse = normalise(x_ref[...].astype(F32))
    out_ref[...] = dresid_ref[...] + norm_back(dh1, normed, inverse, gain_ref[...])
    store_sums(sums_ref, dh1, normed)


VMEM = pl.BlockSpec(memory_space=pltpu.VMEM)
SMEM = pl.BlockSpec(memory_space=pltpu.SMEM)


def after(value, *others):
    return lax.optimization_barrier((value, *others))[0]


def far(value):
    return pltpu.with_memory_space_constraint(value, pltpu.HBM)


def call(kernel, name, outs, args, flops, scalars=0, scratch=(), limit=16, away=(), out_away=(), raw=(), out_raw=()):
    shapes = [
        pltpu.HBM(shape, kind)
        if at in out_away or at in out_raw
        else jax.ShapeDtypeStruct(shape, kind)
        for at, (shape, kind) in enumerate(outs)
    ]

    def spec(at, away, raw):
        if at in raw:
            return pl.BlockSpec(memory_space=pltpu.HBM)
        return pl.BlockSpec() if at in away else VMEM

    size = sum(math.prod(a.shape) * a.dtype.itemsize for a in (*args, *shapes))
    return pl.pallas_call(
        kernel,
        name=name,
        out_shape=shapes,
        in_specs=[
            SMEM if at < scalars else spec(at, away, raw) for at in range(len(args))
        ],
        out_specs=[spec(at, out_away, out_raw) for at in range(len(outs))],
        scratch_shapes=list(scratch),
        cost_estimate=pl.CostEstimate(flops=flops, bytes_accessed=size, transcendentals=0),
        compiler_params=pltpu.CompilerParams(vmem_limit_bytes=limit * MIB),
    )(*[far(value) if at in away or at in raw else value for at, value in enumerate(args)])


def expert(h2, h2_other, upstream, upstream_other, w_up, w_down):
    count, width = h2.shape
    units = w_up.shape[1]
    tile = min(512, units)
    shapes = [
        ((2 * count, units), BF16),
        ((2 * count, units), BF16),
        ((count, width), F32),
        ((count, width), BF16),
        ((2 * count, width), BF16),
        ((2 * count, width), BF16),
    ]
    stay = (2, 3)
    both = pl.BlockSpec((2 * count, width), lambda j: (0, 0))
    rows = pl.BlockSpec((count, width), lambda j: (0, 0))
    by_unit = pl.BlockSpec((2 * count, tile), lambda j: (0, j))
    return pl.pallas_call(
        expert_kernel,
        name="expert",
        grid=(units // tile,),
        out_shape=[
            jax.ShapeDtypeStruct(shape, kind) if at in stay else pltpu.HBM(shape, kind)
            for at, (shape, kind) in enumerate(shapes)
        ],
        in_specs=[rows] * 4
        + [
            pl.BlockSpec((width, tile), lambda j: (0, j)),
            pl.BlockSpec((tile, width), lambda j: (j, 0)),
        ],
        out_specs=[by_unit, by_unit, rows, rows, both, both],
        scratch_shapes=[
            pltpu.VMEM((2 * count, width), F32),
        ],
        cost_estimate=pl.CostEstimate(
            flops=12 * count * width * units, bytes_accessed=16 * MIB, transcendentals=0
        ),
        compiler_params=pltpu.CompilerParams(vmem_limit_bytes=40 * MIB),
    )(h2, h2_other, upstream, upstream_other, far(w_up), far(w_down))


def expert_grads(rows, grads, hidden, dpre):
    count, width = rows.shape
    units = hidden.shape[1]
    tile = min(512, units)
    whole = pl.BlockSpec((count, width), lambda j: (0, 0))
    by_unit = pl.BlockSpec((count, tile), lambda j: (0, j))
    return pl.pallas_call(
        expert_grad_kernel,
        name="expert_grads",
        grid=(units // tile,),
        out_shape=[pltpu.HBM((width, units), F32), pltpu.HBM((units, width), F32)],
        in_specs=[whole] * 2 + [by_unit] * 2,
        out_specs=[
            pl.BlockSpec((width, tile), lambda j: (0, j)),
            pl.BlockSpec((tile, width), lambda j: (j, 0)),
        ],
        scratch_shapes=[pltpu.VMEM((width, count), BF16)],
        cost_estimate=pl.CostEstimate(
            flops=4 * count * width * units, bytes_accessed=24 * MIB, transcendentals=0
        ),
        compiler_params=pltpu.CompilerParams(vmem_limit_bytes=40 * MIB),
    )(far(rows), far(grads), far(hidden), far(dpre))


def expert_branch(hidden, w_down):
    count, units = hidden.shape
    width = w_down.shape[1]
    tile = min(512, units)
    half = pl.BlockSpec((count // 2, width), lambda j: (0, 0))
    return pl.pallas_call(
        branch_kernel,
        name="expert_branch",
        grid=(units // tile,),
        out_shape=[pltpu.HBM((count // 2, width), BF16)] * 2,
        in_specs=[
            pl.BlockSpec((count, tile), lambda j: (0, j)),
            pl.BlockSpec((tile, width), lambda j: (j, 0)),
        ],
        out_specs=[half, half],
        scratch_shapes=[pltpu.VMEM((count, width), F32)],
        cost_estimate=pl.CostEstimate(
            flops=2 * count * width * units, bytes_accessed=8 * MIB, transcendentals=0
        ),
        compiler_params=pltpu.CompilerParams(vmem_limit_bytes=20 * MIB),
    )(far(hidden), far(w_down))


def flip(value, axis, bit):
    size = lax.axis_size(axis)
    return lax.ppermute(value, axis, [(i, i ^ bit) for i in range(size)])


def to_others(values, digit):
    return [
        flip(values[m] if isinstance(values, (list, tuple)) else values, "exp", m << (2 * digit))
        for m in range(1, 4)
    ]


def after_all(values, *others):
    return list(lax.optimization_barrier((*values, *others))[: len(values)])


def sum_and_spread(first, second, where, digits, sums, extra, finish, first_wait):
    bits = 2 * (digits - 1)

    def across(value, bit):
        return flip(value, "exp", 4 << bit)

    def add(halves, came, bit, sums=None):
        owners, rows, columns = came.shape
        if bit + 1 < bits:
            return call(
                functools.partial(add_kernel, bit=bit + 1), "add",
                [((owners // 2, rows, columns), BF16)] * 2, [where, halves[0], came], 0, scalars=1,
                away=(1,), out_away=(0,),
            )
        if sums is None:
            return call(
                last_add_kernel, "last_add", [((rows, columns), BF16)], [halves[0], came], 0,
                away=(0,),
            )
        return call(
            last_add_sums_kernel, "last_add_sums", [((rows + extra, columns), BF16)],
            [halves[0], came, *sums], 0, away=(0,),
        )

    def stack(own, came, sums):
        rows, columns = own.shape
        return call(
            functools.partial(stack_kernel, sums=sums), "stack",
            [((2 * rows - sums, columns), BF16)], [own, came], 0,
        )[0]

    def steps(halves, sums, extra):
        for bit in range(bits):
            came = yield halves[1], [across(halves[1], bit)]
            halves = add(halves, came[0], bit, sums)
        total = halves[0]
        for bit in reversed(range(bits)):
            came = yield total, [across(total, bit)]
            total = stack(total, came[0], extra)
        by_x, by_y = yield total, [flip(total, "exp", 1), flip(total, "exp", 2)]
        middle = total.shape[0] // 2
        sent = [by_y[:middle], by_x[middle:]]
        halves = yield sent[0], [flip(sent[0], "exp", 1), flip(sent[1], "exp", 2)]
        yield None, [total, by_x, by_y, *halves]

    lines, states, last = [steps(first, None, 0), None], [None, None], first_wait
    states[0] = next(lines[0])
    for at, line in enumerate([0] + [0, 1] * (2 * bits + 1) + [1]):
        if at == 1:
            pieces = second(last)
            lines[1], last = steps(pieces, sums, extra), pieces[1]
            states[1] = next(lines[1])
        came = states[line][1]
        states[line] = lines[line].send(came if last is None else after_all(came, last))
        last = states[line][0]
        if line == 0 and last is None:
            finished = finish(states[0][1])
            last = finished[1]
    return finished, states[1][1]


def on_device(
    block_input,
    dispatch,
    lengths,
    ln1_gain,
    ln1_bias,
    ln2_gain,
    ln2_bias,
    w_qkv,
    w_out,
    w_up,
    w_down,
    grad_output,
):
    slots, width = block_input.shape
    seq_rows = dispatch.shape[0]
    n_exp = lax.axis_size("exp")
    devices = n_exp * lax.axis_size("head")
    cap = slots // devices
    span = 2 * seq_rows
    columns = w_qkv.shape[2]
    scale = 1.0 / math.sqrt(HEAD_DIM)
    digits = (n_exp.bit_length() - 1) // 2
    place = lax.axis_index("exp")
    where = jnp.stack(
        [lax.axis_index("head"), place & 3, place >> 2]
    ).astype(jnp.int32)
    step = 128
    reach = 3 * seq_rows // 4
    packed = ((devices * 8, cap * 128), BF16)
    moving = 2 * devices * 8 * max(slots, seq_rows) * width * 3
    gain1, bias1 = ln1_gain.reshape(1, width), ln1_bias.reshape(1, width)
    gain2, bias2 = ln2_gain.reshape(1, width), ln2_bias.reshape(1, width)
    down, along = dispatch.reshape(seq_rows, 1), dispatch.reshape(1, seq_rows)

    def exchange(value):
        value = value.reshape(devices, 8, cap * 128)
        value = lax.all_to_all(value, ("exp", "head"), split_axis=0, concat_axis=0, tiled=True)
        return value.reshape(devices * 8, cap * 128)

    def cross(value):
        return flip(value, "head", 1)

    (h1,) = call(
        functools.partial(norm1_kernel, cap=cap), "norm1", [packed],
        [block_input, gain1, bias1], moving, away=(0, 1, 2),
    )
    arrived = exchange(h1)
    (own,) = call(
        functools.partial(gather_kernel, cap=cap), "gather1", [((seq_rows, width), BF16)],
        [arrived, down], moving,
    )
    other = cross(own)
    own_copy, inputs, qkv, context, logsum, attn_kept, attn_sent = call(
        functools.partial(attend_kernel, step=step, reach=reach, scale=scale),
        "attend",
        [
            ((seq_rows, width), BF16),
            ((span, width), BF16),
            ((3, span, columns), BF16),
            ((span, columns), BF16),
            ((128, span), F32),
            ((seq_rows, width), F32),
            ((seq_rows, width), BF16),
        ],
        [where, lengths, own, other, w_qkv, w_out],
        2 * span * width * columns * 4 + 16 * span * span * columns,
        scalars=2,
        limit=24,
        raw=(4, 5),
        out_raw=range(5),
        scratch=[
            pltpu.VMEM((3, width, columns), BF16),
            pltpu.VMEM((columns, width), BF16),
            pltpu.VMEM((span, width), BF16),
            pltpu.VMEM((3, span, columns), BF16),
            pltpu.VMEM((span, columns), BF16),
            pltpu.VMEM((128, span), F32),
            pltpu.SemaphoreType.DMA((9,)),
        ],
    )
    (sent,) = call(
        functools.partial(scatter_kernel, cap=cap, fill=True), "scatter1", [packed],
        [attn_kept, cross(attn_sent), along], moving,
    )
    attn_back = exchange(sent)
    by_xy = flip(after(own_copy, attn_back), "exp", 3)
    resid, h2, upstream, valid = call(
        functools.partial(norm2_kernel, cap=cap),
        "norm2",
        [((slots, width), F32), ((slots, width), BF16), ((slots, width), BF16), ((slots, 128), F32)],
        [attn_back, block_input, grad_output, gain2, bias2],
        moving,
    )
    h2_other, upstream_other = cross(h2), cross(upstream)
    hidden, dpre, dh2_kept, dh2_sent, rows_all, grads_all = expert(
        h2, h2_other, upstream, upstream_other, w_up[0], w_down[0]
    )
    dh2_sent = after(dh2_sent, by_xy)
    dresid, sent, sums2 = call(
        functools.partial(norm2_back_kernel, cap=cap),
        "norm2_back",
        [((slots, width), F32), packed, ((width // 64, 128), F32)],
        [dh2_kept, cross(dh2_sent), resid, grad_output, gain2],
        moving,
        out_raw=(0,),
        scratch=[pltpu.VMEM((slots, width), F32), pltpu.SemaphoreType.DMA],
    )
    arrived = exchange(sent)
    near_own, hidden, far_own = after_all([own_copy, hidden, by_xy], sent)
    by_x, by_y = flip(near_own, "exp", 1), flip(near_own, "exp", 2)
    far_other = cross(far_own)
    grad_up, grad_down = expert_grads(rows_all, grads_all, hidden, dpre)
    arrived, grad_up, grad_down, by_x, by_y, far_other = lax.optimization_barrier(
        (arrived, grad_up, grad_down, by_x, by_y, far_other)
    )
    plane_own = [by_x, by_y, far_own]
    plane_other = [cross(by_x), cross(by_y), far_other]
    (own,) = call(
        functools.partial(gather_kernel, cap=cap), "gather2", [((seq_rows, width), BF16)],
        [arrived, down], moving,
    )
    other = cross(own)
    piece = 4 * width // n_exp
    dattn, *out_pieces = call(
        out_grad_kernel,
        "out_grad",
        [((span, width), BF16), *[((n_exp // 4, piece, 128), BF16)] * 4],
        [where, own, other, context],
        2 * span * width * columns,
        scalars=1,
        scratch=[
            pltpu.VMEM((span, columns), BF16),
            pltpu.VMEM((columns, width), F32),
            pltpu.VMEM((4, n_exp // 4, piece, 128), BF16),
            pltpu.SemaphoreType.DMA((5,)),
        ],
        raw=(3,),
        out_raw=range(1, 5),
    )
    out_parts = [out_pieces[0], *to_others(out_pieces, 0)]
    du_kept, du_sent, *parts = call(
        functools.partial(attend_back_kernel, step=step, reach=reach, scale=scale),
        "attend_back",
        [
            ((seq_rows, width), F32),
            ((seq_rows, width), BF16),
            *[((span, 128), BF16)] * 4,
            *[((2, span, 128), BF16)] * 4,
        ],
        [where, lengths, dattn, qkv, context, logsum, w_qkv, w_out],
        2 * span * width * columns * 4 + 40 * span * span * columns,
        scalars=2,
        limit=24,
        raw=range(3, 8),
        out_raw=range(2, 10),
        scratch=[
            pltpu.VMEM((span, columns), BF16),
            pltpu.VMEM((16, span), F32),
            pltpu.VMEM((span, columns), F32),
            pltpu.VMEM((3, span, columns), BF16),
            pltpu.VMEM((3, span, columns), BF16),
            pltpu.VMEM((span, columns), BF16),
            pltpu.VMEM((128, span), F32),
            pltpu.VMEM((3, width, columns), BF16),
            pltpu.VMEM((columns, width), BF16),
            pltpu.SemaphoreType.DMA((17,)),
        ],
    )
    du_sent, *parts = after_all([du_sent, *parts], *out_parts[1:], *plane_other)
    value_parts = [parts[0], *to_others(parts[:4], 0)]
    key_query_parts = [parts[4], *to_others(after_all(parts[4:], *value_parts[1:]), 0)]
    (sent,) = call(
        functools.partial(scatter_kernel, cap=cap, fill=False), "scatter2", [packed],
        [du_kept, cross(du_sent), along], moving,
    )
    arrived = exchange(after(sent, *value_parts[1:]))
    input_grad, sums1 = call(
        functools.partial(norm1_back_kernel, cap=cap),
        "norm1_back",
        [((slots, width), F32), ((width // 64, 128), F32)],
        [arrived, block_input, dresid, gain1],
        moving,
        away=(1, 2, 3),
        out_away=(0,),
    )
    tokens = [inputs, *plane_own, *plane_other]
    split = [((n_exp // 8, 2 * piece, 128), BF16)] * 2
    product = 8 * span * width * 128
    out_value = call(
        value_grad_kernel, "value_grad", split, [where, *value_parts, *tokens, *out_parts],
        product, scalars=1, scratch=[pltpu.VMEM((width, 128), F32)], away=(1, *range(5, 13)),
        out_away=(0,),
    )
    branch_kept, branch_sent = expert_branch(after(hidden, out_value[1]), w_down[0])
    branch_came = cross(branch_sent)
    branch = branch_kept.astype(F32) + branch_came.astype(F32)
    result = (resid + valid[:, :1] * branch).astype(BF16)

    def key_query(last):
        came = after_all(key_query_parts[1:], last)
        return call(
            key_query_grad_kernel, "key_query_grad", split,
            [where, key_query_parts[0], *came, *tokens], 2 * product, scalars=1,
            scratch=[pltpu.VMEM((width, 128), F32)], away=(1, *range(5, 12)), out_away=(0,),
        )

    sums = [sums1, cross(sums1), sums2, cross(sums2)]
    extra = 4 * sums1.shape[0]
    whole_qkv = pltpu.HBM((3, width, columns), F32)
    finish = pl.pallas_call(
        functools.partial(finish_out_value_kernel, digits=digits),
        name="finish_out_value",
        grid=(1,),
        out_shape=[whole_qkv, pltpu.HBM((columns, width), F32)],
        in_specs=[SMEM] + [VMEM] * 5,
        out_specs=[
            pl.BlockSpec((1, width, columns), lambda i: (2, 0, 0)),
            pl.BlockSpec((columns, width), lambda i: (0, 0)),
        ],
        cost_estimate=pl.CostEstimate(flops=0, bytes_accessed=6 * MIB, transcendentals=0),
        compiler_params=pltpu.CompilerParams(vmem_limit_bytes=40 * MIB),
    )
    (grad_qkv, grad_out), key_query = sum_and_spread(
        out_value, key_query, where, digits, sums, extra, lambda parts: finish(where, *parts),
        branch_sent,
    )
    grad_qkv, sums = pl.pallas_call(
        functools.partial(finish_key_query_kernel, digits=digits, sums=extra),
        name="finish_key_query",
        grid=(1,),
        out_shape=[whole_qkv, jax.ShapeDtypeStruct((extra // 2, 128), F32)],
        in_specs=[SMEM] + [VMEM] * 5 + [pl.BlockSpec(memory_space=pltpu.HBM)],
        out_specs=[
            pl.BlockSpec((2, width, columns), lambda i: (0, 0, 0)),
            pl.BlockSpec((extra // 2, 128), lambda i: (0, 0)),
        ],
        input_output_aliases={6: 0},
        cost_estimate=pl.CostEstimate(flops=0, bytes_accessed=6 * MIB, transcendentals=0),
        compiler_params=pltpu.CompilerParams(vmem_limit_bytes=40 * MIB),
    )(where, *key_query, grad_qkv)
    sums = sums.reshape(4, width)
    return (
        result,
        input_grad,
        sums[0],
        sums[1],
        sums[2],
        sums[3],
        grad_qkv,
        grad_out,
        grad_up[None],
        grad_down[None],
    )


def solution(mesh):
    placed = (
        P(("exp", "head"), None),
        P(("exp", "head")),
        P("exp", None),
        P(),
        P(),
        P(),
        P(),
        P(None, None, "head"),
        P("head", None),
        P("exp", None, "head"),
        P("exp", "head", None),
        P(("exp", "head"), None),
    )
    return jax.shard_map(
        on_device,
        mesh=mesh,
        in_specs=placed,
        out_specs=(
            P(("exp", "head"), None),
            P(("exp", "head"), None),
            P(),
            P(),
            P(),
            P(),
            P(None, None, "head"),
            P("head", None),
            P("exp", None, "head"),
            P("exp", "head", None),
        ),
        check_vma=False,
    )
```

```python
import functools
import math

import jax
import jax.numpy as jnp
from jax import lax
from jax.experimental import pallas as pl
from jax.experimental.pallas import tpu as pltpu
from jax.sharding import PartitionSpec as P

HEAD_DIM = 64
EPS = 1e-05
BF16 = jnp.bfloat16
F32 = jnp.float32
MIB = 1024 * 1024
EMPTY = 1e30


def dot(left, right):
    return lax.dot_general(left, right, (((1,), (0,)), ((), ())), preferred_element_type=F32)


def dot_nt(left, right):
    return lax.dot_general(left, right, (((1,), (1,)), ((), ())), preferred_element_type=F32)


def dot_tn(left, right):
    return lax.dot_general(left, right, (((0,), (0,)), ((), ())), preferred_element_type=F32)


def normalise(rows):
    mean = jnp.mean(rows, axis=1, keepdims=True)
    centred = rows - mean
    inverse = lax.rsqrt(jnp.mean(centred * centred, axis=1, keepdims=True) + EPS)
    return centred * inverse, inverse


def norm_back(upstream, normed, inverse, gain):
    scaled = upstream * gain
    first = jnp.mean(scaled, axis=1, keepdims=True)
    second = jnp.mean(scaled * normed, axis=1, keepdims=True)
    return inverse * (scaled - first - normed * second)


def pack(out_ref, rows, slot_of, cap, fill):
    total, width = out_ref.shape[0], rows.shape[1]
    place = lax.broadcasted_iota(jnp.int32, (total, slot_of.shape[1]), 0)
    first = (place >> 3) * cap
    sub = lax.broadcasted_iota(jnp.int32, (total, 128), 0) & 7
    piece = width // 8

    def placed(target):
        hit = (slot_of == target).astype(F32)
        moved = dot(hit.astype(BF16), rows)
        if fill:
            moved = moved + (1.0 - jnp.sum(hit, axis=1, keepdims=True)) * EMPTY
        return moved

    whole = cap // 8
    for group in range(whole):
        moved = placed(first + (place & 7) + group * 8)
        out_ref[:, group * width : (group + 1) * width] = moved.astype(BF16)
    for left in range(cap % 8):
        moved = placed(first + whole * 8 + left)
        folded = moved[:, :piece]
        for s in range(1, 8):
            folded = jnp.where(sub == s, moved[:, s * piece : (s + 1) * piece], folded)
        start = whole * width + left * piece
        out_ref[:, start : start + piece] = folded.astype(BF16)


def unpack(packed_ref, slot_of, cap, width):
    total = packed_ref.shape[0]
    place = lax.broadcasted_iota(jnp.int32, (slot_of.shape[0], total), 1)
    first = (place >> 3) * cap
    piece = width // 8
    sub = lax.broadcasted_iota(jnp.int32, (total, piece), 0) & 7
    whole = cap // 8
    rows = None
    for group in range(whole):
        hit = (slot_of == first + (place & 7) + group * 8).astype(BF16)
        part = dot(hit, packed_ref[:, group * width : (group + 1) * width])
        rows = part if rows is None else rows + part
    for left in range(cap % 8):
        start = whole * width + left * piece
        folded = packed_ref[:, start : start + piece].astype(F32)
        spread = jnp.concatenate(
            [jnp.where(sub == s, folded, 0.0).astype(BF16) for s in range(8)], axis=1
        )
        hit = (slot_of == first + whole * 8 + left).astype(BF16)
        part = dot(hit, spread)
        rows = part if rows is None else rows + part
    return rows


def slots_down(count):
    return lax.broadcasted_iota(jnp.int32, (count, 1), 0)


def norm1_kernel(x_ref, gain_ref, bias_ref, out_ref, *, cap):
    normed, _ = normalise(x_ref[...].astype(F32))
    rows = (normed * gain_ref[...] + bias_ref[...]).astype(BF16)
    slot_of = lax.broadcasted_iota(jnp.int32, (1, rows.shape[0]), 1)
    pack(out_ref, rows, slot_of, cap, False)


def gather_kernel(packed_ref, dispatch_ref, out_ref, *, cap):
    out_ref[...] = unpack(packed_ref, dispatch_ref[...], cap, out_ref.shape[1]).astype(BF16)


def two_heads(rows):
    lane = lax.broadcasted_iota(jnp.int32, rows.shape, 1)
    clear = jnp.zeros_like(rows)
    return jnp.concatenate(
        [jnp.where(lane < HEAD_DIM, rows, clear), jnp.where(lane < HEAD_DIM, clear, rows)], axis=0
    )


def started(source, target, sem):
    copy = pltpu.make_async_copy(source, target, sem)
    copy.start()
    return copy


def segments(lengths_ref, places):
    seg = jnp.zeros(places.shape, jnp.int32)
    end = 0
    for index in range(lengths_ref.shape[1]):
        end = end + lengths_ref[0, index]
        seg = seg + (places >= end).astype(jnp.int32)
    return seg


def attend_kernel(
    where_ref,
    lengths_ref,
    own_ref,
    other_ref,
    w_qkv_far,
    w_out_far,
    own_far,
    input_far,
    qkv_far,
    context_far,
    logsum_far,
    kept_ref,
    sent_ref,
    w_qkv_ref,
    w_out_ref,
    input_ref,
    qkv_ref,
    context_ref,
    logsum_ref,
    sems,
    *,
    step,
    reach,
    scale,
):
    weights = [
        started(w_qkv_far.at[which], w_qkv_ref.at[which], sems.at[which]) for which in range(3)
    ]
    last_weight = started(w_out_far, w_out_ref, sems.at[3])
    leaving = [started(own_ref, own_far, sems.at[4])]
    half = own_ref.shape[0]
    span = 2 * half
    here = where_ref[0]
    own_start = pl.multiple_of(here * half, half)
    other_start = pl.multiple_of((1 - here) * half, half)
    input_ref[pl.ds(own_start, half), :] = own_ref[...]
    input_ref[pl.ds(other_start, half), :] = other_ref[...]
    leaving.append(started(input_ref, input_far, sems.at[5]))
    for which in range(3):
        weights[which].wait()
        qkv_ref[which] = dot(input_ref[...], w_qkv_ref[which]).astype(BF16)
    leaving.append(started(qkv_ref, qkv_far, sems.at[6]))
    heads = qkv_ref.shape[2] // HEAD_DIM
    for start in range(0, span, step):
        stop = start + step
        low = max(0, start - reach)
        shape = (step, stop - low)
        query_at = lax.broadcasted_iota(jnp.int32, shape, 0) + start
        key_at = lax.broadcasted_iota(jnp.int32, shape, 1) + low
        allowed = (segments(lengths_ref, query_at) == segments(lengths_ref, key_at)) & (
            key_at <= query_at
        )
        allowed = jnp.concatenate([allowed.astype(F32)] * heads, axis=0) > 0.5
        lane = lax.broadcasted_iota(jnp.int32, (step, 2 * HEAD_DIM), 1)
        pairs = [
            slice(at, at + 2 * HEAD_DIM) for at in range(0, heads * HEAD_DIM, 2 * HEAD_DIM)
        ]
        scores = jnp.concatenate(
            [
                dot_nt(two_heads(qkv_ref[0, start:stop, columns]), qkv_ref[1, low:stop, columns])
                for columns in pairs
            ],
            axis=0,
        )
        scores = jnp.where(allowed, scores * scale, -1e30)
        top = jnp.max(scores, axis=1, keepdims=True)
        expo = jnp.exp(scores - top)
        total = jnp.sum(expo, axis=1, keepdims=True)
        probs = (expo * (1.0 / total)).astype(BF16)
        logsum = top + jnp.log(total)
        logsums = jnp.zeros((step, 128), F32)
        logsum_lane = lax.broadcasted_iota(jnp.int32, (step, 128), 1)
        for head in range(heads):
            mine = logsum[head * step : (head + 1) * step]
            logsums = jnp.where(logsum_lane == head, mine, logsums)
        for at, columns in enumerate(pairs):
            both = dot(
                probs[2 * at * step : 2 * (at + 1) * step], qkv_ref[2, low:stop, columns]
            )
            context_ref[start:stop, columns] = jnp.where(
                lane < HEAD_DIM, both[:step], both[step:]
            ).astype(BF16)
        logsum_ref[:, start:stop] = logsums.T
    leaving.append(started(context_ref, context_far, sems.at[7]))
    leaving.append(started(logsum_ref, logsum_far, sems.at[8]))
    last_weight.wait()
    sent_ref[...] = dot(context_ref[pl.ds(other_start, half), :], w_out_ref[...]).astype(BF16)
    kept_ref[...] = dot(context_ref[pl.ds(own_start, half), :], w_out_ref[...])
    for copy in leaving:
        copy.wait()


def scatter_kernel(kept_ref, came_ref, dispatch_ref, out_ref, *, cap, fill):
    rows = (kept_ref[...] + came_ref[...].astype(F32)).astype(BF16)
    pack(out_ref, rows, dispatch_ref[...], cap, fill)


def norm2_kernel(
    packed_ref, x_ref, grad_ref, gain_ref, bias_ref, resid_ref, h2_ref, up_ref, valid_ref, *, cap
):
    count, width = x_ref.shape
    moved = unpack(packed_ref, slots_down(count), cap, width)
    valid = (moved[:, :1] < 0.5 * EMPTY).astype(F32)
    resid = x_ref[...].astype(F32) + jnp.where(moved < 0.5 * EMPTY, moved, 0.0)
    resid_ref[...] = resid
    normed, _ = normalise(resid)
    h2_ref[...] = (normed * gain_ref[...] + bias_ref[...]).astype(BF16)
    up_ref[...] = (grad_ref[...].astype(F32) * valid).astype(BF16)
    valid_ref[...] = jnp.broadcast_to(valid, valid_ref.shape)


def gelu_and_slope(pre):
    root = math.sqrt(2.0 / math.pi)
    square = pre * pre
    bent = jnp.tanh(pre * (root + (root * 0.044715) * square))
    half = 0.5 + 0.5 * bent
    slope = half + (0.5 * pre) * (1.0 - bent * bent) * (root + (3.0 * 0.044715 * root) * square)
    return pre * half, slope


def expert_kernel(
    h2_ref,
    h2_other_ref,
    up_ref,
    up_other_ref,
    w_up_ref,
    w_down_ref,
    hidden_ref,
    dpre_ref,
    dh2_kept_ref,
    dh2_sent_ref,
    rows_ref,
    grads_ref,
    dh2_ref,
):
    count = h2_ref.shape[0]

    @pl.when(pl.program_id(0) == 0)
    def _():
        rows_ref[:count] = h2_ref[...]
        rows_ref[count:] = h2_other_ref[...]
        grads_ref[:count] = up_ref[...]
        grads_ref[count:] = up_other_ref[...]
        dh2_ref[...] = jnp.zeros_like(dh2_ref)

    w_up, w_down = w_up_ref[...], w_down_ref[...]
    pre = dot(rows_ref[...], w_up)
    gelu, slope = gelu_and_slope(pre)
    hidden = gelu.astype(BF16)
    hidden_ref[...] = hidden
    dpre = (dot_nt(grads_ref[...], w_down) * slope).astype(BF16)
    dpre_ref[...] = dpre
    dh2_ref[...] += dot_nt(dpre, w_up)

    @pl.when(pl.program_id(0) == pl.num_programs(0) - 1)
    def _():
        dh2_kept_ref[...] = dh2_ref[:count]
        dh2_sent_ref[...] = dh2_ref[count:].astype(BF16)


def store_sums(sums_ref, upstream, normed):
    for which, total in enumerate((upstream * normed, upstream)):
        total = jnp.sum(total, axis=0, keepdims=True)
        pieces = total.shape[1] // 128
        for at in range(pieces):
            row = which * pieces + at
            sums_ref[row : row + 1] = total[:, at * 128 : (at + 1) * 128]


def norm2_back_kernel(
    kept_ref,
    came_ref,
    resid_ref,
    grad_ref,
    gain_ref,
    dresid_far,
    packed_ref,
    sums_ref,
    dresid_ref,
    sem,
    *,
    cap,
):
    dh2 = kept_ref[...] + came_ref[...].astype(F32)
    normed, inverse = normalise(resid_ref[...])
    dresid = grad_ref[...].astype(F32) + norm_back(dh2, normed, inverse, gain_ref[...])
    dresid_ref[...] = dresid
    leaving = started(dresid_ref, dresid_far, sem)
    slot_of = lax.broadcasted_iota(jnp.int32, (1, dh2.shape[0]), 1)
    pack(packed_ref, dresid.astype(BF16), slot_of, cap, False)
    store_sums(sums_ref, dh2, normed)
    leaving.wait()


def out_grad_kernel(where_ref, own_ref, other_ref, context_far, dattn_ref, *rest):
    piece_fars, (context_ref, grad_ref, piece_ref, sems) = rest[:4], rest[4:]
    arriving = started(context_far, context_ref, sems.at[4])
    half = own_ref.shape[0]
    here = where_ref[0]
    dattn_ref[pl.ds(pl.multiple_of(here * half, half), half), :] = own_ref[...]
    dattn_ref[pl.ds(pl.multiple_of((1 - here) * half, half), half), :] = other_ref[...]
    arriving.wait()
    grad_ref[...] = dot_tn(context_ref[...], dattn_ref[...])
    width = grad_ref.shape[1]
    quarter = grad_ref.shape[0] // 4
    owners = piece_ref.shape[1]
    rows = quarter // owners
    leaving = []
    for step in (1, 2, 3, 0):
        first = (where_ref[1] ^ step) * quarter
        for owner in range(owners):
            start = pl.multiple_of(first + owner * rows, rows)
            block = grad_ref[pl.ds(start, rows), :]
            piece_ref[step, owner] = jnp.concatenate(
                [block[:, at : at + 128] for at in range(0, width, 128)], axis=0
            ).astype(BF16)
        leaving.append(started(piece_ref.at[step], piece_fars[step], sems.at[step]))
    for copy in leaving:
        copy.wait()


def attend_back_kernel(
    where_ref,
    lengths_ref,
    dattn_ref,
    qkv_far,
    context_far,
    logsum_far,
    w_qkv_far,
    w_out_far,
    kept_ref,
    sent_ref,
    *rest,
    step,
    reach,
    scale,
):
    dvalue_fars, dkq_fars = rest[:4], rest[4:8]
    dcontext_ref, inner_ref, dquery_ref, dqkv_ref = rest[8:12]
    qkv_ref, context_ref, logsum_ref, w_qkv_ref, w_out_ref, sems = rest[12:]
    arriving = [
        started(source, target, sems.at[at])
        for at, (source, target) in enumerate(
            (
                (w_out_far, w_out_ref),
                (context_far, context_ref),
                (qkv_far, qkv_ref),
                (logsum_far, logsum_ref),
                (w_qkv_far, w_qkv_ref),
            )
        )
    ]
    half = kept_ref.shape[0]
    span = 2 * half
    here = where_ref[0]
    own_start = pl.multiple_of(here * half, half)
    other_start = pl.multiple_of((1 - here) * half, half)
    arriving[0].wait()
    dcontext = dot_nt(dattn_ref[...], w_out_ref[...]).astype(BF16)
    dcontext_ref[...] = dcontext
    arriving[1].wait()
    arriving[2].wait()
    arriving[3].wait()
    heads = qkv_ref.shape[2] // HEAD_DIM
    columns_all = qkv_ref.shape[2]
    product = dcontext.astype(F32) * context_ref[...].astype(F32)
    coarse = product.astype(BF16)
    fine = (product - coarse.astype(F32)).astype(BF16)
    of_head = (
        lax.broadcasted_iota(jnp.int32, (16, columns_all), 1) // HEAD_DIM
        == lax.broadcasted_iota(jnp.int32, (16, columns_all), 0)
    ).astype(BF16)
    inner_ref[...] = dot_nt(of_head, coarse) + dot_nt(of_head, fine)
    dquery_ref[...] = jnp.zeros_like(dquery_ref)
    for start in range(0, span, step):
        stop = start + step
        high = min(span, stop + reach)
        shape = (step, high - start)
        key_at = lax.broadcasted_iota(jnp.int32, shape, 0) + start
        query_at = lax.broadcasted_iota(jnp.int32, shape, 1) + start
        allowed = (segments(lengths_ref, query_at) == segments(lengths_ref, key_at)) & (
            key_at <= query_at
        )
        allowed = jnp.concatenate([allowed.astype(F32)] * heads, axis=0) > 0.5
        lane = lax.broadcasted_iota(jnp.int32, (step, 2 * HEAD_DIM), 1)
        pairs = [
            slice(at, at + 2 * HEAD_DIM) for at in range(0, heads * HEAD_DIM, 2 * HEAD_DIM)
        ]
        keys = [two_heads(qkv_ref[1, start:stop, columns]) for columns in pairs]

        def by_head(ref, start=start, high=high):
            return jnp.concatenate(
                [
                    jnp.broadcast_to(ref[head : head + 1, start:high], (step, high - start))
                    for head in range(heads)
                ],
                axis=0,
            )

        scores = jnp.concatenate(
            [
                dot_nt(keys[at], qkv_ref[0, start:high, columns])
                for at, columns in enumerate(pairs)
            ],
            axis=0,
        )
        probs = jnp.exp(jnp.where(allowed, scores * scale - by_head(logsum_ref), -1e30))
        dprobs = jnp.concatenate(
            [
                dot_nt(two_heads(qkv_ref[2, start:stop, columns]), dcontext_ref[start:high, columns])
                for columns in pairs
            ],
            axis=0,
        )
        dscores = (probs * (dprobs - by_head(inner_ref))).astype(BF16)
        probs = probs.astype(BF16)
        for at, columns in enumerate(pairs):
            mine = slice(2 * at * step, 2 * (at + 1) * step)
            dvalues = dot(probs[mine], dcontext_ref[start:high, columns])
            dkeys = dot(dscores[mine], qkv_ref[0, start:high, columns])
            dquery_ref[start:high, columns] += dot_tn(dscores[mine], keys[at])
            dqkv_ref[1, start:stop, columns] = (
                jnp.where(lane < HEAD_DIM, dkeys[:step], dkeys[step:]) * scale
            ).astype(BF16)
            dqkv_ref[2, start:stop, columns] = jnp.where(
                lane < HEAD_DIM, dvalues[:step], dvalues[step:]
            ).astype(BF16)
    dqkv_ref[0] = (dquery_ref[...] * scale).astype(BF16)

    quarter = columns_all // 4
    leaving = []
    for kind, at in ((2, 1), (2, 2), (2, 3), (1, 1), (0, 1), (1, 2), (0, 2), (1, 3), (0, 3), (2, 0), (1, 0), (0, 0)):
        first = pl.multiple_of((where_ref[1] ^ at) * quarter, quarter)
        target = dvalue_fars[at] if kind == 2 else dkq_fars[at].at[1 - kind]
        leaving.append(
            started(dqkv_ref.at[kind, :, pl.ds(first, quarter)], target, sems.at[5 + kind * 4 + at])
        )
    arriving[4].wait()

    def back_rows(start):
        total = dot_nt(dqkv_ref[0, pl.ds(start, half), :], w_qkv_ref[0])
        total = total + dot_nt(dqkv_ref[1, pl.ds(start, half), :], w_qkv_ref[1])
        return total + dot_nt(dqkv_ref[2, pl.ds(start, half), :], w_qkv_ref[2])

    sent_ref[...] = back_rows(other_start).astype(BF16)
    kept_ref[...] = back_rows(own_start)
    for copy in leaving:
        copy.wait()


def token_grad(where_ref, grad_refs, index, input_ref, own_refs, other_refs):
    half = own_refs[0].shape[0]
    own_start = pl.multiple_of(where_ref[0] * half, half)
    other_start = pl.multiple_of((1 - where_ref[0]) * half, half)

    def rows(ref, start, count):
        return ref[pl.ds(start, count), :] if index is None else ref[index, pl.ds(start, count), :]

    total = dot_tn(rows(grad_refs[0], 0, 2 * half), input_ref[...])
    for grad_ref, own_ref, other_ref in zip(grad_refs[1:], own_refs, other_refs):
        total = total + dot_tn(rows(grad_ref, own_start, half), own_ref[...])
        total = total + dot_tn(rows(grad_ref, other_start, half), other_ref[...])
    return total.T


def store_halves(where_ref, bit, half_refs, load, at):
    rows = at.stop - at.start
    for side, half_ref in enumerate(half_refs):
        mine = ((where_ref[2] >> bit) & 1) ^ side
        for index in range(half_ref.shape[0]):
            half_ref[index, at] = load(2 * index + mine, rows).astype(BF16)


def value_grad_kernel(where_ref, *refs):
    grad_refs, input_ref, own_refs, other_refs = refs[0:4], refs[4], refs[5:8], refs[8:11]
    out_refs, half_refs, total_ref = refs[11:15], refs[15:17], refs[17]
    total_ref[...] = token_grad(where_ref, grad_refs, None, input_ref, own_refs, other_refs)
    rows = half_refs[0].shape[1] // 2
    store_halves(
        where_ref, 0, half_refs,
        lambda owner, rows: sum(ref[owner].astype(F32) for ref in out_refs), slice(0, rows),
    )
    store_halves(
        where_ref, 0, half_refs,
        lambda owner, rows: total_ref[pl.ds(pl.multiple_of(owner * rows, rows), rows), :],
        slice(rows, 2 * rows),
    )


def key_query_grad_kernel(where_ref, *refs):
    grad_refs, input_ref, own_refs, other_refs = refs[0:4], refs[4], refs[5:8], refs[8:11]
    half_refs, total_ref = refs[11:13], refs[13]
    rows = half_refs[0].shape[1] // 2
    for index in range(2):
        total_ref[...] = token_grad(where_ref, grad_refs, index, input_ref, own_refs, other_refs)
        store_halves(
            where_ref, 0, half_refs,
            lambda owner, rows: total_ref[pl.ds(pl.multiple_of(owner * rows, rows), rows), :],
            slice(index * rows, (index + 1) * rows),
        )


def add_kernel(where_ref, kept_ref, came_ref, *half_refs, bit):
    store_halves(
        where_ref, bit, half_refs,
        lambda owner, rows: kept_ref[owner].astype(F32) + came_ref[owner].astype(F32),
        slice(0, kept_ref.shape[1]),
    )


def last_add_kernel(kept_ref, came_ref, out_ref):
    out_ref[...] = (kept_ref[0].astype(F32) + came_ref[0].astype(F32)).astype(BF16)


def split_store(out_ref, start, value):
    rows = value.shape[0]
    coarse = value.astype(BF16)
    out_ref[start : start + rows] = coarse
    out_ref[start + rows : start + 2 * rows] = (value - coarse.astype(F32)).astype(BF16)


def last_add_sums_kernel(kept_ref, came_ref, *refs):
    out_ref = refs[4]
    rows = kept_ref.shape[1]
    out_ref[:rows] = (kept_ref[0].astype(F32) + came_ref[0].astype(F32)).astype(BF16)
    sums = jnp.concatenate([refs[0][...] + refs[1][...], refs[2][...] + refs[3][...]], axis=0)
    split_store(out_ref, rows, sums)


def split_sum(refs, start, stop):
    rows = (stop - start) // 2
    return sum(
        ref[start : start + rows].astype(F32) + ref[start + rows : stop].astype(F32)
        for ref in refs
    )


def stack_kernel(own_ref, came_ref, out_ref, *, sums):
    rows = own_ref.shape[0] - sums
    out_ref[:rows] = own_ref[:rows]
    out_ref[rows : 2 * rows] = came_ref[:rows]
    if sums:
        split_store(out_ref, 2 * rows, split_sum((own_ref, came_ref), rows, rows + sums))


def place_rows(where_ref, digits, at):
    bits = 2 * (digits - 1)
    return where_ref[2] ^ sum(((at >> bit) & 1) << (bits - 1 - bit) for bit in range(bits))


def each_piece(where_ref, refs, digits, rows, use, steps=range(4)):
    owners = 4 ** (digits - 1)
    for step in steps:
        column = where_ref[1] ^ step
        for at in range(owners):
            owner = place_rows(where_ref, digits, at)
            first = at * 2 * rows

            def load(low, high, first=first, step=step):
                if step < 3:
                    return refs[step][first + low : first + high]
                middle = refs[3].shape[0]
                start, stop = first + low, first + high
                if stop <= middle:
                    return refs[3][start:stop]
                if start >= middle:
                    return refs[4][start - middle : stop - middle]
                return jnp.concatenate([refs[3][start:middle], refs[4][: stop - middle]], axis=0)

            use(column, owner, load)


def out_value_pieces(where_ref, refs, digits, steps, value_ref, value_column, out_ref, out_first):
    width = value_ref.shape[1]
    rows = width // 4 ** (digits - 1)
    few = rows * 128 // width

    def use(column, owner, load):
        start = pl.multiple_of(out_first(column) + owner * few, few)
        out_ref[pl.ds(start, few), :] = jnp.concatenate(
            [load(at, at + few).astype(F32) for at in range(0, rows, few)], axis=1
        )
        lanes = pl.ds(pl.multiple_of(value_column(column), 128), 128)
        value_ref[0, pl.ds(pl.multiple_of(owner * rows, rows), rows), lanes] = load(
            rows, 2 * rows
        ).astype(F32)

    each_piece(where_ref, refs, digits, rows, use, steps)


def finish_out_value_near_kernel(where_ref, *refs, digits):
    value_ref, out_ref = refs[3:]

    def place(column):
        return column * 128

    out_value_pieces(where_ref, refs[:3], digits, range(3), value_ref, place, out_ref, place)


def finish_out_value_far_kernel(where_ref, *refs, digits):
    halves, (_, _, value_far, out_far, value_ref, out_ref, sems) = refs[:2], refs[2:]
    out_value_pieces(
        where_ref, (None, None, None, *halves), digits, range(3, 4),
        value_ref, lambda column: 0, out_ref, lambda column: 0,
    )
    first = pl.ds(pl.multiple_of((where_ref[1] ^ 3) * 128, 128), 128)
    leaving = [
        started(value_ref, value_far.at[pl.ds(2, 1), :, first], sems.at[0]),
        started(out_ref, out_far.at[first], sems.at[1]),
    ]
    for copy in leaving:
        copy.wait()


def finish_near_kernel(where_ref, *refs, digits, sums):
    qkv_ref, sums_ref = refs[4:]
    width = qkv_ref.shape[1]
    rows = width // 4 ** (digits - 1)

    def use(column, owner, load):
        lanes = pl.ds(pl.multiple_of(column * 128, 128), 128)
        down = pl.ds(pl.multiple_of(owner * rows, rows), rows)
        qkv_ref[1, down, lanes] = load(0, rows).astype(F32)
        qkv_ref[0, down, lanes] = load(rows, 2 * rows).astype(F32)

    each_piece(where_ref, refs[:3], digits, rows, use, range(3))
    total = refs[0].shape[0]
    sums_ref[...] = split_sum(refs[:3], total - sums, total)


def finish_far_kernel(where_ref, *refs, digits, sums):
    halves, near_sums_ref, _, qkv_far, sums_ref, total_ref, sem = refs[:2], *refs[2:]
    width = total_ref.shape[1]
    rows = width // 4 ** (digits - 1)

    def use(column, owner, load):
        down = pl.ds(pl.multiple_of(owner * rows, rows), rows)
        total_ref[1, down, :] = load(0, rows).astype(F32)
        total_ref[0, down, :] = load(rows, 2 * rows).astype(F32)

    each_piece(where_ref, (None, None, None, *halves), digits, rows, use, range(3, 4))
    lanes = pl.ds(pl.multiple_of((where_ref[1] ^ 3) * 128, 128), 128)
    leaving = started(total_ref, qkv_far.at[pl.ds(0, 2), :, lanes], sem)
    half = halves[1].shape[0]
    sums_ref[...] = near_sums_ref[...] + split_sum(halves[1:], half - sums, half)
    leaving.wait()


def expert_grad_kernel(rows_ref, grads_ref, hidden_ref, dpre_ref, up_ref, down_ref, turned_ref):
    @pl.when(pl.program_id(0) == 0)
    def _():
        turned_ref[...] = rows_ref[...].T

    up_ref[...] = dot(turned_ref[...], dpre_ref[...])
    down_ref[...] = dot_tn(hidden_ref[...], grads_ref[...])


def branch_kernel(hidden_ref, w_down_ref, kept_ref, sent_ref, branch_ref):
    @pl.when(pl.program_id(0) == 0)
    def _():
        branch_ref[...] = jnp.zeros_like(branch_ref)

    branch_ref[...] += dot(hidden_ref[...], w_down_ref[...])

    @pl.when(pl.program_id(0) == pl.num_programs(0) - 1)
    def _():
        count = kept_ref.shape[0]
        kept_ref[...] = branch_ref[:count].astype(BF16)
        sent_ref[...] = branch_ref[count:].astype(BF16)


def norm1_back_kernel(packed_ref, x_ref, dresid_ref, gain_ref, out_ref, sums_ref, *, cap):
    count, width = x_ref.shape
    dh1 = unpack(packed_ref, slots_down(count), cap, width)
    normed, inverse = normalise(x_ref[...].astype(F32))
    out_ref[...] = dresid_ref[...] + norm_back(dh1, normed, inverse, gain_ref[...])
    store_sums(sums_ref, dh1, normed)


VMEM = pl.BlockSpec(memory_space=pltpu.VMEM)
SMEM = pl.BlockSpec(memory_space=pltpu.SMEM)


def after(value, *others):
    return lax.optimization_barrier((value, *others))[0]


def far(value):
    return pltpu.with_memory_space_constraint(value, pltpu.HBM)


def call(kernel, name, outs, args, flops, scalars=0, scratch=(), limit=16, away=(), out_away=(), raw=(), out_raw=()):
    shapes = [
        pltpu.HBM(shape, kind)
        if at in out_away or at in out_raw
        else jax.ShapeDtypeStruct(shape, kind)
        for at, (shape, kind) in enumerate(outs)
    ]

    def spec(at, away, raw):
        if at in raw:
            return pl.BlockSpec(memory_space=pltpu.HBM)
        return pl.BlockSpec() if at in away else VMEM

    size = sum(math.prod(a.shape) * a.dtype.itemsize for a in (*args, *shapes))
    return pl.pallas_call(
        kernel,
        name=name,
        out_shape=shapes,
        in_specs=[
            SMEM if at < scalars else spec(at, away, raw) for at in range(len(args))
        ],
        out_specs=[spec(at, out_away, out_raw) for at in range(len(outs))],
        scratch_shapes=list(scratch),
        cost_estimate=pl.CostEstimate(flops=flops, bytes_accessed=size, transcendentals=0),
        compiler_params=pltpu.CompilerParams(vmem_limit_bytes=limit * MIB),
    )(*[far(value) if at in away or at in raw else value for at, value in enumerate(args)])


def expert(h2, h2_other, upstream, upstream_other, w_up, w_down):
    count, width = h2.shape
    units = w_up.shape[1]
    tile = min(512, units)
    shapes = [
        ((2 * count, units), BF16),
        ((2 * count, units), BF16),
        ((count, width), F32),
        ((count, width), BF16),
        ((2 * count, width), BF16),
        ((2 * count, width), BF16),
    ]
    stay = (2, 3)
    both = pl.BlockSpec((2 * count, width), lambda j: (0, 0))
    rows = pl.BlockSpec((count, width), lambda j: (0, 0))
    by_unit = pl.BlockSpec((2 * count, tile), lambda j: (0, j))
    return pl.pallas_call(
        expert_kernel,
        name="expert",
        grid=(units // tile,),
        out_shape=[
            jax.ShapeDtypeStruct(shape, kind) if at in stay else pltpu.HBM(shape, kind)
            for at, (shape, kind) in enumerate(shapes)
        ],
        in_specs=[rows] * 4
        + [
            pl.BlockSpec((width, tile), lambda j: (0, j)),
            pl.BlockSpec((tile, width), lambda j: (j, 0)),
        ],
        out_specs=[by_unit, by_unit, rows, rows, both, both],
        scratch_shapes=[
            pltpu.VMEM((2 * count, width), F32),
        ],
        cost_estimate=pl.CostEstimate(
            flops=12 * count * width * units, bytes_accessed=16 * MIB, transcendentals=0
        ),
        compiler_params=pltpu.CompilerParams(vmem_limit_bytes=40 * MIB),
    )(h2, h2_other, upstream, upstream_other, far(w_up), far(w_down))


def expert_grads(rows, grads, hidden, dpre):
    count, width = rows.shape
    units = hidden.shape[1]
    tile = min(512, units)
    whole = pl.BlockSpec((count, width), lambda j: (0, 0))
    by_unit = pl.BlockSpec((count, tile), lambda j: (0, j))
    return pl.pallas_call(
        expert_grad_kernel,
        name="expert_grads",
        grid=(units // tile,),
        out_shape=[pltpu.HBM((width, units), F32), pltpu.HBM((units, width), F32)],
        in_specs=[whole] * 2 + [by_unit] * 2,
        out_specs=[
            pl.BlockSpec((width, tile), lambda j: (0, j)),
            pl.BlockSpec((tile, width), lambda j: (j, 0)),
        ],
        scratch_shapes=[pltpu.VMEM((width, count), BF16)],
        cost_estimate=pl.CostEstimate(
            flops=4 * count * width * units, bytes_accessed=24 * MIB, transcendentals=0
        ),
        compiler_params=pltpu.CompilerParams(vmem_limit_bytes=40 * MIB),
    )(far(rows), far(grads), far(hidden), far(dpre))


def expert_branch(hidden, w_down):
    count, units = hidden.shape
    width = w_down.shape[1]
    tile = min(512, units)
    half = pl.BlockSpec((count // 2, width), lambda j: (0, 0))
    return pl.pallas_call(
        branch_kernel,
        name="expert_branch",
        grid=(units // tile,),
        out_shape=[pltpu.HBM((count // 2, width), BF16)] * 2,
        in_specs=[
            pl.BlockSpec((count, tile), lambda j: (0, j)),
            pl.BlockSpec((tile, width), lambda j: (j, 0)),
        ],
        out_specs=[half, half],
        scratch_shapes=[pltpu.VMEM((count, width), F32)],
        cost_estimate=pl.CostEstimate(
            flops=2 * count * width * units, bytes_accessed=8 * MIB, transcendentals=0
        ),
        compiler_params=pltpu.CompilerParams(vmem_limit_bytes=20 * MIB),
    )(far(hidden), far(w_down))


def flip(value, axis, bit):
    size = lax.axis_size(axis)
    return lax.ppermute(value, axis, [(i, i ^ bit) for i in range(size)])


def to_others(values, digit):
    return [
        flip(values[m] if isinstance(values, (list, tuple)) else values, "exp", m << (2 * digit))
        for m in range(1, 4)
    ]


def after_all(values, *others):
    return list(lax.optimization_barrier((*values, *others))[: len(values)])


def sum_and_spread(first, second, where, digits, sums, extra, finish_near, finish_far, first_wait, filler):
    bits = 2 * (digits - 1)

    def across(value, bit):
        return flip(value, "exp", 4 << bit)

    def add(halves, came, bit, sums=None):
        owners, rows, columns = came.shape
        if bit + 1 < bits:
            return call(
                functools.partial(add_kernel, bit=bit + 1), "add",
                [((owners // 2, rows, columns), BF16)] * 2, [where, halves[0], came], 0, scalars=1,
                away=(1,), out_away=(0,),
            )
        if sums is None:
            return call(
                last_add_kernel, "last_add", [((rows, columns), BF16)], [halves[0], came], 0,
                away=(0,),
            )
        return call(
            last_add_sums_kernel, "last_add_sums", [((rows + extra, columns), BF16)],
            [halves[0], came, *sums], 0, away=(0,),
        )

    def stack(own, came, sums):
        rows, columns = own.shape
        return call(
            functools.partial(stack_kernel, sums=sums), "stack",
            [((2 * rows - sums, columns), BF16)], [own, came], 0,
        )[0]

    def steps(halves, sums, extra):
        for bit in range(bits):
            came = yield halves[1], [across(halves[1], bit)]
            halves = add(halves, came[0], bit, sums)
        total = halves[0]
        for bit in reversed(range(bits)):
            came = yield total, [across(total, bit)]
            total = stack(total, came[0], extra)
        by_x, by_y = yield total, [flip(total, "exp", 1), flip(total, "exp", 2)]
        if extra == 0:
            near.extend(finish_near(total, by_x, by_y))
        middle = total.shape[0] // 2
        sent = [by_y[:middle], by_x[middle:]]
        halves = yield sent[0], [flip(sent[0], "exp", 1), flip(sent[1], "exp", 2)]
        yield None, [total, by_x, by_y, *halves]

    near = []
    lines, states, last, finished = [steps(first, None, 0), None], [None, None], first_wait, None
    states[0] = next(lines[0])
    for at, line in enumerate([0] + [0, 1] * (2 * bits + 1) + [1]):
        if at == 1:
            pieces = second(last)
            lines[1], last = steps(pieces, sums, extra), pieces[1]
            states[1] = next(lines[1])
        ahead = [*near[1:], filler] if line == 0 and near else []
        states[line] = lines[line].send(after_all(states[line][1], last, *ahead))
        last = states[line][0]
        if line == 0 and last is None:
            finished = finish_far(*states[0][1][3:], *near)
            last = states[0][1][3]
        elif finished is not None:
            last = finished[1]
    return finished, states[1][1]


def on_device(
    block_input,
    dispatch,
    lengths,
    ln1_gain,
    ln1_bias,
    ln2_gain,
    ln2_bias,
    w_qkv,
    w_out,
    w_up,
    w_down,
    grad_output,
):
    slots, width = block_input.shape
    seq_rows = dispatch.shape[0]
    n_exp = lax.axis_size("exp")
    devices = n_exp * lax.axis_size("head")
    cap = slots // devices
    span = 2 * seq_rows
    columns = w_qkv.shape[2]
    scale = 1.0 / math.sqrt(HEAD_DIM)
    digits = (n_exp.bit_length() - 1) // 2
    place = lax.axis_index("exp")
    where = jnp.stack(
        [lax.axis_index("head"), place & 3, place >> 2]
    ).astype(jnp.int32)
    step = 128
    reach = 3 * seq_rows // 4
    packed = ((devices * 8, cap * 128), BF16)
    moving = 2 * devices * 8 * max(slots, seq_rows) * width * 3
    gain1, bias1 = ln1_gain.reshape(1, width), ln1_bias.reshape(1, width)
    gain2, bias2 = ln2_gain.reshape(1, width), ln2_bias.reshape(1, width)
    down, along = dispatch.reshape(seq_rows, 1), dispatch.reshape(1, seq_rows)

    def exchange(value):
        value = value.reshape(devices, 8, cap * 128)
        value = lax.all_to_all(value, ("exp", "head"), split_axis=0, concat_axis=0, tiled=True)
        return value.reshape(devices * 8, cap * 128)

    def cross(value):
        return flip(value, "head", 1)

    (h1,) = call(
        functools.partial(norm1_kernel, cap=cap), "norm1", [packed],
        [block_input, gain1, bias1], moving, away=(0, 1, 2),
    )
    arrived = exchange(h1)
    (own,) = call(
        functools.partial(gather_kernel, cap=cap), "gather1", [((seq_rows, width), BF16)],
        [arrived, down], moving,
    )
    other = cross(own)
    own_copy, inputs, qkv, context, logsum, attn_kept, attn_sent = call(
        functools.partial(attend_kernel, step=step, reach=reach, scale=scale),
        "attend",
        [
            ((seq_rows, width), BF16),
            ((span, width), BF16),
            ((3, span, columns), BF16),
            ((span, columns), BF16),
            ((128, span), F32),
            ((seq_rows, width), F32),
            ((seq_rows, width), BF16),
        ],
        [where, lengths, own, other, w_qkv, w_out],
        2 * span * width * columns * 4 + 16 * span * span * columns,
        scalars=2,
        limit=24,
        raw=(4, 5),
        out_raw=range(5),
        scratch=[
            pltpu.VMEM((3, width, columns), BF16),
            pltpu.VMEM((columns, width), BF16),
            pltpu.VMEM((span, width), BF16),
            pltpu.VMEM((3, span, columns), BF16),
            pltpu.VMEM((span, columns), BF16),
            pltpu.VMEM((128, span), F32),
            pltpu.SemaphoreType.DMA((9,)),
        ],
    )
    (sent,) = call(
        functools.partial(scatter_kernel, cap=cap, fill=True), "scatter1", [packed],
        [attn_kept, cross(attn_sent), along], moving,
    )
    attn_back = exchange(sent)
    by_xy = flip(after(own_copy, attn_back), "exp", 3)
    resid, h2, upstream, valid = call(
        functools.partial(norm2_kernel, cap=cap),
        "norm2",
        [((slots, width), F32), ((slots, width), BF16), ((slots, width), BF16), ((slots, 128), F32)],
        [attn_back, block_input, grad_output, gain2, bias2],
        moving,
    )
    h2_other, upstream_other = cross(h2), cross(upstream)
    hidden, dpre, dh2_kept, dh2_sent, rows_all, grads_all = expert(
        h2, h2_other, upstream, upstream_other, w_up[0], w_down[0]
    )
    dh2_sent = after(dh2_sent, by_xy)
    dresid, sent, sums2 = call(
        functools.partial(norm2_back_kernel, cap=cap),
        "norm2_back",
        [((slots, width), F32), packed, ((width // 64, 128), F32)],
        [dh2_kept, cross(dh2_sent), resid, grad_output, gain2],
        moving,
        out_raw=(0,),
        scratch=[pltpu.VMEM((slots, width), F32), pltpu.SemaphoreType.DMA],
    )
    arrived = exchange(sent)
    near_own, hidden, far_own = after_all([own_copy, hidden, by_xy], sent)
    by_x, by_y = flip(near_own, "exp", 1), flip(near_own, "exp", 2)
    far_other = cross(far_own)
    grad_up, grad_down = expert_grads(rows_all, grads_all, hidden, dpre)
    arrived, grad_up, grad_down, by_x, by_y, far_other = lax.optimization_barrier(
        (arrived, grad_up, grad_down, by_x, by_y, far_other)
    )
    plane_own = [by_x, by_y, far_own]
    plane_other = [cross(by_x), cross(by_y), far_other]
    (own,) = call(
        functools.partial(gather_kernel, cap=cap), "gather2", [((seq_rows, width), BF16)],
        [arrived, down], moving,
    )
    other = cross(own)
    piece = 4 * width // n_exp
    dattn, *out_pieces = call(
        out_grad_kernel,
        "out_grad",
        [((span, width), BF16), *[((n_exp // 4, piece, 128), BF16)] * 4],
        [where, own, other, context],
        2 * span * width * columns,
        scalars=1,
        scratch=[
            pltpu.VMEM((span, columns), BF16),
            pltpu.VMEM((columns, width), F32),
            pltpu.VMEM((4, n_exp // 4, piece, 128), BF16),
            pltpu.SemaphoreType.DMA((5,)),
        ],
        raw=(3,),
        out_raw=range(1, 5),
    )
    out_parts = [out_pieces[0], *to_others(out_pieces, 0)]
    du_kept, du_sent, *parts = call(
        functools.partial(attend_back_kernel, step=step, reach=reach, scale=scale),
        "attend_back",
        [
            ((seq_rows, width), F32),
            ((seq_rows, width), BF16),
            *[((span, 128), BF16)] * 4,
            *[((2, span, 128), BF16)] * 4,
        ],
        [where, lengths, dattn, qkv, context, logsum, w_qkv, w_out],
        2 * span * width * columns * 4 + 40 * span * span * columns,
        scalars=2,
        limit=24,
        raw=range(3, 8),
        out_raw=range(2, 10),
        scratch=[
            pltpu.VMEM((span, columns), BF16),
            pltpu.VMEM((16, span), F32),
            pltpu.VMEM((span, columns), F32),
            pltpu.VMEM((3, span, columns), BF16),
            pltpu.VMEM((3, span, columns), BF16),
            pltpu.VMEM((span, columns), BF16),
            pltpu.VMEM((128, span), F32),
            pltpu.VMEM((3, width, columns), BF16),
            pltpu.VMEM((columns, width), BF16),
            pltpu.SemaphoreType.DMA((17,)),
        ],
    )
    du_sent, *parts = after_all([du_sent, *parts], *out_parts[1:], *plane_other)
    value_parts = [parts[0], *to_others(parts[:4], 0)]
    key_query_parts = [parts[4], *to_others(after_all(parts[4:], *value_parts[1:]), 0)]
    (sent,) = call(
        functools.partial(scatter_kernel, cap=cap, fill=False), "scatter2", [packed],
        [du_kept, cross(du_sent), along], moving,
    )
    arrived = exchange(after(sent, *value_parts[1:]))
    input_grad, sums1 = call(
        functools.partial(norm1_back_kernel, cap=cap),
        "norm1_back",
        [((slots, width), F32), ((width // 64, 128), F32)],
        [arrived, block_input, dresid, gain1],
        moving,
        away=(1, 2, 3),
        out_away=(0,),
    )
    tokens = [inputs, *after_all([*plane_own, *plane_other], du_sent)]
    split = [((n_exp // 8, 2 * piece, 128), BF16)] * 2
    product = 8 * span * width * 128
    out_value = call(
        value_grad_kernel, "value_grad", split, [where, *value_parts, *tokens, *out_parts],
        product, scalars=1, scratch=[pltpu.VMEM((width, 128), F32)], away=(1, *range(5, 13)),
        out_away=(0,),
    )
    branch_kept, branch_sent = expert_branch(after(hidden, out_value[1]), w_down[0])
    branch_came = cross(branch_sent)
    branch = branch_kept.astype(F32) + branch_came.astype(F32)
    result = (resid + valid[:, :1] * branch).astype(BF16)

    def key_query(last):
        came = after_all(key_query_parts[1:], last)
        return call(
            key_query_grad_kernel, "key_query_grad", split,
            [where, key_query_parts[0], *came, *tokens], 2 * product, scalars=1,
            scratch=[pltpu.VMEM((width, 128), F32)], away=(1, *range(5, 12)), out_away=(0,),
        )

    sums = [sums1, cross(sums1), sums2, cross(sums2)]
    extra = 4 * sums1.shape[0]
    whole_qkv = pltpu.HBM((3, width, columns), F32)
    whole_out = pltpu.HBM((columns, width), F32)
    in_place = pl.BlockSpec(memory_space=pltpu.HBM)
    finish_near = pl.pallas_call(
        functools.partial(finish_out_value_near_kernel, digits=digits),
        name="finish_out_value_near",
        grid=(1,),
        out_shape=[whole_qkv, whole_out],
        in_specs=[SMEM] + [VMEM] * 3,
        out_specs=[
            pl.BlockSpec((1, width, columns), lambda i: (2, 0, 0)),
            pl.BlockSpec((columns, width), lambda i: (0, 0)),
        ],
        cost_estimate=pl.CostEstimate(flops=0, bytes_accessed=6 * MIB, transcendentals=0),
        compiler_params=pltpu.CompilerParams(vmem_limit_bytes=20 * MIB),
    )
    finish_far = pl.pallas_call(
        functools.partial(finish_out_value_far_kernel, digits=digits),
        name="finish_out_value_far",
        out_shape=[whole_qkv, whole_out],
        in_specs=[SMEM] + [VMEM] * 2 + [in_place] * 2,
        out_specs=[in_place] * 2,
        scratch_shapes=[
            pltpu.VMEM((1, width, 128), F32),
            pltpu.VMEM((128, width), F32),
            pltpu.SemaphoreType.DMA((2,)),
        ],
        input_output_aliases={3: 0, 4: 1},
        cost_estimate=pl.CostEstimate(flops=0, bytes_accessed=2 * MIB, transcendentals=0),
        compiler_params=pltpu.CompilerParams(vmem_limit_bytes=16 * MIB),
    )
    (grad_qkv, grad_out), key_query = sum_and_spread(
        out_value, key_query, where, digits, sums, extra, functools.partial(finish_near, where),
        functools.partial(finish_far, where), branch_sent, result,
    )
    sums_shape = jax.ShapeDtypeStruct((extra // 2, 128), F32)
    grad_qkv, sums = pl.pallas_call(
        functools.partial(finish_near_kernel, digits=digits, sums=extra),
        name="finish_near",
        grid=(1,),
        out_shape=[whole_qkv, sums_shape],
        in_specs=[SMEM] + [VMEM] * 3 + [in_place],
        out_specs=[
            pl.BlockSpec((2, width, columns), lambda i: (0, 0, 0)),
            pl.BlockSpec((extra // 2, 128), lambda i: (0, 0)),
        ],
        input_output_aliases={4: 0},
        cost_estimate=pl.CostEstimate(flops=0, bytes_accessed=6 * MIB, transcendentals=0),
        compiler_params=pltpu.CompilerParams(vmem_limit_bytes=20 * MIB),
    )(where, *key_query[:3], grad_qkv)
    halves = after_all(key_query[3:], sums)
    grad_qkv, sums = pl.pallas_call(
        functools.partial(finish_far_kernel, digits=digits, sums=extra),
        name="finish_far",
        out_shape=[whole_qkv, sums_shape],
        in_specs=[SMEM] + [VMEM] * 3 + [in_place],
        out_specs=[in_place, VMEM],
        scratch_shapes=[pltpu.VMEM((2, width, 128), F32), pltpu.SemaphoreType.DMA],
        input_output_aliases={4: 0},
        cost_estimate=pl.CostEstimate(flops=0, bytes_accessed=2 * MIB, transcendentals=0),
        compiler_params=pltpu.CompilerParams(vmem_limit_bytes=16 * MIB),
    )(where, *halves, sums, grad_qkv)
    sums = sums.reshape(4, width)
    return (
        result,
        input_grad,
        sums[0],
        sums[1],
        sums[2],
        sums[3],
        grad_qkv,
        grad_out,
        grad_up[None],
        grad_down[None],
    )


def solution(mesh):
    placed = (
        P(("exp", "head"), None),
        P(("exp", "head")),
        P("exp", None),
        P(),
        P(),
        P(),
        P(),
        P(None, None, "head"),
        P("head", None),
        P("exp", None, "head"),
        P("exp", "head", None),
        P(("exp", "head"), None),
    )
    return jax.shard_map(
        on_device,
        mesh=mesh,
        in_specs=placed,
        out_specs=(
            P(("exp", "head"), None),
            P(("exp", "head"), None),
            P(),
            P(),
            P(),
            P(),
            P(None, None, "head"),
            P("head", None),
            P("exp", None, "head"),
            P("exp", "head", None),
        ),
        check_vma=False,
    )
```

```python
import functools
import math

import jax
import jax.numpy as jnp
from jax import lax
from jax.experimental import pallas as pl
from jax.experimental.pallas import tpu as pltpu
from jax.sharding import PartitionSpec as P

HEAD_DIM = 64
EPS = 1e-05
BF16 = jnp.bfloat16
F32 = jnp.float32
MIB = 1024 * 1024
EMPTY = 1e30


def dot(left, right):
    return lax.dot_general(left, right, (((1,), (0,)), ((), ())), preferred_element_type=F32)


def dot_nt(left, right):
    return lax.dot_general(left, right, (((1,), (1,)), ((), ())), preferred_element_type=F32)


def dot_tn(left, right):
    return lax.dot_general(left, right, (((0,), (0,)), ((), ())), preferred_element_type=F32)


def normalise(rows):
    mean = jnp.mean(rows, axis=1, keepdims=True)
    centred = rows - mean
    inverse = lax.rsqrt(jnp.mean(centred * centred, axis=1, keepdims=True) + EPS)
    return centred * inverse, inverse


def norm_back(upstream, normed, inverse, gain):
    scaled = upstream * gain
    first = jnp.mean(scaled, axis=1, keepdims=True)
    second = jnp.mean(scaled * normed, axis=1, keepdims=True)
    return inverse * (scaled - first - normed * second)


def pack(out_ref, rows, slot_of, cap, fill):
    total, width = out_ref.shape[0], rows.shape[1]
    place = lax.broadcasted_iota(jnp.int32, (total, slot_of.shape[1]), 0)
    first = (place >> 3) * cap
    sub = lax.broadcasted_iota(jnp.int32, (total, 128), 0) & 7
    piece = width // 8

    def placed(target):
        hit = (slot_of == target).astype(F32)
        moved = dot(hit.astype(BF16), rows)
        if fill:
            moved = moved + (1.0 - jnp.sum(hit, axis=1, keepdims=True)) * EMPTY
        return moved

    whole = cap // 8
    for group in range(whole):
        moved = placed(first + (place & 7) + group * 8)
        out_ref[:, group * width : (group + 1) * width] = moved.astype(BF16)
    for left in range(cap % 8):
        moved = placed(first + whole * 8 + left)
        folded = moved[:, :piece]
        for s in range(1, 8):
            folded = jnp.where(sub == s, moved[:, s * piece : (s + 1) * piece], folded)
        start = whole * width + left * piece
        out_ref[:, start : start + piece] = folded.astype(BF16)


def unpack(packed_ref, slot_of, cap, width):
    total = packed_ref.shape[0]
    place = lax.broadcasted_iota(jnp.int32, (slot_of.shape[0], total), 1)
    first = (place >> 3) * cap
    piece = width // 8
    sub = lax.broadcasted_iota(jnp.int32, (total, piece), 0) & 7
    whole = cap // 8
    rows = None
    for group in range(whole):
        hit = (slot_of == first + (place & 7) + group * 8).astype(BF16)
        part = dot(hit, packed_ref[:, group * width : (group + 1) * width])
        rows = part if rows is None else rows + part
    for left in range(cap % 8):
        start = whole * width + left * piece
        folded = packed_ref[:, start : start + piece].astype(F32)
        spread = jnp.concatenate(
            [jnp.where(sub == s, folded, 0.0).astype(BF16) for s in range(8)], axis=1
        )
        hit = (slot_of == first + whole * 8 + left).astype(BF16)
        part = dot(hit, spread)
        rows = part if rows is None else rows + part
    return rows


def slots_down(count):
    return lax.broadcasted_iota(jnp.int32, (count, 1), 0)


def norm1_kernel(x_ref, gain_ref, bias_ref, out_ref, *, cap):
    normed, _ = normalise(x_ref[...].astype(F32))
    rows = (normed * gain_ref[...] + bias_ref[...]).astype(BF16)
    slot_of = lax.broadcasted_iota(jnp.int32, (1, rows.shape[0]), 1)
    pack(out_ref, rows, slot_of, cap, False)


def gather_kernel(packed_ref, dispatch_ref, out_ref, *, cap):
    count = dispatch_ref.shape[1]
    along = jnp.broadcast_to(dispatch_ref[...].astype(F32), (128, count))
    slot_of = along.T[:, :1].astype(jnp.int32)
    out_ref[...] = unpack(packed_ref, slot_of, cap, out_ref.shape[1]).astype(BF16)


def two_heads(rows):
    lane = lax.broadcasted_iota(jnp.int32, rows.shape, 1)
    clear = jnp.zeros_like(rows)
    return jnp.concatenate(
        [jnp.where(lane < HEAD_DIM, rows, clear), jnp.where(lane < HEAD_DIM, clear, rows)], axis=0
    )


def started(source, target, sem):
    copy = pltpu.make_async_copy(source, target, sem)
    copy.start()
    return copy


def segments(lengths_ref, places):
    seg = jnp.zeros(places.shape, jnp.int32)
    end = 0
    for index in range(lengths_ref.shape[1]):
        end = end + lengths_ref[0, index]
        seg = seg + (places >= end).astype(jnp.int32)
    return seg


def attend_kernel(
    where_ref,
    lengths_ref,
    own_ref,
    other_ref,
    w_qkv_far,
    w_out_far,
    own_far,
    input_far,
    qkv_far,
    context_far,
    logsum_far,
    kept_ref,
    sent_ref,
    w_qkv_ref,
    w_out_ref,
    input_ref,
    qkv_ref,
    context_ref,
    logsum_ref,
    sems,
    *,
    step,
    reach,
    scale,
):
    weights = [
        started(w_qkv_far.at[which], w_qkv_ref.at[which], sems.at[which]) for which in range(3)
    ]
    last_weight = started(w_out_far, w_out_ref, sems.at[3])
    leaving = [started(own_ref, own_far, sems.at[4])]
    half = own_ref.shape[0]
    span = 2 * half
    here = where_ref[0]
    own_start = pl.multiple_of(here * half, half)
    other_start = pl.multiple_of((1 - here) * half, half)
    input_ref[pl.ds(own_start, half), :] = own_ref[...]
    input_ref[pl.ds(other_start, half), :] = other_ref[...]
    leaving.append(started(input_ref, input_far, sems.at[5]))
    for which in range(3):
        weights[which].wait()
        qkv_ref[which] = dot(input_ref[...], w_qkv_ref[which]).astype(BF16)
    leaving.append(started(qkv_ref, qkv_far, sems.at[6]))
    heads = qkv_ref.shape[2] // HEAD_DIM
    for start in range(0, span, step):
        stop = start + step
        low = max(0, start - reach)
        shape = (step, stop - low)
        query_at = lax.broadcasted_iota(jnp.int32, shape, 0) + start
        key_at = lax.broadcasted_iota(jnp.int32, shape, 1) + low
        allowed = (segments(lengths_ref, query_at) == segments(lengths_ref, key_at)) & (
            key_at <= query_at
        )
        allowed = jnp.concatenate([allowed.astype(F32)] * heads, axis=0) > 0.5
        lane = lax.broadcasted_iota(jnp.int32, (step, 2 * HEAD_DIM), 1)
        pairs = [
            slice(at, at + 2 * HEAD_DIM) for at in range(0, heads * HEAD_DIM, 2 * HEAD_DIM)
        ]
        scores = jnp.concatenate(
            [
                dot_nt(two_heads(qkv_ref[0, start:stop, columns]), qkv_ref[1, low:stop, columns])
                for columns in pairs
            ],
            axis=0,
        )
        scores = jnp.where(allowed, scores * scale, -1e30)
        top = jnp.max(scores, axis=1, keepdims=True)
        expo = jnp.exp(scores - top)
        total = jnp.sum(expo, axis=1, keepdims=True)
        probs = (expo * (1.0 / total)).astype(BF16)
        logsum = top + jnp.log(total)
        logsums = jnp.zeros((step, 128), F32)
        logsum_lane = lax.broadcasted_iota(jnp.int32, (step, 128), 1)
        for head in range(heads):
            mine = logsum[head * step : (head + 1) * step]
            logsums = jnp.where(logsum_lane == head, mine, logsums)
        for at, columns in enumerate(pairs):
            both = dot(
                probs[2 * at * step : 2 * (at + 1) * step], qkv_ref[2, low:stop, columns]
            )
            context_ref[start:stop, columns] = jnp.where(
                lane < HEAD_DIM, both[:step], both[step:]
            ).astype(BF16)
        logsum_ref[:, start:stop] = logsums.T
    leaving.append(started(context_ref, context_far, sems.at[7]))
    leaving.append(started(logsum_ref, logsum_far, sems.at[8]))
    last_weight.wait()
    sent_ref[...] = dot(context_ref[pl.ds(other_start, half), :], w_out_ref[...]).astype(BF16)
    kept_ref[...] = dot(context_ref[pl.ds(own_start, half), :], w_out_ref[...])
    for copy in leaving:
        copy.wait()


def scatter_kernel(kept_ref, came_ref, dispatch_ref, out_ref, *, cap, fill):
    rows = (kept_ref[...] + came_ref[...].astype(F32)).astype(BF16)
    pack(out_ref, rows, dispatch_ref[...], cap, fill)


def norm2_kernel(
    packed_ref, x_ref, grad_ref, gain_ref, bias_ref, resid_ref, h2_ref, up_ref, valid_ref, *, cap
):
    count, width = x_ref.shape
    moved = unpack(packed_ref, slots_down(count), cap, width)
    valid = (moved[:, :1] < 0.5 * EMPTY).astype(F32)
    resid = x_ref[...].astype(F32) + jnp.where(moved < 0.5 * EMPTY, moved, 0.0)
    resid_ref[...] = resid
    normed, _ = normalise(resid)
    h2_ref[...] = (normed * gain_ref[...] + bias_ref[...]).astype(BF16)
    up_ref[...] = (grad_ref[...].astype(F32) * valid).astype(BF16)
    valid_ref[...] = jnp.broadcast_to(valid, valid_ref.shape)


def gelu_and_slope(pre):
    root = math.sqrt(2.0 / math.pi)
    square = pre * pre
    bent = jnp.tanh(pre * (root + (root * 0.044715) * square))
    half = 0.5 + 0.5 * bent
    slope = half + (0.5 * pre) * (1.0 - bent * bent) * (root + (3.0 * 0.044715 * root) * square)
    return pre * half, slope


def expert_kernel(
    h2_ref,
    h2_other_ref,
    up_ref,
    up_other_ref,
    w_up_ref,
    w_down_ref,
    hidden_ref,
    dpre_ref,
    dh2_kept_ref,
    dh2_sent_ref,
    rows_ref,
    grads_ref,
    dh2_ref,
):
    count = h2_ref.shape[0]

    @pl.when(pl.program_id(0) == 0)
    def _():
        rows_ref[:count] = h2_ref[...]
        rows_ref[count:] = h2_other_ref[...]
        grads_ref[:count] = up_ref[...]
        grads_ref[count:] = up_other_ref[...]
        dh2_ref[...] = jnp.zeros_like(dh2_ref)

    w_up, w_down = w_up_ref[...], w_down_ref[...]
    pre = dot(rows_ref[...], w_up)
    gelu, slope = gelu_and_slope(pre)
    hidden = gelu.astype(BF16)
    hidden_ref[...] = hidden
    dpre = (dot_nt(grads_ref[...], w_down) * slope).astype(BF16)
    dpre_ref[...] = dpre
    dh2_ref[...] += dot_nt(dpre, w_up)

    @pl.when(pl.program_id(0) == pl.num_programs(0) - 1)
    def _():
        dh2_kept_ref[...] = dh2_ref[:count]
        dh2_sent_ref[...] = dh2_ref[count:].astype(BF16)


def store_sums(sums_ref, upstream, normed):
    for which, total in enumerate((upstream * normed, upstream)):
        total = jnp.sum(total, axis=0, keepdims=True)
        pieces = total.shape[1] // 128
        for at in range(pieces):
            row = which * pieces + at
            sums_ref[row : row + 1] = total[:, at * 128 : (at + 1) * 128]


def norm2_back_kernel(
    kept_ref,
    came_ref,
    resid_ref,
    grad_ref,
    gain_ref,
    dresid_far,
    packed_ref,
    sums_ref,
    dresid_ref,
    sem,
    *,
    cap,
):
    dh2 = kept_ref[...] + came_ref[...].astype(F32)
    normed, inverse = normalise(resid_ref[...])
    dresid = grad_ref[...].astype(F32) + norm_back(dh2, normed, inverse, gain_ref[...])
    dresid_ref[...] = dresid
    leaving = started(dresid_ref, dresid_far, sem)
    slot_of = lax.broadcasted_iota(jnp.int32, (1, dh2.shape[0]), 1)
    pack(packed_ref, dresid.astype(BF16), slot_of, cap, False)
    store_sums(sums_ref, dh2, normed)
    leaving.wait()


def out_grad_kernel(where_ref, own_ref, other_ref, context_far, dattn_ref, *rest):
    piece_fars, (context_ref, grad_ref, piece_ref, sems) = rest[:4], rest[4:]
    arriving = started(context_far, context_ref, sems.at[4])
    half = own_ref.shape[0]
    here = where_ref[0]
    dattn_ref[pl.ds(pl.multiple_of(here * half, half), half), :] = own_ref[...]
    dattn_ref[pl.ds(pl.multiple_of((1 - here) * half, half), half), :] = other_ref[...]
    arriving.wait()
    grad_ref[...] = dot_tn(context_ref[...], dattn_ref[...])
    width = grad_ref.shape[1]
    quarter = grad_ref.shape[0] // 4
    owners = piece_ref.shape[1]
    rows = quarter // owners
    leaving = []
    for step in (1, 2, 3, 0):
        first = (where_ref[1] ^ step) * quarter
        for owner in range(owners):
            start = pl.multiple_of(first + owner * rows, rows)
            block = grad_ref[pl.ds(start, rows), :]
            piece_ref[step, owner] = jnp.concatenate(
                [block[:, at : at + 128] for at in range(0, width, 128)], axis=0
            ).astype(BF16)
        leaving.append(started(piece_ref.at[step], piece_fars[step], sems.at[step]))
    for copy in leaving:
        copy.wait()


def attend_back_kernel(
    where_ref,
    lengths_ref,
    dattn_ref,
    qkv_far,
    context_far,
    logsum_far,
    w_qkv_far,
    w_out_far,
    kept_ref,
    sent_ref,
    *rest,
    step,
    reach,
    scale,
):
    dvalue_fars, dkq_fars = rest[:4], rest[4:8]
    dcontext_ref, inner_ref, dquery_ref, dqkv_ref = rest[8:12]
    qkv_ref, context_ref, logsum_ref, w_qkv_ref, w_out_ref, sems = rest[12:]
    arriving = [
        started(source, target, sems.at[at])
        for at, (source, target) in enumerate(
            (
                (w_out_far, w_out_ref),
                (context_far, context_ref),
                (qkv_far, qkv_ref),
                (logsum_far, logsum_ref),
                (w_qkv_far, w_qkv_ref),
            )
        )
    ]
    half = kept_ref.shape[0]
    span = 2 * half
    here = where_ref[0]
    own_start = pl.multiple_of(here * half, half)
    other_start = pl.multiple_of((1 - here) * half, half)
    arriving[0].wait()
    dcontext = dot_nt(dattn_ref[...], w_out_ref[...]).astype(BF16)
    dcontext_ref[...] = dcontext
    arriving[1].wait()
    arriving[2].wait()
    arriving[3].wait()
    heads = qkv_ref.shape[2] // HEAD_DIM
    columns_all = qkv_ref.shape[2]
    product = dcontext.astype(F32) * context_ref[...].astype(F32)
    coarse = product.astype(BF16)
    fine = (product - coarse.astype(F32)).astype(BF16)
    of_head = (
        lax.broadcasted_iota(jnp.int32, (16, columns_all), 1) // HEAD_DIM
        == lax.broadcasted_iota(jnp.int32, (16, columns_all), 0)
    ).astype(BF16)
    inner_ref[...] = dot_nt(of_head, coarse) + dot_nt(of_head, fine)
    dquery_ref[...] = jnp.zeros_like(dquery_ref)
    for start in range(0, span, step):
        stop = start + step
        high = min(span, stop + reach)
        shape = (step, high - start)
        key_at = lax.broadcasted_iota(jnp.int32, shape, 0) + start
        query_at = lax.broadcasted_iota(jnp.int32, shape, 1) + start
        allowed = (segments(lengths_ref, query_at) == segments(lengths_ref, key_at)) & (
            key_at <= query_at
        )
        allowed = jnp.concatenate([allowed.astype(F32)] * heads, axis=0) > 0.5
        lane = lax.broadcasted_iota(jnp.int32, (step, 2 * HEAD_DIM), 1)
        pairs = [
            slice(at, at + 2 * HEAD_DIM) for at in range(0, heads * HEAD_DIM, 2 * HEAD_DIM)
        ]
        keys = [two_heads(qkv_ref[1, start:stop, columns]) for columns in pairs]

        def by_head(ref, start=start, high=high):
            return jnp.concatenate(
                [
                    jnp.broadcast_to(ref[head : head + 1, start:high], (step, high - start))
                    for head in range(heads)
                ],
                axis=0,
            )

        scores = jnp.concatenate(
            [
                dot_nt(keys[at], qkv_ref[0, start:high, columns])
                for at, columns in enumerate(pairs)
            ],
            axis=0,
        )
        probs = jnp.exp(jnp.where(allowed, scores * scale - by_head(logsum_ref), -1e30))
        dprobs = jnp.concatenate(
            [
                dot_nt(two_heads(qkv_ref[2, start:stop, columns]), dcontext_ref[start:high, columns])
                for columns in pairs
            ],
            axis=0,
        )
        dscores = (probs * (dprobs - by_head(inner_ref))).astype(BF16)
        probs = probs.astype(BF16)
        for at, columns in enumerate(pairs):
            mine = slice(2 * at * step, 2 * (at + 1) * step)
            dvalues = dot(probs[mine], dcontext_ref[start:high, columns])
            dkeys = dot(dscores[mine], qkv_ref[0, start:high, columns])
            dquery_ref[start:high, columns] += dot_tn(dscores[mine], keys[at])
            dqkv_ref[1, start:stop, columns] = (
                jnp.where(lane < HEAD_DIM, dkeys[:step], dkeys[step:]) * scale
            ).astype(BF16)
            dqkv_ref[2, start:stop, columns] = jnp.where(
                lane < HEAD_DIM, dvalues[:step], dvalues[step:]
            ).astype(BF16)
    dqkv_ref[0] = (dquery_ref[...] * scale).astype(BF16)

    quarter = columns_all // 4
    leaving = []
    for kind, at in ((2, 1), (2, 2), (2, 3), (1, 1), (0, 1), (1, 2), (0, 2), (1, 3), (0, 3), (2, 0), (1, 0), (0, 0)):
        first = pl.multiple_of((where_ref[1] ^ at) * quarter, quarter)
        target = dvalue_fars[at] if kind == 2 else dkq_fars[at].at[1 - kind]
        leaving.append(
            started(dqkv_ref.at[kind, :, pl.ds(first, quarter)], target, sems.at[5 + kind * 4 + at])
        )
    arriving[4].wait()

    def back_rows(start):
        total = dot_nt(dqkv_ref[0, pl.ds(start, half), :], w_qkv_ref[0])
        total = total + dot_nt(dqkv_ref[1, pl.ds(start, half), :], w_qkv_ref[1])
        return total + dot_nt(dqkv_ref[2, pl.ds(start, half), :], w_qkv_ref[2])

    sent_ref[...] = back_rows(other_start).astype(BF16)
    kept_ref[...] = back_rows(own_start)
    for copy in leaving:
        copy.wait()


def token_grad(where_ref, grad_refs, index, input_ref, own_refs, other_refs):
    half = own_refs[0].shape[0]
    own_start = pl.multiple_of(where_ref[0] * half, half)
    other_start = pl.multiple_of((1 - where_ref[0]) * half, half)

    def rows(ref, start, count):
        return ref[pl.ds(start, count), :] if index is None else ref[index, pl.ds(start, count), :]

    total = dot_tn(rows(grad_refs[0], 0, 2 * half), input_ref[...])
    for grad_ref, own_ref, other_ref in zip(grad_refs[1:], own_refs, other_refs):
        total = total + dot_tn(rows(grad_ref, own_start, half), own_ref[...])
        total = total + dot_tn(rows(grad_ref, other_start, half), other_ref[...])
    return total.T


def store_halves(where_ref, bit, half_refs, load, at):
    rows = at.stop - at.start
    for side, half_ref in enumerate(half_refs):
        mine = ((where_ref[2] >> bit) & 1) ^ side
        for index in range(half_ref.shape[0]):
            half_ref[index, at] = load(2 * index + mine, rows).astype(BF16)


def value_grad_kernel(where_ref, *refs):
    grad_refs, input_ref, own_refs, other_refs = refs[0:4], refs[4], refs[5:8], refs[8:11]
    out_refs, half_refs, total_ref = refs[11:15], refs[15:17], refs[17]
    total_ref[...] = token_grad(where_ref, grad_refs, None, input_ref, own_refs, other_refs)
    rows = half_refs[0].shape[1] // 2
    store_halves(
        where_ref, 0, half_refs,
        lambda owner, rows: sum(ref[owner].astype(F32) for ref in out_refs), slice(0, rows),
    )
    store_halves(
        where_ref, 0, half_refs,
        lambda owner, rows: total_ref[pl.ds(pl.multiple_of(owner * rows, rows), rows), :],
        slice(rows, 2 * rows),
    )


def key_query_grad_kernel(where_ref, *refs):
    grad_refs, input_ref, own_refs, other_refs = refs[0:4], refs[4], refs[5:8], refs[8:11]
    half_refs, total_ref = refs[11:13], refs[13]
    rows = half_refs[0].shape[1] // 2
    for index in range(2):
        total_ref[...] = token_grad(where_ref, grad_refs, index, input_ref, own_refs, other_refs)
        store_halves(
            where_ref, 0, half_refs,
            lambda owner, rows: total_ref[pl.ds(pl.multiple_of(owner * rows, rows), rows), :],
            slice(index * rows, (index + 1) * rows),
        )


def add_kernel(where_ref, kept_ref, came_ref, *half_refs, bit):
    store_halves(
        where_ref, bit, half_refs,
        lambda owner, rows: kept_ref[owner].astype(F32) + came_ref[owner].astype(F32),
        slice(0, kept_ref.shape[1]),
    )


def last_add_kernel(kept_ref, came_ref, out_ref):
    out_ref[...] = (kept_ref[0].astype(F32) + came_ref[0].astype(F32)).astype(BF16)


def split_store(out_ref, start, value):
    rows = value.shape[0]
    coarse = value.astype(BF16)
    out_ref[start : start + rows] = coarse
    out_ref[start + rows : start + 2 * rows] = (value - coarse.astype(F32)).astype(BF16)


def last_add_sums_kernel(kept_ref, came_ref, *refs):
    out_ref = refs[4]
    rows = kept_ref.shape[1]
    out_ref[:rows] = (kept_ref[0].astype(F32) + came_ref[0].astype(F32)).astype(BF16)
    sums = jnp.concatenate([refs[0][...] + refs[1][...], refs[2][...] + refs[3][...]], axis=0)
    split_store(out_ref, rows, sums)


def split_sum(refs, start, stop):
    rows = (stop - start) // 2
    return sum(
        ref[start : start + rows].astype(F32) + ref[start + rows : stop].astype(F32)
        for ref in refs
    )


def stack_kernel(own_ref, came_ref, out_ref, *, sums):
    rows = own_ref.shape[0] - sums
    out_ref[:rows] = own_ref[:rows]
    out_ref[rows : 2 * rows] = came_ref[:rows]
    if sums:
        split_store(out_ref, 2 * rows, split_sum((own_ref, came_ref), rows, rows + sums))


def place_rows(where_ref, digits, at):
    bits = 2 * (digits - 1)
    return where_ref[2] ^ sum(((at >> bit) & 1) << (bits - 1 - bit) for bit in range(bits))


def each_piece(where_ref, refs, digits, rows, use, steps=range(4)):
    owners = 4 ** (digits - 1)
    for step in steps:
        column = where_ref[1] ^ step
        for at in range(owners):
            owner = place_rows(where_ref, digits, at)
            first = at * 2 * rows

            def load(low, high, first=first, step=step):
                if step < 3:
                    return refs[step][first + low : first + high]
                middle = refs[3].shape[0]
                start, stop = first + low, first + high
                if stop <= middle:
                    return refs[3][start:stop]
                if start >= middle:
                    return refs[4][start - middle : stop - middle]
                return jnp.concatenate([refs[3][start:middle], refs[4][: stop - middle]], axis=0)

            use(column, owner, load)


def out_value_pieces(where_ref, refs, digits, steps, value_ref, value_column, out_ref, out_first):
    width = value_ref.shape[1]
    rows = width // 4 ** (digits - 1)
    few = rows * 128 // width

    def use(column, owner, load):
        start = pl.multiple_of(out_first(column) + owner * few, few)
        out_ref[pl.ds(start, few), :] = jnp.concatenate(
            [load(at, at + few).astype(F32) for at in range(0, rows, few)], axis=1
        )
        lanes = pl.ds(pl.multiple_of(value_column(column), 128), 128)
        value_ref[0, pl.ds(pl.multiple_of(owner * rows, rows), rows), lanes] = load(
            rows, 2 * rows
        ).astype(F32)

    each_piece(where_ref, refs, digits, rows, use, steps)


def finish_out_value_near_kernel(where_ref, *refs, digits):
    value_ref, out_ref = refs[3:]

    def place(column):
        return column * 128

    out_value_pieces(where_ref, refs[:3], digits, range(3), value_ref, place, out_ref, place)


def finish_out_value_far_kernel(where_ref, *refs, digits):
    halves, (_, _, value_far, out_far, value_ref, out_ref, sems) = refs[:2], refs[2:]
    out_value_pieces(
        where_ref, (None, None, None, *halves), digits, range(3, 4),
        value_ref, lambda column: 0, out_ref, lambda column: 0,
    )
    first = pl.ds(pl.multiple_of((where_ref[1] ^ 3) * 128, 128), 128)
    leaving = [
        started(value_ref, value_far.at[pl.ds(2, 1), :, first], sems.at[0]),
        started(out_ref, out_far.at[first], sems.at[1]),
    ]
    for copy in leaving:
        copy.wait()


def finish_near_kernel(where_ref, *refs, digits, sums):
    qkv_ref, sums_ref = refs[4:]
    width = qkv_ref.shape[1]
    rows = width // 4 ** (digits - 1)

    def use(column, owner, load):
        lanes = pl.ds(pl.multiple_of(column * 128, 128), 128)
        down = pl.ds(pl.multiple_of(owner * rows, rows), rows)
        qkv_ref[1, down, lanes] = load(0, rows).astype(F32)
        qkv_ref[0, down, lanes] = load(rows, 2 * rows).astype(F32)

    each_piece(where_ref, refs[:3], digits, rows, use, range(3))
    total = refs[0].shape[0]
    sums_ref[...] = split_sum(refs[:3], total - sums, total)


def finish_far_kernel(where_ref, *refs, digits, sums):
    halves, near_sums_ref, _, qkv_far, *sums_refs, total_ref, sem = refs[:2], *refs[2:]
    width = total_ref.shape[1]
    rows = width // 4 ** (digits - 1)

    def use(column, owner, load):
        down = pl.ds(pl.multiple_of(owner * rows, rows), rows)
        total_ref[1, down, :] = load(0, rows).astype(F32)
        total_ref[0, down, :] = load(rows, 2 * rows).astype(F32)

    each_piece(where_ref, (None, None, None, *halves), digits, rows, use, range(3, 4))
    lanes = pl.ds(pl.multiple_of((where_ref[1] ^ 3) * 128, 128), 128)
    leaving = started(total_ref, qkv_far.at[pl.ds(0, 2), :, lanes], sem)
    half = halves[1].shape[0]
    total_sums = near_sums_ref[...] + split_sum(halves[1:], half - sums, half)
    count = total_sums.shape[0] // len(sums_refs)
    for at, sums_ref in enumerate(sums_refs):
        sums_ref[...] = total_sums[at * count : (at + 1) * count]
    leaving.wait()


def expert_grad_kernel(rows_ref, grads_ref, hidden_ref, dpre_ref, up_ref, down_ref, turned_ref):
    @pl.when(pl.program_id(0) == 0)
    def _():
        turned_ref[...] = rows_ref[...].T

    up_ref[...] = dot(turned_ref[...], dpre_ref[...])
    down_ref[...] = dot_tn(hidden_ref[...], grads_ref[...])


def branch_kernel(hidden_ref, w_down_ref, kept_ref, sent_ref, branch_ref):
    @pl.when(pl.program_id(0) == 0)
    def _():
        branch_ref[...] = jnp.zeros_like(branch_ref)

    branch_ref[...] += dot(hidden_ref[...], w_down_ref[...])

    @pl.when(pl.program_id(0) == pl.num_programs(0) - 1)
    def _():
        count = kept_ref.shape[0]
        kept_ref[...] = branch_ref[:count].astype(BF16)
        sent_ref[...] = branch_ref[count:].astype(BF16)


def norm1_back_kernel(packed_ref, x_ref, dresid_ref, gain_ref, out_ref, sums_ref, *, cap):
    count, width = x_ref.shape
    dh1 = unpack(packed_ref, slots_down(count), cap, width)
    normed, inverse = normalise(x_ref[...].astype(F32))
    out_ref[...] = dresid_ref[...] + norm_back(dh1, normed, inverse, gain_ref[...])
    store_sums(sums_ref, dh1, normed)


VMEM = pl.BlockSpec(memory_space=pltpu.VMEM)
SMEM = pl.BlockSpec(memory_space=pltpu.SMEM)


def after(value, *others):
    return lax.optimization_barrier((value, *others))[0]


def far(value):
    return pltpu.with_memory_space_constraint(value, pltpu.HBM)


def call(kernel, name, outs, args, flops, scalars=0, scratch=(), limit=16, away=(), out_away=(), raw=(), out_raw=()):
    shapes = [
        pltpu.HBM(shape, kind)
        if at in out_away or at in out_raw
        else jax.ShapeDtypeStruct(shape, kind)
        for at, (shape, kind) in enumerate(outs)
    ]

    def spec(at, away, raw):
        if at in raw:
            return pl.BlockSpec(memory_space=pltpu.HBM)
        return pl.BlockSpec() if at in away else VMEM

    size = sum(math.prod(a.shape) * a.dtype.itemsize for a in (*args, *shapes))
    return pl.pallas_call(
        kernel,
        name=name,
        out_shape=shapes,
        in_specs=[
            SMEM if at < scalars else spec(at, away, raw) for at in range(len(args))
        ],
        out_specs=[spec(at, out_away, out_raw) for at in range(len(outs))],
        scratch_shapes=list(scratch),
        cost_estimate=pl.CostEstimate(flops=flops, bytes_accessed=size, transcendentals=0),
        compiler_params=pltpu.CompilerParams(vmem_limit_bytes=limit * MIB),
    )(*[far(value) if at in away or at in raw else value for at, value in enumerate(args)])


def expert(h2, h2_other, upstream, upstream_other, w_up, w_down):
    count, width = h2.shape
    units = w_up.shape[1]
    tile = min(512, units)
    shapes = [
        ((2 * count, units), BF16),
        ((2 * count, units), BF16),
        ((count, width), F32),
        ((count, width), BF16),
        ((2 * count, width), BF16),
        ((2 * count, width), BF16),
    ]
    stay = (2, 3)
    both = pl.BlockSpec((2 * count, width), lambda j: (0, 0))
    rows = pl.BlockSpec((count, width), lambda j: (0, 0))
    by_unit = pl.BlockSpec((2 * count, tile), lambda j: (0, j))
    return pl.pallas_call(
        expert_kernel,
        name="expert",
        grid=(units // tile,),
        out_shape=[
            jax.ShapeDtypeStruct(shape, kind) if at in stay else pltpu.HBM(shape, kind)
            for at, (shape, kind) in enumerate(shapes)
        ],
        in_specs=[rows] * 4
        + [
            pl.BlockSpec((width, tile), lambda j: (0, j)),
            pl.BlockSpec((tile, width), lambda j: (j, 0)),
        ],
        out_specs=[by_unit, by_unit, rows, rows, both, both],
        scratch_shapes=[
            pltpu.VMEM((2 * count, width), F32),
        ],
        cost_estimate=pl.CostEstimate(
            flops=12 * count * width * units, bytes_accessed=16 * MIB, transcendentals=0
        ),
        compiler_params=pltpu.CompilerParams(vmem_limit_bytes=40 * MIB),
    )(h2, h2_other, upstream, upstream_other, w_up, w_down)


def expert_grads(rows, grads, hidden, dpre):
    count, width = rows.shape
    units = hidden.shape[1]
    tile = min(512, units)
    whole = pl.BlockSpec((count, width), lambda j: (0, 0))
    by_unit = pl.BlockSpec((count, tile), lambda j: (0, j))
    return pl.pallas_call(
        expert_grad_kernel,
        name="expert_grads",
        grid=(units // tile,),
        out_shape=[pltpu.HBM((width, units), F32), pltpu.HBM((units, width), F32)],
        in_specs=[whole] * 2 + [by_unit] * 2,
        out_specs=[
            pl.BlockSpec((width, tile), lambda j: (0, j)),
            pl.BlockSpec((tile, width), lambda j: (j, 0)),
        ],
        scratch_shapes=[pltpu.VMEM((width, count), BF16)],
        cost_estimate=pl.CostEstimate(
            flops=4 * count * width * units, bytes_accessed=24 * MIB, transcendentals=0
        ),
        compiler_params=pltpu.CompilerParams(vmem_limit_bytes=40 * MIB),
    )(far(rows), far(grads), far(hidden), far(dpre))


def expert_branch(hidden, w_down):
    count, units = hidden.shape
    width = w_down.shape[1]
    tile = min(512, units)
    half = pl.BlockSpec((count // 2, width), lambda j: (0, 0))
    return pl.pallas_call(
        branch_kernel,
        name="expert_branch",
        grid=(units // tile,),
        out_shape=[pltpu.HBM((count // 2, width), BF16)] * 2,
        in_specs=[
            pl.BlockSpec((count, tile), lambda j: (0, j)),
            pl.BlockSpec((tile, width), lambda j: (j, 0)),
        ],
        out_specs=[half, half],
        scratch_shapes=[pltpu.VMEM((count, width), F32)],
        cost_estimate=pl.CostEstimate(
            flops=2 * count * width * units, bytes_accessed=8 * MIB, transcendentals=0
        ),
        compiler_params=pltpu.CompilerParams(vmem_limit_bytes=20 * MIB),
    )(far(hidden), far(w_down))


def flip(value, axis, bit):
    size = lax.axis_size(axis)
    return lax.ppermute(value, axis, [(i, i ^ bit) for i in range(size)])


def to_others(values, digit):
    return [
        flip(values[m] if isinstance(values, (list, tuple)) else values, "exp", m << (2 * digit))
        for m in range(1, 4)
    ]


def after_all(values, *others):
    return list(lax.optimization_barrier((*values, *others))[: len(values)])


def sum_and_spread(first, second, where, digits, sums, extra, finish_near, finish_far, first_wait, filler):
    bits = 2 * (digits - 1)

    def across(value, bit):
        return flip(value, "exp", 4 << bit)

    def add(halves, came, bit, sums=None):
        owners, rows, columns = came.shape
        if bit + 1 < bits:
            return call(
                functools.partial(add_kernel, bit=bit + 1), "add",
                [((owners // 2, rows, columns), BF16)] * 2, [where, halves[0], came], 0, scalars=1,
                away=(1,), out_away=(0,),
            )
        if sums is None:
            return call(
                last_add_kernel, "last_add", [((rows, columns), BF16)], [halves[0], came], 0,
                away=(0,),
            )
        return call(
            last_add_sums_kernel, "last_add_sums", [((rows + extra, columns), BF16)],
            [halves[0], came, *sums], 0, away=(0,),
        )

    def stack(own, came, sums):
        rows, columns = own.shape
        return call(
            functools.partial(stack_kernel, sums=sums), "stack",
            [((2 * rows - sums, columns), BF16)], [own, came], 0,
        )[0]

    def steps(halves, sums, extra):
        for bit in range(bits):
            came = yield halves[1], [across(halves[1], bit)]
            halves = add(halves, came[0], bit, sums)
        total = halves[0]
        for bit in reversed(range(bits)):
            came = yield total, [across(total, bit)]
            total = stack(total, came[0], extra)
        by_x, by_y = yield total, [flip(total, "exp", 1), flip(total, "exp", 2)]
        if extra == 0:
            near.extend(finish_near(total, by_x, by_y))
        middle = total.shape[0] // 2
        sent = [by_y[:middle], by_x[middle:]]
        halves = yield sent[0], [flip(sent[0], "exp", 1), flip(sent[1], "exp", 2)]
        yield None, [total, by_x, by_y, *halves]

    near = []
    lines, states, last, finished = [steps(first, None, 0), None], [None, None], first_wait, None
    states[0] = next(lines[0])
    for at, line in enumerate([0] + [0, 1] * (2 * bits + 1) + [1]):
        if at == 1:
            pieces = second(last)
            lines[1], last = steps(pieces, sums, extra), pieces[1]
            states[1] = next(lines[1])
        ahead = [*near[1:], filler] if line == 0 and near else []
        states[line] = lines[line].send(after_all(states[line][1], last, *ahead))
        last = states[line][0]
        if line == 0 and last is None:
            finished = finish_far(*states[0][1][3:], *near)
            last = states[0][1][3]
        elif finished is not None:
            last = finished[1]
    return finished, states[1][1]


def on_device(
    block_input,
    dispatch,
    lengths,
    ln1_gain,
    ln1_bias,
    ln2_gain,
    ln2_bias,
    w_qkv,
    w_out,
    w_up,
    w_down,
    grad_output,
):
    slots, width = block_input.shape
    seq_rows = dispatch.shape[0]
    n_exp = lax.axis_size("exp")
    devices = n_exp * lax.axis_size("head")
    cap = slots // devices
    span = 2 * seq_rows
    columns = w_qkv.shape[2]
    scale = 1.0 / math.sqrt(HEAD_DIM)
    digits = (n_exp.bit_length() - 1) // 2
    place = lax.axis_index("exp")
    where = jnp.stack(
        [lax.axis_index("head"), place & 3, place >> 2]
    ).astype(jnp.int32)
    step = 128
    reach = 3 * seq_rows // 4
    packed = ((devices * 8, cap * 128), BF16)
    moving = 2 * devices * 8 * max(slots, seq_rows) * width * 3
    gain1, bias1 = ln1_gain.reshape(1, width), ln1_bias.reshape(1, width)
    gain2, bias2 = ln2_gain.reshape(1, width), ln2_bias.reshape(1, width)
    along = dispatch.reshape(1, seq_rows)

    def exchange(value):
        value = value.reshape(devices, 8, cap * 128)
        value = lax.all_to_all(value, ("exp", "head"), split_axis=0, concat_axis=0, tiled=True)
        return value.reshape(devices * 8, cap * 128)

    def cross(value):
        return flip(value, "head", 1)

    (h1,) = call(
        functools.partial(norm1_kernel, cap=cap), "norm1", [packed],
        [block_input, gain1, bias1], moving, away=(0, 1, 2),
    )
    arrived = exchange(h1)
    (own,) = call(
        functools.partial(gather_kernel, cap=cap), "gather1", [((seq_rows, width), BF16)],
        [arrived, along], moving,
    )
    other = cross(own)
    own_copy, inputs, qkv, context, logsum, attn_kept, attn_sent = call(
        functools.partial(attend_kernel, step=step, reach=reach, scale=scale),
        "attend",
        [
            ((seq_rows, width), BF16),
            ((span, width), BF16),
            ((3, span, columns), BF16),
            ((span, columns), BF16),
            ((128, span), F32),
            ((seq_rows, width), F32),
            ((seq_rows, width), BF16),
        ],
        [where, lengths, own, other, w_qkv, w_out],
        2 * span * width * columns * 4 + 16 * span * span * columns,
        scalars=2,
        limit=24,
        raw=(4, 5),
        out_raw=range(5),
        scratch=[
            pltpu.VMEM((3, width, columns), BF16),
            pltpu.VMEM((columns, width), BF16),
            pltpu.VMEM((span, width), BF16),
            pltpu.VMEM((3, span, columns), BF16),
            pltpu.VMEM((span, columns), BF16),
            pltpu.VMEM((128, span), F32),
            pltpu.SemaphoreType.DMA((9,)),
        ],
    )
    (sent,) = call(
        functools.partial(scatter_kernel, cap=cap, fill=True), "scatter1", [packed],
        [attn_kept, cross(attn_sent), along], moving,
    )
    attn_back = exchange(sent)
    by_xy = flip(after(own_copy, attn_back), "exp", 3)
    resid, h2, upstream, valid = call(
        functools.partial(norm2_kernel, cap=cap),
        "norm2",
        [((slots, width), F32), ((slots, width), BF16), ((slots, width), BF16), ((slots, 128), F32)],
        [attn_back, block_input, grad_output, gain2, bias2],
        moving,
    )
    h2_other, upstream_other = cross(h2), cross(upstream)
    hidden, dpre, dh2_kept, dh2_sent, rows_all, grads_all = expert(
        h2, h2_other, upstream, upstream_other, w_up[0], w_down[0]
    )
    dh2_sent = after(dh2_sent, by_xy)
    dresid, sent, sums2 = call(
        functools.partial(norm2_back_kernel, cap=cap),
        "norm2_back",
        [((slots, width), F32), packed, ((width // 64, 128), F32)],
        [dh2_kept, cross(dh2_sent), resid, grad_output, gain2],
        moving,
        out_raw=(0,),
        scratch=[pltpu.VMEM((slots, width), F32), pltpu.SemaphoreType.DMA],
    )
    arrived = exchange(sent)
    near_own, hidden, far_own = after_all([own_copy, hidden, by_xy], sent)
    by_x, by_y = flip(near_own, "exp", 1), flip(near_own, "exp", 2)
    far_other = cross(far_own)
    grad_up, grad_down = expert_grads(rows_all, grads_all, hidden, dpre)
    arrived, grad_up, grad_down, by_x, by_y, far_other = lax.optimization_barrier(
        (arrived, grad_up, grad_down, by_x, by_y, far_other)
    )
    plane_own = [by_x, by_y, far_own]
    plane_other = [cross(by_x), cross(by_y), far_other]
    (own,) = call(
        functools.partial(gather_kernel, cap=cap), "gather2", [((seq_rows, width), BF16)],
        [arrived, along], moving,
    )
    other = cross(own)
    piece = 4 * width // n_exp
    dattn, *out_pieces = call(
        out_grad_kernel,
        "out_grad",
        [((span, width), BF16), *[((n_exp // 4, piece, 128), BF16)] * 4],
        [where, own, other, context],
        2 * span * width * columns,
        scalars=1,
        scratch=[
            pltpu.VMEM((span, columns), BF16),
            pltpu.VMEM((columns, width), F32),
            pltpu.VMEM((4, n_exp // 4, piece, 128), BF16),
            pltpu.SemaphoreType.DMA((5,)),
        ],
        raw=(3,),
        out_raw=range(1, 5),
    )
    out_parts = [out_pieces[0], *to_others(out_pieces, 0)]
    du_kept, du_sent, *parts = call(
        functools.partial(attend_back_kernel, step=step, reach=reach, scale=scale),
        "attend_back",
        [
            ((seq_rows, width), F32),
            ((seq_rows, width), BF16),
            *[((span, 128), BF16)] * 4,
            *[((2, span, 128), BF16)] * 4,
        ],
        [where, lengths, dattn, qkv, context, logsum, w_qkv, w_out],
        2 * span * width * columns * 4 + 40 * span * span * columns,
        scalars=2,
        limit=24,
        raw=range(3, 8),
        out_raw=range(2, 10),
        scratch=[
            pltpu.VMEM((span, columns), BF16),
            pltpu.VMEM((16, span), F32),
            pltpu.VMEM((span, columns), F32),
            pltpu.VMEM((3, span, columns), BF16),
            pltpu.VMEM((3, span, columns), BF16),
            pltpu.VMEM((span, columns), BF16),
            pltpu.VMEM((128, span), F32),
            pltpu.VMEM((3, width, columns), BF16),
            pltpu.VMEM((columns, width), BF16),
            pltpu.SemaphoreType.DMA((17,)),
        ],
    )
    du_sent, *parts = after_all([du_sent, *parts], *out_parts[1:], *plane_other)
    value_parts = [parts[0], *to_others(parts[:4], 0)]
    key_query_parts = [parts[4], *to_others(after_all(parts[4:], *value_parts[1:]), 0)]
    (sent,) = call(
        functools.partial(scatter_kernel, cap=cap, fill=False), "scatter2", [packed],
        [du_kept, cross(du_sent), along], moving,
    )
    arrived = exchange(after(sent, *value_parts[1:]))
    input_grad, sums1 = call(
        functools.partial(norm1_back_kernel, cap=cap),
        "norm1_back",
        [((slots, width), F32), ((width // 64, 128), F32)],
        [arrived, block_input, dresid, gain1],
        moving,
        away=(1, 2, 3),
        out_away=(0,),
    )
    tokens = [inputs, *after_all([*plane_own, *plane_other], du_sent)]
    split = [((n_exp // 8, 2 * piece, 128), BF16)] * 2
    product = 8 * span * width * 128
    out_value = call(
        value_grad_kernel, "value_grad", split, [where, *value_parts, *tokens, *out_parts],
        product, scalars=1, scratch=[pltpu.VMEM((width, 128), F32)], away=(1, *range(5, 13)),
        out_away=(0,),
    )
    branch_kept, branch_sent = expert_branch(after(hidden, out_value[1]), w_down[0])
    branch_came = cross(branch_sent)
    branch = branch_kept.astype(F32) + branch_came.astype(F32)
    result = (resid + valid[:, :1] * branch).astype(BF16)

    def key_query(last):
        came = after_all(key_query_parts[1:], last)
        return call(
            key_query_grad_kernel, "key_query_grad", split,
            [where, key_query_parts[0], *came, *tokens], 2 * product, scalars=1,
            scratch=[pltpu.VMEM((width, 128), F32)], away=(1, *range(5, 12)), out_away=(0,),
        )

    sums = [sums1, cross(sums1), sums2, cross(sums2)]
    extra = 4 * sums1.shape[0]
    whole_qkv = pltpu.HBM((3, width, columns), F32)
    whole_out = pltpu.HBM((columns, width), F32)
    in_place = pl.BlockSpec(memory_space=pltpu.HBM)
    finish_near = pl.pallas_call(
        functools.partial(finish_out_value_near_kernel, digits=digits),
        name="finish_out_value_near",
        grid=(1,),
        out_shape=[whole_qkv, whole_out],
        in_specs=[SMEM] + [VMEM] * 3,
        out_specs=[
            pl.BlockSpec((1, width, columns), lambda i: (2, 0, 0)),
            pl.BlockSpec((columns, width), lambda i: (0, 0)),
        ],
        cost_estimate=pl.CostEstimate(flops=0, bytes_accessed=6 * MIB, transcendentals=0),
        compiler_params=pltpu.CompilerParams(vmem_limit_bytes=20 * MIB),
    )
    finish_far = pl.pallas_call(
        functools.partial(finish_out_value_far_kernel, digits=digits),
        name="finish_out_value_far",
        out_shape=[whole_qkv, whole_out],
        in_specs=[SMEM] + [VMEM] * 2 + [in_place] * 2,
        out_specs=[in_place] * 2,
        scratch_shapes=[
            pltpu.VMEM((1, width, 128), F32),
            pltpu.VMEM((128, width), F32),
            pltpu.SemaphoreType.DMA((2,)),
        ],
        input_output_aliases={3: 0, 4: 1},
        cost_estimate=pl.CostEstimate(flops=0, bytes_accessed=2 * MIB, transcendentals=0),
        compiler_params=pltpu.CompilerParams(vmem_limit_bytes=16 * MIB),
    )
    (grad_qkv, grad_out), key_query = sum_and_spread(
        out_value, key_query, where, digits, sums, extra, functools.partial(finish_near, where),
        functools.partial(finish_far, where), branch_sent, result,
    )
    sums_shape = jax.ShapeDtypeStruct((extra // 2, 128), F32)
    grad_qkv, sums = pl.pallas_call(
        functools.partial(finish_near_kernel, digits=digits, sums=extra),
        name="finish_near",
        grid=(1,),
        out_shape=[whole_qkv, sums_shape],
        in_specs=[SMEM] + [VMEM] * 3 + [in_place],
        out_specs=[
            pl.BlockSpec((2, width, columns), lambda i: (0, 0, 0)),
            pl.BlockSpec((extra // 2, 128), lambda i: (0, 0)),
        ],
        input_output_aliases={4: 0},
        cost_estimate=pl.CostEstimate(flops=0, bytes_accessed=6 * MIB, transcendentals=0),
        compiler_params=pltpu.CompilerParams(vmem_limit_bytes=20 * MIB),
    )(where, *key_query[:3], grad_qkv)
    halves = after_all(key_query[3:], sums)
    grad_qkv, *sums = pl.pallas_call(
        functools.partial(finish_far_kernel, digits=digits, sums=extra),
        name="finish_far",
        out_shape=[whole_qkv, *[jax.ShapeDtypeStruct((width // 128, 128), F32)] * 4],
        in_specs=[SMEM] + [VMEM] * 3 + [in_place],
        out_specs=[in_place, *[VMEM] * 4],
        scratch_shapes=[pltpu.VMEM((2, width, 128), F32), pltpu.SemaphoreType.DMA],
        input_output_aliases={4: 0},
        cost_estimate=pl.CostEstimate(flops=0, bytes_accessed=2 * MIB, transcendentals=0),
        compiler_params=pltpu.CompilerParams(vmem_limit_bytes=16 * MIB),
    )(where, *halves, sums, grad_qkv)
    sums = [total.reshape(width) for total in sums]
    return (
        result,
        input_grad,
        sums[0],
        sums[1],
        sums[2],
        sums[3],
        grad_qkv,
        grad_out,
        grad_up[None],
        grad_down[None],
    )


def solution(mesh):
    placed = (
        P(("exp", "head"), None),
        P(("exp", "head")),
        P("exp", None),
        P(),
        P(),
        P(),
        P(),
        P(None, None, "head"),
        P("head", None),
        P("exp", None, "head"),
        P("exp", "head", None),
        P(("exp", "head"), None),
    )
    return jax.shard_map(
        on_device,
        mesh=mesh,
        in_specs=placed,
        out_specs=(
            P(("exp", "head"), None),
            P(("exp", "head"), None),
            P(),
            P(),
            P(),
            P(),
            P(None, None, "head"),
            P("head", None),
            P("exp", None, "head"),
            P("exp", "head", None),
        ),
        check_vma=False,
    )
```

```python
import functools
import math

import jax
import jax.numpy as jnp
from jax import lax
from jax.experimental import pallas as pl
from jax.experimental.pallas import tpu as pltpu
from jax.sharding import PartitionSpec as P

HEAD_DIM = 64
EPS = 1e-05
BF16 = jnp.bfloat16
F32 = jnp.float32
MIB = 1024 * 1024
EMPTY = 1e30


def dot(left, right):
    return lax.dot_general(left, right, (((1,), (0,)), ((), ())), preferred_element_type=F32)


def dot_nt(left, right):
    return lax.dot_general(left, right, (((1,), (1,)), ((), ())), preferred_element_type=F32)


def dot_tn(left, right):
    return lax.dot_general(left, right, (((0,), (0,)), ((), ())), preferred_element_type=F32)


def normalise(rows):
    mean = jnp.mean(rows, axis=1, keepdims=True)
    centred = rows - mean
    inverse = lax.rsqrt(jnp.mean(centred * centred, axis=1, keepdims=True) + EPS)
    return centred * inverse, inverse


def norm_back(upstream, normed, inverse, gain):
    scaled = upstream * gain
    first = jnp.mean(scaled, axis=1, keepdims=True)
    second = jnp.mean(scaled * normed, axis=1, keepdims=True)
    return inverse * (scaled - first - normed * second)


def pack(out_ref, rows, slot_of, cap, fill):
    total, width = out_ref.shape[0], rows.shape[1]
    place = lax.broadcasted_iota(jnp.int32, (total, slot_of.shape[1]), 0)
    first = (place >> 3) * cap
    sub = lax.broadcasted_iota(jnp.int32, (total, 128), 0) & 7
    piece = width // 8

    def placed(target):
        hit = (slot_of == target).astype(F32)
        moved = dot(hit.astype(BF16), rows)
        if fill:
            moved = moved + (1.0 - jnp.sum(hit, axis=1, keepdims=True)) * EMPTY
        return moved

    whole = cap // 8
    for group in range(whole):
        moved = placed(first + (place & 7) + group * 8)
        out_ref[:, group * width : (group + 1) * width] = moved.astype(BF16)
    for left in range(cap % 8):
        moved = placed(first + whole * 8 + left)
        folded = moved[:, :piece]
        for s in range(1, 8):
            folded = jnp.where(sub == s, moved[:, s * piece : (s + 1) * piece], folded)
        start = whole * width + left * piece
        out_ref[:, start : start + piece] = folded.astype(BF16)


def unpack(packed_ref, slot_of, cap, width):
    total = packed_ref.shape[0]
    place = lax.broadcasted_iota(jnp.int32, (slot_of.shape[0], total), 1)
    first = (place >> 3) * cap
    piece = width // 8
    sub = lax.broadcasted_iota(jnp.int32, (total, piece), 0) & 7
    whole = cap // 8
    rows = None
    for group in range(whole):
        hit = (slot_of == first + (place & 7) + group * 8).astype(BF16)
        part = dot(hit, packed_ref[:, group * width : (group + 1) * width])
        rows = part if rows is None else rows + part
    for left in range(cap % 8):
        start = whole * width + left * piece
        folded = packed_ref[:, start : start + piece].astype(F32)
        spread = jnp.concatenate(
            [jnp.where(sub == s, folded, 0.0).astype(BF16) for s in range(8)], axis=1
        )
        hit = (slot_of == first + whole * 8 + left).astype(BF16)
        part = dot(hit, spread)
        rows = part if rows is None else rows + part
    return rows


def slots_down(count):
    return lax.broadcasted_iota(jnp.int32, (count, 1), 0)


def norm1_kernel(x_ref, gain_ref, bias_ref, out_ref, *, cap):
    normed, _ = normalise(x_ref[...].astype(F32))
    rows = (normed * gain_ref[...] + bias_ref[...]).astype(BF16)
    slot_of = lax.broadcasted_iota(jnp.int32, (1, rows.shape[0]), 1)
    pack(out_ref, rows, slot_of, cap, False)


def gather_kernel(packed_ref, dispatch_ref, out_ref, *, cap):
    count = dispatch_ref.shape[1]
    along = jnp.broadcast_to(dispatch_ref[...].astype(F32), (128, count))
    slot_of = along.T[:, :1].astype(jnp.int32)
    out_ref[...] = unpack(packed_ref, slot_of, cap, out_ref.shape[1]).astype(BF16)


def two_heads(rows):
    lane = lax.broadcasted_iota(jnp.int32, rows.shape, 1)
    clear = jnp.zeros_like(rows)
    return jnp.concatenate(
        [jnp.where(lane < HEAD_DIM, rows, clear), jnp.where(lane < HEAD_DIM, clear, rows)], axis=0
    )


def started(source, target, sem):
    copy = pltpu.make_async_copy(source, target, sem)
    copy.start()
    return copy


def segments(lengths_ref, places):
    seg = jnp.zeros(places.shape, jnp.int32)
    end = 0
    for index in range(lengths_ref.shape[1]):
        end = end + lengths_ref[0, index]
        seg = seg + (places >= end).astype(jnp.int32)
    return seg


def attend_kernel(
    where_ref,
    lengths_ref,
    own_ref,
    other_ref,
    w_qkv_far,
    w_out_far,
    own_far,
    input_far,
    qkv_far,
    context_far,
    logsum_far,
    kept_ref,
    sent_ref,
    w_qkv_ref,
    w_out_ref,
    input_ref,
    qkv_ref,
    context_ref,
    logsum_ref,
    sems,
    *,
    step,
    reach,
    scale,
):
    weights = [
        started(w_qkv_far.at[which], w_qkv_ref.at[which], sems.at[which]) for which in range(3)
    ]
    last_weight = started(w_out_far, w_out_ref, sems.at[3])
    leaving = [started(own_ref, own_far, sems.at[4])]
    half = own_ref.shape[0]
    span = 2 * half
    here = where_ref[0]
    own_start = pl.multiple_of(here * half, half)
    other_start = pl.multiple_of((1 - here) * half, half)
    input_ref[pl.ds(own_start, half), :] = own_ref[...]
    input_ref[pl.ds(other_start, half), :] = other_ref[...]
    leaving.append(started(input_ref, input_far, sems.at[5]))
    for which in range(3):
        weights[which].wait()
        qkv_ref[which] = dot(input_ref[...], w_qkv_ref[which]).astype(BF16)
    leaving.append(started(qkv_ref, qkv_far, sems.at[6]))
    heads = qkv_ref.shape[2] // HEAD_DIM
    for start in range(0, span, step):
        stop = start + step
        low = max(0, start - reach)
        shape = (step, stop - low)
        query_at = lax.broadcasted_iota(jnp.int32, shape, 0) + start
        key_at = lax.broadcasted_iota(jnp.int32, shape, 1) + low
        allowed = (segments(lengths_ref, query_at) == segments(lengths_ref, key_at)) & (
            key_at <= query_at
        )
        allowed = jnp.concatenate([allowed.astype(F32)] * heads, axis=0) > 0.5
        lane = lax.broadcasted_iota(jnp.int32, (step, 2 * HEAD_DIM), 1)
        pairs = [
            slice(at, at + 2 * HEAD_DIM) for at in range(0, heads * HEAD_DIM, 2 * HEAD_DIM)
        ]
        scores = jnp.concatenate(
            [
                dot_nt(two_heads(qkv_ref[0, start:stop, columns]), qkv_ref[1, low:stop, columns])
                for columns in pairs
            ],
            axis=0,
        )
        scores = jnp.where(allowed, scores * scale, -1e30)
        top = jnp.max(scores, axis=1, keepdims=True)
        expo = jnp.exp(scores - top)
        total = jnp.sum(expo, axis=1, keepdims=True)
        probs = (expo * (1.0 / total)).astype(BF16)
        logsum = top + jnp.log(total)
        logsums = jnp.zeros((step, 128), F32)
        logsum_lane = lax.broadcasted_iota(jnp.int32, (step, 128), 1)
        for head in range(heads):
            mine = logsum[head * step : (head + 1) * step]
            logsums = jnp.where(logsum_lane == head, mine, logsums)
        for at, columns in enumerate(pairs):
            both = dot(
                probs[2 * at * step : 2 * (at + 1) * step], qkv_ref[2, low:stop, columns]
            )
            context_ref[start:stop, columns] = jnp.where(
                lane < HEAD_DIM, both[:step], both[step:]
            ).astype(BF16)
        logsum_ref[:, start:stop] = logsums.T
    leaving.append(started(context_ref, context_far, sems.at[7]))
    leaving.append(started(logsum_ref, logsum_far, sems.at[8]))
    last_weight.wait()
    sent_ref[...] = dot(context_ref[pl.ds(other_start, half), :], w_out_ref[...]).astype(BF16)
    kept_ref[...] = dot(context_ref[pl.ds(own_start, half), :], w_out_ref[...])
    for copy in leaving:
        copy.wait()


def scatter_kernel(kept_ref, came_ref, dispatch_ref, out_ref, *, cap, fill):
    rows = (kept_ref[...] + came_ref[...].astype(F32)).astype(BF16)
    pack(out_ref, rows, dispatch_ref[...], cap, fill)


def norm2_kernel(
    packed_ref, x_ref, grad_ref, gain_ref, bias_ref, resid_ref, h2_ref, up_ref, valid_ref, *, cap
):
    count, width = x_ref.shape
    moved = unpack(packed_ref, slots_down(count), cap, width)
    valid = (moved[:, :1] < 0.5 * EMPTY).astype(F32)
    resid = x_ref[...].astype(F32) + jnp.where(moved < 0.5 * EMPTY, moved, 0.0)
    resid_ref[...] = resid
    normed, _ = normalise(resid)
    h2_ref[...] = (normed * gain_ref[...] + bias_ref[...]).astype(BF16)
    up_ref[...] = (grad_ref[...].astype(F32) * valid).astype(BF16)
    valid_ref[...] = jnp.broadcast_to(valid, valid_ref.shape)


def gelu_and_slope(pre):
    root = math.sqrt(2.0 / math.pi)
    square = pre * pre
    bent = jnp.tanh(pre * (root + (root * 0.044715) * square))
    half = 0.5 + 0.5 * bent
    slope = half + (0.5 * pre) * (1.0 - bent * bent) * (root + (3.0 * 0.044715 * root) * square)
    return pre * half, slope


def expert_kernel(
    h2_ref,
    h2_other_ref,
    up_ref,
    up_other_ref,
    w_up_ref,
    w_down_ref,
    hidden_ref,
    dpre_ref,
    dh2_kept_ref,
    dh2_sent_ref,
    rows_ref,
    grads_ref,
    dh2_ref,
):
    count = h2_ref.shape[0]

    @pl.when(pl.program_id(0) == 0)
    def _():
        rows_ref[:count] = h2_ref[...]
        rows_ref[count:] = h2_other_ref[...]
        grads_ref[:count] = up_ref[...]
        grads_ref[count:] = up_other_ref[...]
        dh2_ref[...] = jnp.zeros_like(dh2_ref)

    w_up, w_down = w_up_ref[...], w_down_ref[...]
    pre = dot(rows_ref[...], w_up)
    gelu, slope = gelu_and_slope(pre)
    hidden = gelu.astype(BF16)
    hidden_ref[...] = hidden
    dpre = (dot_nt(grads_ref[...], w_down) * slope).astype(BF16)
    dpre_ref[...] = dpre
    dh2_ref[...] += dot_nt(dpre, w_up)

    @pl.when(pl.program_id(0) == pl.num_programs(0) - 1)
    def _():
        dh2_kept_ref[...] = dh2_ref[:count]
        dh2_sent_ref[...] = dh2_ref[count:].astype(BF16)


def store_sums(sums_ref, upstream, normed):
    for which, total in enumerate((upstream * normed, upstream)):
        total = jnp.sum(total, axis=0, keepdims=True)
        pieces = total.shape[1] // 128
        for at in range(pieces):
            row = which * pieces + at
            sums_ref[row : row + 1] = total[:, at * 128 : (at + 1) * 128]


def norm2_back_kernel(
    kept_ref,
    came_ref,
    resid_ref,
    grad_ref,
    gain_ref,
    dresid_far,
    packed_ref,
    sums_ref,
    dresid_ref,
    sem,
    *,
    cap,
):
    dh2 = kept_ref[...] + came_ref[...].astype(F32)
    normed, inverse = normalise(resid_ref[...])
    dresid = grad_ref[...].astype(F32) + norm_back(dh2, normed, inverse, gain_ref[...])
    dresid_ref[...] = dresid
    leaving = started(dresid_ref, dresid_far, sem)
    slot_of = lax.broadcasted_iota(jnp.int32, (1, dh2.shape[0]), 1)
    pack(packed_ref, dresid.astype(BF16), slot_of, cap, False)
    store_sums(sums_ref, dh2, normed)
    leaving.wait()


def out_grad_kernel(where_ref, own_ref, other_ref, context_far, dattn_ref, *rest):
    piece_fars, (context_ref, grad_ref, piece_ref, sems) = rest[:4], rest[4:]
    arriving = started(context_far, context_ref, sems.at[4])
    half = own_ref.shape[0]
    here = where_ref[0]
    dattn_ref[pl.ds(pl.multiple_of(here * half, half), half), :] = own_ref[...]
    dattn_ref[pl.ds(pl.multiple_of((1 - here) * half, half), half), :] = other_ref[...]
    arriving.wait()
    grad_ref[...] = dot_tn(context_ref[...], dattn_ref[...])
    width = grad_ref.shape[1]
    quarter = grad_ref.shape[0] // 4
    owners = piece_ref.shape[1]
    rows = quarter // owners
    leaving = []
    for step in (1, 2, 3, 0):
        first = (where_ref[1] ^ step) * quarter
        for owner in range(owners):
            start = pl.multiple_of(first + owner * rows, rows)
            block = grad_ref[pl.ds(start, rows), :]
            piece_ref[step, owner] = jnp.concatenate(
                [block[:, at : at + 128] for at in range(0, width, 128)], axis=0
            ).astype(BF16)
        leaving.append(started(piece_ref.at[step], piece_fars[step], sems.at[step]))
    for copy in leaving:
        copy.wait()


def attend_back_kernel(
    where_ref,
    lengths_ref,
    dattn_ref,
    qkv_far,
    context_far,
    logsum_far,
    w_qkv_far,
    w_out_far,
    kept_ref,
    sent_ref,
    *rest,
    step,
    reach,
    scale,
):
    dvalue_fars, dkq_fars = rest[:4], rest[4:8]
    dcontext_ref, inner_ref, dquery_ref, dqkv_ref = rest[8:12]
    qkv_ref, context_ref, logsum_ref, w_qkv_ref, w_out_ref, sems = rest[12:]
    arriving = [
        started(source, target, sems.at[at])
        for at, (source, target) in enumerate(
            (
                (w_out_far, w_out_ref),
                (context_far, context_ref),
                (qkv_far, qkv_ref),
                (logsum_far, logsum_ref),
                (w_qkv_far, w_qkv_ref),
            )
        )
    ]
    half = kept_ref.shape[0]
    span = 2 * half
    here = where_ref[0]
    own_start = pl.multiple_of(here * half, half)
    other_start = pl.multiple_of((1 - here) * half, half)
    arriving[0].wait()
    dcontext = dot_nt(dattn_ref[...], w_out_ref[...]).astype(BF16)
    dcontext_ref[...] = dcontext
    arriving[1].wait()
    arriving[2].wait()
    arriving[3].wait()
    heads = qkv_ref.shape[2] // HEAD_DIM
    columns_all = qkv_ref.shape[2]
    product = dcontext.astype(F32) * context_ref[...].astype(F32)
    coarse = product.astype(BF16)
    fine = (product - coarse.astype(F32)).astype(BF16)
    of_head = (
        lax.broadcasted_iota(jnp.int32, (16, columns_all), 1) // HEAD_DIM
        == lax.broadcasted_iota(jnp.int32, (16, columns_all), 0)
    ).astype(BF16)
    inner_ref[...] = dot_nt(of_head, coarse) + dot_nt(of_head, fine)
    dquery_ref[...] = jnp.zeros_like(dquery_ref)
    for start in range(0, span, step):
        stop = start + step
        high = min(span, stop + reach)
        shape = (step, high - start)
        key_at = lax.broadcasted_iota(jnp.int32, shape, 0) + start
        query_at = lax.broadcasted_iota(jnp.int32, shape, 1) + start
        allowed = (segments(lengths_ref, query_at) == segments(lengths_ref, key_at)) & (
            key_at <= query_at
        )
        allowed = jnp.concatenate([allowed.astype(F32)] * heads, axis=0) > 0.5
        lane = lax.broadcasted_iota(jnp.int32, (step, 2 * HEAD_DIM), 1)
        pairs = [
            slice(at, at + 2 * HEAD_DIM) for at in range(0, heads * HEAD_DIM, 2 * HEAD_DIM)
        ]
        keys = [two_heads(qkv_ref[1, start:stop, columns]) for columns in pairs]

        def by_head(ref, start=start, high=high):
            return jnp.concatenate(
                [
                    jnp.broadcast_to(ref[head : head + 1, start:high], (step, high - start))
                    for head in range(heads)
                ],
                axis=0,
            )

        scores = jnp.concatenate(
            [
                dot_nt(keys[at], qkv_ref[0, start:high, columns])
                for at, columns in enumerate(pairs)
            ],
            axis=0,
        )
        probs = jnp.exp(jnp.where(allowed, scores * scale - by_head(logsum_ref), -1e30))
        dprobs = jnp.concatenate(
            [
                dot_nt(two_heads(qkv_ref[2, start:stop, columns]), dcontext_ref[start:high, columns])
                for columns in pairs
            ],
            axis=0,
        )
        dscores = (probs * (dprobs - by_head(inner_ref))).astype(BF16)
        probs = probs.astype(BF16)
        for at, columns in enumerate(pairs):
            mine = slice(2 * at * step, 2 * (at + 1) * step)
            dvalues = dot(probs[mine], dcontext_ref[start:high, columns])
            dkeys = dot(dscores[mine], qkv_ref[0, start:high, columns])
            dquery_ref[start:high, columns] += dot_tn(dscores[mine], keys[at])
            dqkv_ref[1, start:stop, columns] = (
                jnp.where(lane < HEAD_DIM, dkeys[:step], dkeys[step:]) * scale
            ).astype(BF16)
            dqkv_ref[2, start:stop, columns] = jnp.where(
                lane < HEAD_DIM, dvalues[:step], dvalues[step:]
            ).astype(BF16)
    dqkv_ref[0] = (dquery_ref[...] * scale).astype(BF16)

    quarter = columns_all // 4
    leaving = []
    for kind, at in ((2, 1), (2, 2), (2, 3), (1, 1), (0, 1), (1, 2), (0, 2), (1, 3), (0, 3), (2, 0), (1, 0), (0, 0)):
        first = pl.multiple_of((where_ref[1] ^ at) * quarter, quarter)
        target = dvalue_fars[at] if kind == 2 else dkq_fars[at].at[1 - kind]
        leaving.append(
            started(dqkv_ref.at[kind, :, pl.ds(first, quarter)], target, sems.at[5 + kind * 4 + at])
        )
    arriving[4].wait()

    def back_rows(start):
        total = dot_nt(dqkv_ref[0, pl.ds(start, half), :], w_qkv_ref[0])
        total = total + dot_nt(dqkv_ref[1, pl.ds(start, half), :], w_qkv_ref[1])
        return total + dot_nt(dqkv_ref[2, pl.ds(start, half), :], w_qkv_ref[2])

    sent_ref[...] = back_rows(other_start).astype(BF16)
    kept_ref[...] = back_rows(own_start)
    for copy in leaving:
        copy.wait()


def token_grad(where_ref, grad_refs, index, input_ref, own_refs, other_refs):
    half = own_refs[0].shape[0]
    own_start = pl.multiple_of(where_ref[0] * half, half)
    other_start = pl.multiple_of((1 - where_ref[0]) * half, half)

    def rows(ref, start, count):
        return ref[pl.ds(start, count), :] if index is None else ref[index, pl.ds(start, count), :]

    total = dot_tn(rows(grad_refs[0], 0, 2 * half), input_ref[...])
    for grad_ref, own_ref, other_ref in zip(grad_refs[1:], own_refs, other_refs):
        total = total + dot_tn(rows(grad_ref, own_start, half), own_ref[...])
        total = total + dot_tn(rows(grad_ref, other_start, half), other_ref[...])
    return total.T


def store_halves(where_ref, bit, half_refs, load, at):
    rows = at.stop - at.start
    for side, half_ref in enumerate(half_refs):
        mine = ((where_ref[2] >> bit) & 1) ^ side
        for index in range(half_ref.shape[0]):
            half_ref[index, at] = load(2 * index + mine, rows).astype(BF16)


def value_grad_kernel(where_ref, *refs):
    grad_refs, input_ref, own_refs, other_refs = refs[0:4], refs[4], refs[5:8], refs[8:11]
    out_refs, half_refs, total_ref = refs[11:15], refs[15:17], refs[17]
    total_ref[...] = token_grad(where_ref, grad_refs, None, input_ref, own_refs, other_refs)
    rows = half_refs[0].shape[1] // 2
    store_halves(
        where_ref, 0, half_refs,
        lambda owner, rows: sum(ref[owner].astype(F32) for ref in out_refs), slice(0, rows),
    )
    store_halves(
        where_ref, 0, half_refs,
        lambda owner, rows: total_ref[pl.ds(pl.multiple_of(owner * rows, rows), rows), :],
        slice(rows, 2 * rows),
    )


def key_query_grad_kernel(where_ref, *refs):
    grad_refs, input_ref, own_refs, other_refs = refs[0:4], refs[4], refs[5:8], refs[8:11]
    half_refs, total_ref = refs[11:13], refs[13]
    rows = half_refs[0].shape[1] // 2
    for index in range(2):
        total_ref[...] = token_grad(where_ref, grad_refs, index, input_ref, own_refs, other_refs)
        store_halves(
            where_ref, 0, half_refs,
            lambda owner, rows: total_ref[pl.ds(pl.multiple_of(owner * rows, rows), rows), :],
            slice(index * rows, (index + 1) * rows),
        )


def add_kernel(where_ref, kept_ref, came_ref, *half_refs, bit):
    store_halves(
        where_ref, bit, half_refs,
        lambda owner, rows: kept_ref[owner].astype(F32) + came_ref[owner].astype(F32),
        slice(0, kept_ref.shape[1]),
    )


def last_add_kernel(kept_ref, came_ref, out_ref):
    out_ref[...] = (kept_ref[0].astype(F32) + came_ref[0].astype(F32)).astype(BF16)


def split_store(out_ref, start, value):
    rows = value.shape[0]
    coarse = value.astype(BF16)
    out_ref[start : start + rows] = coarse
    out_ref[start + rows : start + 2 * rows] = (value - coarse.astype(F32)).astype(BF16)


def last_add_sums_kernel(kept_ref, came_ref, *refs):
    out_ref = refs[4]
    rows = kept_ref.shape[1]
    out_ref[:rows] = (kept_ref[0].astype(F32) + came_ref[0].astype(F32)).astype(BF16)
    sums = jnp.concatenate([refs[0][...] + refs[1][...], refs[2][...] + refs[3][...]], axis=0)
    split_store(out_ref, rows, sums)


def split_sum(refs, start, stop):
    rows = (stop - start) // 2
    return sum(
        ref[start : start + rows].astype(F32) + ref[start + rows : stop].astype(F32)
        for ref in refs
    )


def stack_kernel(own_ref, came_ref, out_ref, *, sums):
    rows = own_ref.shape[0] - sums
    out_ref[:rows] = own_ref[:rows]
    out_ref[rows : 2 * rows] = came_ref[:rows]
    if sums:
        split_store(out_ref, 2 * rows, split_sum((own_ref, came_ref), rows, rows + sums))


def place_rows(where_ref, digits, at):
    bits = 2 * (digits - 1)
    return where_ref[2] ^ sum(((at >> bit) & 1) << (bits - 1 - bit) for bit in range(bits))


def each_piece(where_ref, refs, digits, rows, use, steps=range(4)):
    owners = 4 ** (digits - 1)
    for step in steps:
        column = where_ref[1] ^ step
        for at in range(owners):
            owner = place_rows(where_ref, digits, at)
            first = at * 2 * rows

            def load(low, high, first=first, step=step):
                if step < 3:
                    return refs[step][first + low : first + high]
                middle = refs[3].shape[0]
                start, stop = first + low, first + high
                if stop <= middle:
                    return refs[3][start:stop]
                if start >= middle:
                    return refs[4][start - middle : stop - middle]
                return jnp.concatenate([refs[3][start:middle], refs[4][: stop - middle]], axis=0)

            use(column, owner, load)


def out_value_pieces(where_ref, refs, digits, steps, value_ref, value_column, out_ref, out_first):
    width = value_ref.shape[1]
    rows = width // 4 ** (digits - 1)
    few = rows * 128 // width

    def use(column, owner, load):
        start = pl.multiple_of(out_first(column) + owner * few, few)
        out_ref[pl.ds(start, few), :] = jnp.concatenate(
            [load(at, at + few).astype(F32) for at in range(0, rows, few)], axis=1
        )
        lanes = pl.ds(pl.multiple_of(value_column(column), 128), 128)
        value_ref[0, pl.ds(pl.multiple_of(owner * rows, rows), rows), lanes] = load(
            rows, 2 * rows
        ).astype(F32)

    each_piece(where_ref, refs, digits, rows, use, steps)


def finish_out_value_near_kernel(where_ref, *refs, digits):
    value_ref, out_ref = refs[3:]

    def place(column):
        return column * 128

    out_value_pieces(where_ref, refs[:3], digits, range(3), value_ref, place, out_ref, place)


def finish_out_value_far_kernel(where_ref, *refs, digits):
    halves, (_, _, value_far, out_far, value_ref, out_ref, sems) = refs[:2], refs[2:]
    out_value_pieces(
        where_ref, (None, None, None, *halves), digits, range(3, 4),
        value_ref, lambda column: 0, out_ref, lambda column: 0,
    )
    first = pl.ds(pl.multiple_of((where_ref[1] ^ 3) * 128, 128), 128)
    leaving = [
        started(value_ref, value_far.at[pl.ds(2, 1), :, first], sems.at[0]),
        started(out_ref, out_far.at[first], sems.at[1]),
    ]
    for copy in leaving:
        copy.wait()


def finish_near_kernel(where_ref, *refs, digits, sums):
    qkv_ref, sums_ref = refs[4:]
    width = qkv_ref.shape[1]
    rows = width // 4 ** (digits - 1)

    def use(column, owner, load):
        lanes = pl.ds(pl.multiple_of(column * 128, 128), 128)
        down = pl.ds(pl.multiple_of(owner * rows, rows), rows)
        qkv_ref[1, down, lanes] = load(0, rows).astype(F32)
        qkv_ref[0, down, lanes] = load(rows, 2 * rows).astype(F32)

    each_piece(where_ref, refs[:3], digits, rows, use, range(3))
    total = refs[0].shape[0]
    sums_ref[...] = split_sum(refs[:3], total - sums, total)


def finish_far_kernel(where_ref, *refs, digits, sums):
    halves, near_sums_ref, _, qkv_far, *sums_refs, total_ref, sem = refs[:2], *refs[2:]
    width = total_ref.shape[1]
    rows = width // 4 ** (digits - 1)

    def use(column, owner, load):
        down = pl.ds(pl.multiple_of(owner * rows, rows), rows)
        total_ref[1, down, :] = load(0, rows).astype(F32)
        total_ref[0, down, :] = load(rows, 2 * rows).astype(F32)

    each_piece(where_ref, (None, None, None, *halves), digits, rows, use, range(3, 4))
    lanes = pl.ds(pl.multiple_of((where_ref[1] ^ 3) * 128, 128), 128)
    leaving = started(total_ref, qkv_far.at[pl.ds(0, 2), :, lanes], sem)
    half = halves[1].shape[0]
    total_sums = near_sums_ref[...] + split_sum(halves[1:], half - sums, half)
    count = total_sums.shape[0] // len(sums_refs)
    for at, sums_ref in enumerate(sums_refs):
        sums_ref[...] = total_sums[at * count : (at + 1) * count]
    leaving.wait()


def expert_grad_kernel(rows_ref, grads_ref, hidden_ref, dpre_ref, up_ref, down_ref, turned_ref):
    @pl.when(pl.program_id(0) == 0)
    def _():
        turned_ref[...] = rows_ref[...].T

    up_ref[...] = dot(turned_ref[...], dpre_ref[...])
    down_ref[...] = dot_tn(hidden_ref[...], grads_ref[...])


def branch_kernel(hidden_ref, w_down_ref, kept_ref, sent_ref, branch_ref):
    @pl.when(pl.program_id(0) == 0)
    def _():
        branch_ref[...] = jnp.zeros_like(branch_ref)

    branch_ref[...] += dot(hidden_ref[...], w_down_ref[...])

    @pl.when(pl.program_id(0) == pl.num_programs(0) - 1)
    def _():
        count = kept_ref.shape[0]
        kept_ref[...] = branch_ref[:count].astype(BF16)
        sent_ref[...] = branch_ref[count:].astype(BF16)


def norm1_back_kernel(packed_ref, x_ref, dresid_ref, gain_ref, out_ref, sums_ref, *, cap):
    count, width = x_ref.shape
    dh1 = unpack(packed_ref, slots_down(count), cap, width)
    normed, inverse = normalise(x_ref[...].astype(F32))
    out_ref[...] = dresid_ref[...] + norm_back(dh1, normed, inverse, gain_ref[...])
    store_sums(sums_ref, dh1, normed)


VMEM = pl.BlockSpec(memory_space=pltpu.VMEM)
SMEM = pl.BlockSpec(memory_space=pltpu.SMEM)


def after(value, *others):
    return lax.optimization_barrier((value, *others))[0]


def far(value):
    return pltpu.with_memory_space_constraint(value, pltpu.HBM)


def call(kernel, name, outs, args, flops, scalars=0, scratch=(), limit=16, away=(), out_away=(), raw=(), out_raw=()):
    shapes = [
        pltpu.HBM(shape, kind)
        if at in out_away or at in out_raw
        else jax.ShapeDtypeStruct(shape, kind)
        for at, (shape, kind) in enumerate(outs)
    ]

    def spec(at, away, raw):
        if at in raw:
            return pl.BlockSpec(memory_space=pltpu.HBM)
        return pl.BlockSpec() if at in away else VMEM

    size = sum(math.prod(a.shape) * a.dtype.itemsize for a in (*args, *shapes))
    return pl.pallas_call(
        kernel,
        name=name,
        out_shape=shapes,
        in_specs=[
            SMEM if at < scalars else spec(at, away, raw) for at in range(len(args))
        ],
        out_specs=[spec(at, out_away, out_raw) for at in range(len(outs))],
        scratch_shapes=list(scratch),
        cost_estimate=pl.CostEstimate(flops=flops, bytes_accessed=size, transcendentals=0),
        compiler_params=pltpu.CompilerParams(vmem_limit_bytes=limit * MIB),
    )(*[far(value) if at in away or at in raw else value for at, value in enumerate(args)])


def expert(h2, h2_other, upstream, upstream_other, w_up, w_down):
    count, width = h2.shape
    units = w_up.shape[1]
    tile = min(512, units)
    shapes = [
        ((2 * count, units), BF16),
        ((2 * count, units), BF16),
        ((count, width), F32),
        ((count, width), BF16),
        ((2 * count, width), BF16),
        ((2 * count, width), BF16),
    ]
    stay = (2, 3)
    both = pl.BlockSpec((2 * count, width), lambda j: (0, 0))
    rows = pl.BlockSpec((count, width), lambda j: (0, 0))
    by_unit = pl.BlockSpec((2 * count, tile), lambda j: (0, j))
    return pl.pallas_call(
        expert_kernel,
        name="expert",
        grid=(units // tile,),
        out_shape=[
            jax.ShapeDtypeStruct(shape, kind) if at in stay else pltpu.HBM(shape, kind)
            for at, (shape, kind) in enumerate(shapes)
        ],
        in_specs=[rows] * 4
        + [
            pl.BlockSpec((width, tile), lambda j: (0, j)),
            pl.BlockSpec((tile, width), lambda j: (j, 0)),
        ],
        out_specs=[by_unit, by_unit, rows, rows, both, both],
        scratch_shapes=[
            pltpu.VMEM((2 * count, width), F32),
        ],
        cost_estimate=pl.CostEstimate(
            flops=12 * count * width * units, bytes_accessed=16 * MIB, transcendentals=0
        ),
        compiler_params=pltpu.CompilerParams(vmem_limit_bytes=40 * MIB),
    )(h2, h2_other, upstream, upstream_other, w_up, w_down)


def expert_grads(rows, grads, hidden, dpre):
    count, width = rows.shape
    units = hidden.shape[1]
    tile = min(512, units)
    whole = pl.BlockSpec((count, width), lambda j: (0, 0))
    by_unit = pl.BlockSpec((count, tile), lambda j: (0, j))
    return pl.pallas_call(
        expert_grad_kernel,
        name="expert_grads",
        grid=(units // tile,),
        out_shape=[pltpu.HBM((width, units), F32), pltpu.HBM((units, width), F32)],
        in_specs=[whole] * 2 + [by_unit] * 2,
        out_specs=[
            pl.BlockSpec((width, tile), lambda j: (0, j)),
            pl.BlockSpec((tile, width), lambda j: (j, 0)),
        ],
        scratch_shapes=[pltpu.VMEM((width, count), BF16)],
        cost_estimate=pl.CostEstimate(
            flops=4 * count * width * units, bytes_accessed=24 * MIB, transcendentals=0
        ),
        compiler_params=pltpu.CompilerParams(vmem_limit_bytes=40 * MIB),
    )(far(rows), far(grads), far(hidden), far(dpre))


def expert_branch(hidden, w_down):
    count, units = hidden.shape
    width = w_down.shape[1]
    tile = min(512, units)
    half = pl.BlockSpec((count // 2, width), lambda j: (0, 0))
    return pl.pallas_call(
        branch_kernel,
        name="expert_branch",
        grid=(units // tile,),
        out_shape=[pltpu.HBM((count // 2, width), BF16)] * 2,
        in_specs=[
            pl.BlockSpec((count, tile), lambda j: (0, j)),
            pl.BlockSpec((tile, width), lambda j: (j, 0)),
        ],
        out_specs=[half, half],
        scratch_shapes=[pltpu.VMEM((count, width), F32)],
        cost_estimate=pl.CostEstimate(
            flops=2 * count * width * units, bytes_accessed=8 * MIB, transcendentals=0
        ),
        compiler_params=pltpu.CompilerParams(vmem_limit_bytes=20 * MIB),
    )(far(hidden), far(w_down))


def flip(value, axis, bit):
    size = lax.axis_size(axis)
    return lax.ppermute(value, axis, [(i, i ^ bit) for i in range(size)])


def to_others(values, digit):
    return [
        flip(values[m] if isinstance(values, (list, tuple)) else values, "exp", m << (2 * digit))
        for m in range(1, 4)
    ]


def after_all(values, *others):
    return list(lax.optimization_barrier((*values, *others))[: len(values)])


def sum_and_spread(first, second, where, digits, sums, extra, finish_near, finish_far, first_wait, filler):
    bits = 2 * (digits - 1)

    def across(value, bit):
        return flip(value, "exp", 4 << bit)

    def add(halves, came, bit, sums=None):
        owners, rows, columns = came.shape
        if bit + 1 < bits:
            return call(
                functools.partial(add_kernel, bit=bit + 1), "add",
                [((owners // 2, rows, columns), BF16)] * 2, [where, halves[0], came], 0, scalars=1,
            )
        if sums is None:
            return call(
                last_add_kernel, "last_add", [((rows, columns), BF16)], [halves[0], came], 0,
            )
        return call(
            last_add_sums_kernel, "last_add_sums", [((rows + extra, columns), BF16)],
            [halves[0], came, *sums], 0,
        )

    def stack(own, came, sums):
        rows, columns = own.shape
        return call(
            functools.partial(stack_kernel, sums=sums), "stack",
            [((2 * rows - sums, columns), BF16)], [own, came], 0,
        )[0]

    def steps(halves, sums, extra):
        for bit in range(bits):
            came = yield halves[1], [across(halves[1], bit)]
            halves = add(halves, came[0], bit, sums)
        total = halves[0]
        for bit in reversed(range(bits)):
            came = yield total, [across(total, bit)]
            total = stack(total, came[0], extra)
        by_x, by_y = yield total, [flip(total, "exp", 1), flip(total, "exp", 2)]
        if extra == 0:
            near.extend(finish_near(total, by_x, by_y))
        middle = total.shape[0] // 2
        sent = [by_y[:middle], by_x[middle:]]
        halves = yield sent[0], [flip(sent[0], "exp", 1), flip(sent[1], "exp", 2)]
        yield None, [total, by_x, by_y, *halves]

    near = []
    lines, states, last, finished = [steps(first, None, 0), None], [None, None], first_wait, None
    states[0] = next(lines[0])
    for at, line in enumerate([0] + [0, 1] * (2 * bits + 1) + [1]):
        if at == 1:
            pieces = second(last)
            lines[1], last = steps(pieces, sums, extra), pieces[1]
            states[1] = next(lines[1])
        ahead = [*near[1:], filler] if line == 0 and near else []
        states[line] = lines[line].send(after_all(states[line][1], last, *ahead))
        last = states[line][0]
        if line == 0 and last is None:
            finished = finish_far(*states[0][1][3:], *near)
            last = states[0][1][3]
        elif finished is not None:
            last = finished[1]
    return finished, states[1][1]


def on_device(
    block_input,
    dispatch,
    lengths,
    ln1_gain,
    ln1_bias,
    ln2_gain,
    ln2_bias,
    w_qkv,
    w_out,
    w_up,
    w_down,
    grad_output,
):
    slots, width = block_input.shape
    seq_rows = dispatch.shape[0]
    n_exp = lax.axis_size("exp")
    devices = n_exp * lax.axis_size("head")
    cap = slots // devices
    span = 2 * seq_rows
    columns = w_qkv.shape[2]
    scale = 1.0 / math.sqrt(HEAD_DIM)
    digits = (n_exp.bit_length() - 1) // 2
    place = lax.axis_index("exp")
    where = jnp.stack(
        [lax.axis_index("head"), place & 3, place >> 2]
    ).astype(jnp.int32)
    step = 128
    reach = 3 * seq_rows // 4
    packed = ((devices * 8, cap * 128), BF16)
    moving = 2 * devices * 8 * max(slots, seq_rows) * width * 3
    gain1, bias1 = ln1_gain.reshape(1, width), ln1_bias.reshape(1, width)
    gain2, bias2 = ln2_gain.reshape(1, width), ln2_bias.reshape(1, width)
    along = dispatch.reshape(1, seq_rows)

    def exchange(value):
        value = value.reshape(devices, 8, cap * 128)
        value = lax.all_to_all(value, ("exp", "head"), split_axis=0, concat_axis=0, tiled=True)
        return value.reshape(devices * 8, cap * 128)

    def cross(value):
        return flip(value, "head", 1)

    (h1,) = call(
        functools.partial(norm1_kernel, cap=cap), "norm1", [packed],
        [block_input, gain1, bias1], moving, away=(0, 1, 2),
    )
    arrived = exchange(h1)
    (own,) = call(
        functools.partial(gather_kernel, cap=cap), "gather1", [((seq_rows, width), BF16)],
        [arrived, along], moving,
    )
    other = cross(own)
    own_copy, inputs, qkv, context, logsum, attn_kept, attn_sent = call(
        functools.partial(attend_kernel, step=step, reach=reach, scale=scale),
        "attend",
        [
            ((seq_rows, width), BF16),
            ((span, width), BF16),
            ((3, span, columns), BF16),
            ((span, columns), BF16),
            ((128, span), F32),
            ((seq_rows, width), F32),
            ((seq_rows, width), BF16),
        ],
        [where, lengths, own, other, w_qkv, w_out],
        2 * span * width * columns * 4 + 16 * span * span * columns,
        scalars=2,
        limit=24,
        raw=(4, 5),
        out_raw=range(5),
        scratch=[
            pltpu.VMEM((3, width, columns), BF16),
            pltpu.VMEM((columns, width), BF16),
            pltpu.VMEM((span, width), BF16),
            pltpu.VMEM((3, span, columns), BF16),
            pltpu.VMEM((span, columns), BF16),
            pltpu.VMEM((128, span), F32),
            pltpu.SemaphoreType.DMA((9,)),
        ],
    )
    (sent,) = call(
        functools.partial(scatter_kernel, cap=cap, fill=True), "scatter1", [packed],
        [attn_kept, cross(attn_sent), along], moving,
    )
    attn_back = exchange(sent)
    by_xy = flip(after(own_copy, attn_back), "exp", 3)
    resid, h2, upstream, valid = call(
        functools.partial(norm2_kernel, cap=cap),
        "norm2",
        [((slots, width), F32), ((slots, width), BF16), ((slots, width), BF16), ((slots, 128), F32)],
        [attn_back, block_input, grad_output, gain2, bias2],
        moving,
    )
    h2_other, upstream_other = cross(h2), cross(upstream)
    hidden, dpre, dh2_kept, dh2_sent, rows_all, grads_all = expert(
        h2, h2_other, upstream, upstream_other, w_up[0], w_down[0]
    )
    dh2_sent = after(dh2_sent, by_xy)
    dresid, sent, sums2 = call(
        functools.partial(norm2_back_kernel, cap=cap),
        "norm2_back",
        [((slots, width), F32), packed, ((width // 64, 128), F32)],
        [dh2_kept, cross(dh2_sent), resid, grad_output, gain2],
        moving,
        out_raw=(0,),
        scratch=[pltpu.VMEM((slots, width), F32), pltpu.SemaphoreType.DMA],
    )
    arrived = exchange(sent)
    near_own, hidden, far_own = after_all([own_copy, hidden, by_xy], sent)
    by_x, by_y = flip(near_own, "exp", 1), flip(near_own, "exp", 2)
    far_other = cross(far_own)
    grad_up, grad_down = expert_grads(rows_all, grads_all, hidden, dpre)
    arrived, grad_up, grad_down, by_x, by_y, far_other = lax.optimization_barrier(
        (arrived, grad_up, grad_down, by_x, by_y, far_other)
    )
    plane_own = [by_x, by_y, far_own]
    plane_other = [cross(by_x), cross(by_y), far_other]
    (own,) = call(
        functools.partial(gather_kernel, cap=cap), "gather2", [((seq_rows, width), BF16)],
        [arrived, along], moving,
    )
    other = cross(own)
    piece = 4 * width // n_exp
    dattn, *out_pieces = call(
        out_grad_kernel,
        "out_grad",
        [((span, width), BF16), *[((n_exp // 4, piece, 128), BF16)] * 4],
        [where, own, other, context],
        2 * span * width * columns,
        scalars=1,
        scratch=[
            pltpu.VMEM((span, columns), BF16),
            pltpu.VMEM((columns, width), F32),
            pltpu.VMEM((4, n_exp // 4, piece, 128), BF16),
            pltpu.SemaphoreType.DMA((5,)),
        ],
        raw=(3,),
        out_raw=range(1, 5),
    )
    out_parts = [out_pieces[0], *to_others(out_pieces, 0)]
    du_kept, du_sent, *parts = call(
        functools.partial(attend_back_kernel, step=step, reach=reach, scale=scale),
        "attend_back",
        [
            ((seq_rows, width), F32),
            ((seq_rows, width), BF16),
            *[((span, 128), BF16)] * 4,
            *[((2, span, 128), BF16)] * 4,
        ],
        [where, lengths, dattn, qkv, context, logsum, w_qkv, w_out],
        2 * span * width * columns * 4 + 40 * span * span * columns,
        scalars=2,
        limit=24,
        raw=range(3, 8),
        out_raw=range(2, 10),
        scratch=[
            pltpu.VMEM((span, columns), BF16),
            pltpu.VMEM((16, span), F32),
            pltpu.VMEM((span, columns), F32),
            pltpu.VMEM((3, span, columns), BF16),
            pltpu.VMEM((3, span, columns), BF16),
            pltpu.VMEM((span, columns), BF16),
            pltpu.VMEM((128, span), F32),
            pltpu.VMEM((3, width, columns), BF16),
            pltpu.VMEM((columns, width), BF16),
            pltpu.SemaphoreType.DMA((17,)),
        ],
    )
    du_sent, *parts = after_all([du_sent, *parts], *out_parts[1:], *plane_other)
    value_parts = [parts[0], *to_others(parts[:4], 0)]
    key_query_parts = [parts[4], *to_others(after_all(parts[4:], *value_parts[1:]), 0)]
    (sent,) = call(
        functools.partial(scatter_kernel, cap=cap, fill=False), "scatter2", [packed],
        [du_kept, cross(du_sent), along], moving,
    )
    arrived = exchange(after(sent, *value_parts[1:]))
    input_grad, sums1 = call(
        functools.partial(norm1_back_kernel, cap=cap),
        "norm1_back",
        [((slots, width), F32), ((width // 64, 128), F32)],
        [arrived, block_input, dresid, gain1],
        moving,
        away=(1, 2, 3),
        out_away=(0,),
    )
    tokens = [inputs, *after_all([*plane_own, *plane_other], du_sent)]
    split = [((n_exp // 8, 2 * piece, 128), BF16)] * 2
    product = 8 * span * width * 128
    out_value = call(
        value_grad_kernel, "value_grad", split, [where, *value_parts, *tokens, *out_parts],
        product, scalars=1, scratch=[pltpu.VMEM((width, 128), F32)], away=(1, *range(5, 13)),
    )
    branch_kept, branch_sent = expert_branch(after(hidden, out_value[1]), w_down[0])
    branch_came = cross(branch_sent)
    branch = branch_kept.astype(F32) + branch_came.astype(F32)
    result = (resid + valid[:, :1] * branch).astype(BF16)

    def key_query(last):
        came = after_all(key_query_parts[1:], last)
        return call(
            key_query_grad_kernel, "key_query_grad", split,
            [where, key_query_parts[0], *came, *tokens], 2 * product, scalars=1,
            scratch=[pltpu.VMEM((width, 128), F32)], away=(1, *range(5, 12)),
        )

    sums = [sums1, cross(sums1), sums2, cross(sums2)]
    extra = 4 * sums1.shape[0]
    whole_qkv = pltpu.HBM((3, width, columns), F32)
    whole_out = pltpu.HBM((columns, width), F32)
    in_place = pl.BlockSpec(memory_space=pltpu.HBM)
    finish_near = pl.pallas_call(
        functools.partial(finish_out_value_near_kernel, digits=digits),
        name="finish_out_value_near",
        grid=(1,),
        out_shape=[whole_qkv, whole_out],
        in_specs=[SMEM] + [VMEM] * 3,
        out_specs=[
            pl.BlockSpec((1, width, columns), lambda i: (2, 0, 0)),
            pl.BlockSpec((columns, width), lambda i: (0, 0)),
        ],
        cost_estimate=pl.CostEstimate(flops=0, bytes_accessed=6 * MIB, transcendentals=0),
        compiler_params=pltpu.CompilerParams(vmem_limit_bytes=20 * MIB),
    )
    finish_far = pl.pallas_call(
        functools.partial(finish_out_value_far_kernel, digits=digits),
        name="finish_out_value_far",
        out_shape=[whole_qkv, whole_out],
        in_specs=[SMEM] + [VMEM] * 2 + [in_place] * 2,
        out_specs=[in_place] * 2,
        scratch_shapes=[
            pltpu.VMEM((1, width, 128), F32),
            pltpu.VMEM((128, width), F32),
            pltpu.SemaphoreType.DMA((2,)),
        ],
        input_output_aliases={3: 0, 4: 1},
        cost_estimate=pl.CostEstimate(flops=0, bytes_accessed=2 * MIB, transcendentals=0),
        compiler_params=pltpu.CompilerParams(vmem_limit_bytes=16 * MIB),
    )
    (grad_qkv, grad_out), key_query = sum_and_spread(
        out_value, key_query, where, digits, sums, extra, functools.partial(finish_near, where),
        functools.partial(finish_far, where), branch_sent, result,
    )
    sums_shape = jax.ShapeDtypeStruct((extra // 2, 128), F32)
    grad_qkv, sums = pl.pallas_call(
        functools.partial(finish_near_kernel, digits=digits, sums=extra),
        name="finish_near",
        grid=(1,),
        out_shape=[whole_qkv, sums_shape],
        in_specs=[SMEM] + [VMEM] * 3 + [in_place],
        out_specs=[
            pl.BlockSpec((2, width, columns), lambda i: (0, 0, 0)),
            pl.BlockSpec((extra // 2, 128), lambda i: (0, 0)),
        ],
        input_output_aliases={4: 0},
        cost_estimate=pl.CostEstimate(flops=0, bytes_accessed=6 * MIB, transcendentals=0),
        compiler_params=pltpu.CompilerParams(vmem_limit_bytes=20 * MIB),
    )(where, *key_query[:3], grad_qkv)
    halves = after_all(key_query[3:], sums)
    grad_qkv, *sums = pl.pallas_call(
        functools.partial(finish_far_kernel, digits=digits, sums=extra),
        name="finish_far",
        out_shape=[whole_qkv, *[jax.ShapeDtypeStruct((width // 128, 128), F32)] * 4],
        in_specs=[SMEM] + [VMEM] * 3 + [in_place],
        out_specs=[in_place, *[VMEM] * 4],
        scratch_shapes=[pltpu.VMEM((2, width, 128), F32), pltpu.SemaphoreType.DMA],
        input_output_aliases={4: 0},
        cost_estimate=pl.CostEstimate(flops=0, bytes_accessed=2 * MIB, transcendentals=0),
        compiler_params=pltpu.CompilerParams(vmem_limit_bytes=16 * MIB),
    )(where, *halves, sums, grad_qkv)
    sums = [total.reshape(width) for total in sums]
    return (
        result,
        input_grad,
        sums[0],
        sums[1],
        sums[2],
        sums[3],
        grad_qkv,
        grad_out,
        grad_up[None],
        grad_down[None],
    )


def solution(mesh):
    placed = (
        P(("exp", "head"), None),
        P(("exp", "head")),
        P("exp", None),
        P(),
        P(),
        P(),
        P(),
        P(None, None, "head"),
        P("head", None),
        P("exp", None, "head"),
        P("exp", "head", None),
        P(("exp", "head"), None),
    )
    return jax.shard_map(
        on_device,
        mesh=mesh,
        in_specs=placed,
        out_specs=(
            P(("exp", "head"), None),
            P(("exp", "head"), None),
            P(),
            P(),
            P(),
            P(),
            P(None, None, "head"),
            P("head", None),
            P("exp", None, "head"),
            P("exp", "head", None),
        ),
        check_vma=False,
    )
```

```python
import functools
import math

import jax
import jax.numpy as jnp
from jax import lax
from jax.experimental import pallas as pl
from jax.experimental.pallas import tpu as pltpu
from jax.sharding import PartitionSpec as P

HEAD_DIM = 64
EPS = 1e-05
BF16 = jnp.bfloat16
F32 = jnp.float32
MIB = 1024 * 1024
EMPTY = 1e30


def dot(left, right):
    return lax.dot_general(left, right, (((1,), (0,)), ((), ())), preferred_element_type=F32)


def dot_nt(left, right):
    return lax.dot_general(left, right, (((1,), (1,)), ((), ())), preferred_element_type=F32)


def dot_tn(left, right):
    return lax.dot_general(left, right, (((0,), (0,)), ((), ())), preferred_element_type=F32)


def normalise(rows):
    mean = jnp.mean(rows, axis=1, keepdims=True)
    centred = rows - mean
    inverse = lax.rsqrt(jnp.mean(centred * centred, axis=1, keepdims=True) + EPS)
    return centred * inverse, inverse


def norm_back(upstream, normed, inverse, gain):
    scaled = upstream * gain
    first = jnp.mean(scaled, axis=1, keepdims=True)
    second = jnp.mean(scaled * normed, axis=1, keepdims=True)
    return inverse * (scaled - first - normed * second)


def pack(out_ref, rows, slot_of, cap, fill):
    total, width = out_ref.shape[0], rows.shape[1]
    place = lax.broadcasted_iota(jnp.int32, (total, slot_of.shape[1]), 0)
    first = (place >> 3) * cap
    sub = lax.broadcasted_iota(jnp.int32, (total, 128), 0) & 7
    piece = width // 8

    def placed(target):
        hit = (slot_of == target).astype(F32)
        moved = dot(hit.astype(BF16), rows)
        if fill:
            moved = moved + (1.0 - jnp.sum(hit, axis=1, keepdims=True)) * EMPTY
        return moved

    whole = cap // 8
    for group in range(whole):
        moved = placed(first + (place & 7) + group * 8)
        out_ref[:, group * width : (group + 1) * width] = moved.astype(BF16)
    for left in range(cap % 8):
        moved = placed(first + whole * 8 + left)
        folded = moved[:, :piece]
        for s in range(1, 8):
            folded = jnp.where(sub == s, moved[:, s * piece : (s + 1) * piece], folded)
        start = whole * width + left * piece
        out_ref[:, start : start + piece] = folded.astype(BF16)


def unpack(packed_ref, slot_of, cap, width):
    total = packed_ref.shape[0]
    place = lax.broadcasted_iota(jnp.int32, (slot_of.shape[0], total), 1)
    first = (place >> 3) * cap
    piece = width // 8
    sub = lax.broadcasted_iota(jnp.int32, (total, piece), 0) & 7
    whole = cap // 8
    rows = None
    for group in range(whole):
        hit = (slot_of == first + (place & 7) + group * 8).astype(BF16)
        part = dot(hit, packed_ref[:, group * width : (group + 1) * width])
        rows = part if rows is None else rows + part
    for left in range(cap % 8):
        start = whole * width + left * piece
        folded = packed_ref[:, start : start + piece].astype(F32)
        spread = jnp.concatenate(
            [jnp.where(sub == s, folded, 0.0).astype(BF16) for s in range(8)], axis=1
        )
        hit = (slot_of == first + whole * 8 + left).astype(BF16)
        part = dot(hit, spread)
        rows = part if rows is None else rows + part
    return rows


def slots_down(count):
    return lax.broadcasted_iota(jnp.int32, (count, 1), 0)


def norm1_kernel(x_ref, gain_ref, bias_ref, out_ref, *, cap):
    normed, _ = normalise(x_ref[...].astype(F32))
    rows = (normed * gain_ref[...] + bias_ref[...]).astype(BF16)
    slot_of = lax.broadcasted_iota(jnp.int32, (1, rows.shape[0]), 1)
    pack(out_ref, rows, slot_of, cap, False)


def gather_kernel(packed_ref, dispatch_ref, out_ref, *, cap):
    count = dispatch_ref.shape[1]
    along = jnp.broadcast_to(dispatch_ref[...].astype(F32), (128, count))
    slot_of = along.T[:, :1].astype(jnp.int32)
    out_ref[...] = unpack(packed_ref, slot_of, cap, out_ref.shape[1]).astype(BF16)


def two_heads(rows):
    lane = lax.broadcasted_iota(jnp.int32, rows.shape, 1)
    clear = jnp.zeros_like(rows)
    return jnp.concatenate(
        [jnp.where(lane < HEAD_DIM, rows, clear), jnp.where(lane < HEAD_DIM, clear, rows)], axis=0
    )


def started(source, target, sem):
    copy = pltpu.make_async_copy(source, target, sem)
    copy.start()
    return copy


def segments(lengths_ref, places):
    seg = jnp.zeros(places.shape, jnp.int32)
    end = 0
    for index in range(lengths_ref.shape[1]):
        end = end + lengths_ref[0, index]
        seg = seg + (places >= end).astype(jnp.int32)
    return seg


def attend_kernel(
    where_ref,
    lengths_ref,
    own_ref,
    other_ref,
    w_qkv_far,
    w_out_far,
    own_far,
    input_far,
    qkv_far,
    context_far,
    logsum_far,
    kept_ref,
    sent_ref,
    w_qkv_ref,
    w_out_ref,
    input_ref,
    qkv_ref,
    context_ref,
    logsum_ref,
    sems,
    *,
    step,
    reach,
    scale,
):
    weights = [
        started(w_qkv_far.at[which], w_qkv_ref.at[which], sems.at[which]) for which in range(3)
    ]
    last_weight = started(w_out_far, w_out_ref, sems.at[3])
    leaving = [started(own_ref, own_far, sems.at[4])]
    half = own_ref.shape[0]
    span = 2 * half
    here = where_ref[0]
    own_start = pl.multiple_of(here * half, half)
    other_start = pl.multiple_of((1 - here) * half, half)
    input_ref[pl.ds(own_start, half), :] = own_ref[...]
    input_ref[pl.ds(other_start, half), :] = other_ref[...]
    leaving.append(started(input_ref, input_far, sems.at[5]))
    for which in range(3):
        weights[which].wait()
        qkv_ref[which] = dot(input_ref[...], w_qkv_ref[which]).astype(BF16)
    leaving.append(started(qkv_ref, qkv_far, sems.at[6]))
    heads = qkv_ref.shape[2] // HEAD_DIM
    for start in range(0, span, step):
        stop = start + step
        low = max(0, start - reach)
        shape = (step, stop - low)
        query_at = lax.broadcasted_iota(jnp.int32, shape, 0) + start
        key_at = lax.broadcasted_iota(jnp.int32, shape, 1) + low
        allowed = (segments(lengths_ref, query_at) == segments(lengths_ref, key_at)) & (
            key_at <= query_at
        )
        allowed = jnp.concatenate([allowed.astype(F32)] * heads, axis=0) > 0.5
        lane = lax.broadcasted_iota(jnp.int32, (step, 2 * HEAD_DIM), 1)
        pairs = [
            slice(at, at + 2 * HEAD_DIM) for at in range(0, heads * HEAD_DIM, 2 * HEAD_DIM)
        ]
        scores = jnp.concatenate(
            [
                dot_nt(two_heads(qkv_ref[0, start:stop, columns]), qkv_ref[1, low:stop, columns])
                for columns in pairs
            ],
            axis=0,
        )
        scores = jnp.where(allowed, scores * scale, -1e30)
        top = jnp.max(scores, axis=1, keepdims=True)
        expo = jnp.exp(scores - top)
        total = jnp.sum(expo, axis=1, keepdims=True)
        probs = (expo * (1.0 / total)).astype(BF16)
        logsum = top + jnp.log(total)
        logsums = jnp.zeros((step, 128), F32)
        logsum_lane = lax.broadcasted_iota(jnp.int32, (step, 128), 1)
        for head in range(heads):
            mine = logsum[head * step : (head + 1) * step]
            logsums = jnp.where(logsum_lane == head, mine, logsums)
        for at, columns in enumerate(pairs):
            both = dot(
                probs[2 * at * step : 2 * (at + 1) * step], qkv_ref[2, low:stop, columns]
            )
            context_ref[start:stop, columns] = jnp.where(
                lane < HEAD_DIM, both[:step], both[step:]
            ).astype(BF16)
        logsum_ref[:, start:stop] = logsums.T
    leaving.append(started(context_ref, context_far, sems.at[7]))
    leaving.append(started(logsum_ref, logsum_far, sems.at[8]))
    last_weight.wait()
    sent_ref[...] = dot(context_ref[pl.ds(other_start, half), :], w_out_ref[...]).astype(BF16)
    kept_ref[...] = dot(context_ref[pl.ds(own_start, half), :], w_out_ref[...])
    for copy in leaving:
        copy.wait()


def scatter_kernel(kept_ref, came_ref, dispatch_ref, out_ref, *, cap, fill):
    rows = (kept_ref[...] + came_ref[...].astype(F32)).astype(BF16)
    pack(out_ref, rows, dispatch_ref[...], cap, fill)


def norm2_kernel(
    packed_ref, x_ref, grad_ref, gain_ref, bias_ref, resid_ref, h2_ref, up_ref, valid_ref, *, cap
):
    count, width = x_ref.shape
    moved = unpack(packed_ref, slots_down(count), cap, width)
    valid = (moved[:, :1] < 0.5 * EMPTY).astype(F32)
    resid = x_ref[...].astype(F32) + jnp.where(moved < 0.5 * EMPTY, moved, 0.0)
    resid_ref[...] = resid
    normed, _ = normalise(resid)
    h2_ref[...] = (normed * gain_ref[...] + bias_ref[...]).astype(BF16)
    up_ref[...] = (grad_ref[...].astype(F32) * valid).astype(BF16)
    valid_ref[...] = jnp.broadcast_to(valid, valid_ref.shape)


def gelu_and_slope(pre):
    root = math.sqrt(2.0 / math.pi)
    square = pre * pre
    bent = jnp.tanh(pre * (root + (root * 0.044715) * square))
    half = 0.5 + 0.5 * bent
    slope = half + (0.5 * pre) * (1.0 - bent * bent) * (root + (3.0 * 0.044715 * root) * square)
    return pre * half, slope


def expert_kernel(
    h2_ref,
    h2_other_ref,
    up_ref,
    up_other_ref,
    w_up_ref,
    w_down_ref,
    hidden_ref,
    dpre_ref,
    dh2_kept_ref,
    dh2_sent_ref,
    rows_ref,
    grads_ref,
    dh2_ref,
):
    count = h2_ref.shape[0]

    @pl.when(pl.program_id(0) == 0)
    def _():
        rows_ref[:count] = h2_ref[...]
        rows_ref[count:] = h2_other_ref[...]
        grads_ref[:count] = up_ref[...]
        grads_ref[count:] = up_other_ref[...]
        dh2_ref[...] = jnp.zeros_like(dh2_ref)

    w_up, w_down = w_up_ref[...], w_down_ref[...]
    pre = dot(rows_ref[...], w_up)
    gelu, slope = gelu_and_slope(pre)
    hidden = gelu.astype(BF16)
    hidden_ref[...] = hidden
    dpre = (dot_nt(grads_ref[...], w_down) * slope).astype(BF16)
    dpre_ref[...] = dpre
    dh2_ref[...] += dot_nt(dpre, w_up)

    @pl.when(pl.program_id(0) == pl.num_programs(0) - 1)
    def _():
        dh2_kept_ref[...] = dh2_ref[:count]
        dh2_sent_ref[...] = dh2_ref[count:].astype(BF16)


def store_sums(sums_ref, upstream, normed):
    for which, total in enumerate((upstream * normed, upstream)):
        total = jnp.sum(total, axis=0, keepdims=True)
        pieces = total.shape[1] // 128
        for at in range(pieces):
            row = which * pieces + at
            sums_ref[row : row + 1] = total[:, at * 128 : (at + 1) * 128]


def norm2_back_kernel(
    kept_ref,
    came_ref,
    resid_ref,
    grad_ref,
    gain_ref,
    dresid_far,
    packed_ref,
    sums_ref,
    dresid_ref,
    sem,
    *,
    cap,
):
    dh2 = kept_ref[...] + came_ref[...].astype(F32)
    normed, inverse = normalise(resid_ref[...])
    dresid = grad_ref[...].astype(F32) + norm_back(dh2, normed, inverse, gain_ref[...])
    dresid_ref[...] = dresid
    leaving = started(dresid_ref, dresid_far, sem)
    slot_of = lax.broadcasted_iota(jnp.int32, (1, dh2.shape[0]), 1)
    pack(packed_ref, dresid.astype(BF16), slot_of, cap, False)
    store_sums(sums_ref, dh2, normed)
    leaving.wait()


def out_grad_kernel(where_ref, own_ref, other_ref, context_far, dattn_ref, *rest):
    piece_fars, (context_ref, grad_ref, piece_ref, sems) = rest[:4], rest[4:]
    arriving = started(context_far, context_ref, sems.at[1])
    half = own_ref.shape[0]
    here = where_ref[0]
    dattn_ref[pl.ds(pl.multiple_of(here * half, half), half), :] = own_ref[...]
    dattn_ref[pl.ds(pl.multiple_of((1 - here) * half, half), half), :] = other_ref[...]
    arriving.wait()
    grad_ref[...] = dot_tn(context_ref[...], dattn_ref[...])
    width = grad_ref.shape[1]
    quarter = grad_ref.shape[0] // 4
    owners = piece_ref.shape[0]
    rows = quarter // owners
    for step in range(4):
        first = (where_ref[1] ^ step) * quarter
        for owner in range(owners):
            start = pl.multiple_of(first + owner * rows, rows)
            block = grad_ref[pl.ds(start, rows), :]
            target_ref = piece_fars[step] if step else piece_ref
            target_ref[owner] = jnp.concatenate(
                [block[:, at : at + 128] for at in range(0, width, 128)], axis=0
            ).astype(BF16)
    started(piece_ref, piece_fars[0], sems.at[0]).wait()


def attend_back_kernel(
    where_ref,
    lengths_ref,
    dattn_ref,
    qkv_far,
    context_far,
    logsum_far,
    w_qkv_far,
    w_out_far,
    kept_ref,
    sent_ref,
    *rest,
    step,
    reach,
    scale,
):
    dvalue_fars, dkq_fars = rest[:4], rest[4:8]
    dcontext_ref, inner_ref, dquery_ref, dqkv_ref = rest[8:12]
    qkv_ref, context_ref, logsum_ref, w_qkv_ref, w_out_ref, sems = rest[12:]
    arriving = [
        started(source, target, sems.at[at])
        for at, (source, target) in enumerate(
            (
                (w_out_far, w_out_ref),
                (context_far, context_ref),
                (qkv_far, qkv_ref),
                (logsum_far, logsum_ref),
                (w_qkv_far, w_qkv_ref),
            )
        )
    ]
    half = kept_ref.shape[0]
    span = 2 * half
    here = where_ref[0]
    own_start = pl.multiple_of(here * half, half)
    other_start = pl.multiple_of((1 - here) * half, half)
    arriving[0].wait()
    dcontext = dot_nt(dattn_ref[...], w_out_ref[...]).astype(BF16)
    dcontext_ref[...] = dcontext
    arriving[1].wait()
    arriving[2].wait()
    arriving[3].wait()
    heads = qkv_ref.shape[2] // HEAD_DIM
    columns_all = qkv_ref.shape[2]
    product = dcontext.astype(F32) * context_ref[...].astype(F32)
    coarse = product.astype(BF16)
    fine = (product - coarse.astype(F32)).astype(BF16)
    of_head = (
        lax.broadcasted_iota(jnp.int32, (16, columns_all), 1) // HEAD_DIM
        == lax.broadcasted_iota(jnp.int32, (16, columns_all), 0)
    ).astype(BF16)
    inner_ref[...] = dot_nt(of_head, coarse) + dot_nt(of_head, fine)
    dquery_ref[...] = jnp.zeros_like(dquery_ref)
    for start in range(0, span, step):
        stop = start + step
        high = min(span, stop + reach)
        shape = (step, high - start)
        key_at = lax.broadcasted_iota(jnp.int32, shape, 0) + start
        query_at = lax.broadcasted_iota(jnp.int32, shape, 1) + start
        allowed = (segments(lengths_ref, query_at) == segments(lengths_ref, key_at)) & (
            key_at <= query_at
        )
        allowed = jnp.concatenate([allowed.astype(F32)] * heads, axis=0) > 0.5
        lane = lax.broadcasted_iota(jnp.int32, (step, 2 * HEAD_DIM), 1)
        pairs = [
            slice(at, at + 2 * HEAD_DIM) for at in range(0, heads * HEAD_DIM, 2 * HEAD_DIM)
        ]
        keys = [two_heads(qkv_ref[1, start:stop, columns]) for columns in pairs]

        def by_head(ref, start=start, high=high):
            return jnp.concatenate(
                [
                    jnp.broadcast_to(ref[head : head + 1, start:high], (step, high - start))
                    for head in range(heads)
                ],
                axis=0,
            )

        scores = jnp.concatenate(
            [
                dot_nt(keys[at], qkv_ref[0, start:high, columns])
                for at, columns in enumerate(pairs)
            ],
            axis=0,
        )
        probs = jnp.exp(jnp.where(allowed, scores * scale - by_head(logsum_ref), -1e30))
        dprobs = jnp.concatenate(
            [
                dot_nt(two_heads(qkv_ref[2, start:stop, columns]), dcontext_ref[start:high, columns])
                for columns in pairs
            ],
            axis=0,
        )
        dscores = (probs * (dprobs - by_head(inner_ref))).astype(BF16)
        probs = probs.astype(BF16)
        for at, columns in enumerate(pairs):
            mine = slice(2 * at * step, 2 * (at + 1) * step)
            dvalues = dot(probs[mine], dcontext_ref[start:high, columns])
            dkeys = dot(dscores[mine], qkv_ref[0, start:high, columns])
            dquery_ref[start:high, columns] += dot_tn(dscores[mine], keys[at])
            dqkv_ref[1, start:stop, columns] = (
                jnp.where(lane < HEAD_DIM, dkeys[:step], dkeys[step:]) * scale
            ).astype(BF16)
            dqkv_ref[2, start:stop, columns] = jnp.where(
                lane < HEAD_DIM, dvalues[:step], dvalues[step:]
            ).astype(BF16)
    dqkv_ref[0] = (dquery_ref[...] * scale).astype(BF16)

    quarter = columns_all // 4
    leaving = []
    for kind, at in ((2, 1), (2, 2), (2, 3), (1, 1), (0, 1), (1, 2), (0, 2), (1, 3), (0, 3), (2, 0), (1, 0), (0, 0)):
        first = pl.multiple_of((where_ref[1] ^ at) * quarter, quarter)
        target = dvalue_fars[at] if kind == 2 else dkq_fars[at].at[1 - kind]
        leaving.append(
            started(dqkv_ref.at[kind, :, pl.ds(first, quarter)], target, sems.at[5 + kind * 4 + at])
        )
    arriving[4].wait()

    def back_rows(start):
        total = dot_nt(dqkv_ref[0, pl.ds(start, half), :], w_qkv_ref[0])
        total = total + dot_nt(dqkv_ref[1, pl.ds(start, half), :], w_qkv_ref[1])
        return total + dot_nt(dqkv_ref[2, pl.ds(start, half), :], w_qkv_ref[2])

    sent_ref[...] = back_rows(other_start).astype(BF16)
    kept_ref[...] = back_rows(own_start)
    for copy in leaving:
        copy.wait()


def token_grad(where_ref, grad_refs, index, input_ref, own_refs, other_refs):
    half = own_refs[0].shape[0]
    own_start = pl.multiple_of(where_ref[0] * half, half)
    other_start = pl.multiple_of((1 - where_ref[0]) * half, half)

    def rows(ref, start, count):
        return ref[pl.ds(start, count), :] if index is None else ref[index, pl.ds(start, count), :]

    total = dot_tn(rows(grad_refs[0], 0, 2 * half), input_ref[...])
    for grad_ref, own_ref, other_ref in zip(grad_refs[1:], own_refs, other_refs):
        total = total + dot_tn(rows(grad_ref, own_start, half), own_ref[...])
        total = total + dot_tn(rows(grad_ref, other_start, half), other_ref[...])
    return total.T


def store_halves(where_ref, bit, half_refs, load, at):
    rows = at.stop - at.start
    for side, half_ref in enumerate(half_refs):
        mine = ((where_ref[2] >> bit) & 1) ^ side
        for index in range(half_ref.shape[0]):
            half_ref[index, at] = load(2 * index + mine, rows).astype(BF16)


def value_grad_kernel(where_ref, *refs):
    grad_refs, input_ref, own_refs, other_refs = refs[0:4], refs[4], refs[5:8], refs[8:11]
    out_refs, half_refs, total_ref = refs[11:15], refs[15:17], refs[17]
    total_ref[...] = token_grad(where_ref, grad_refs, None, input_ref, own_refs, other_refs)
    rows = half_refs[0].shape[1] // 2
    store_halves(
        where_ref, 0, half_refs,
        lambda owner, rows: sum(ref[owner].astype(F32) for ref in out_refs), slice(0, rows),
    )
    store_halves(
        where_ref, 0, half_refs,
        lambda owner, rows: total_ref[pl.ds(pl.multiple_of(owner * rows, rows), rows), :],
        slice(rows, 2 * rows),
    )


def key_query_grad_kernel(where_ref, *refs):
    grad_refs, input_ref, own_refs, other_refs = refs[0:4], refs[4], refs[5:8], refs[8:11]
    half_refs, total_ref = refs[11:13], refs[13]
    rows = half_refs[0].shape[1] // 2
    for index in range(2):
        total_ref[...] = token_grad(where_ref, grad_refs, index, input_ref, own_refs, other_refs)
        store_halves(
            where_ref, 0, half_refs,
            lambda owner, rows: total_ref[pl.ds(pl.multiple_of(owner * rows, rows), rows), :],
            slice(index * rows, (index + 1) * rows),
        )


def add_kernel(where_ref, kept_ref, came_ref, *half_refs, bit):
    store_halves(
        where_ref, bit, half_refs,
        lambda owner, rows: kept_ref[owner].astype(F32) + came_ref[owner].astype(F32),
        slice(0, kept_ref.shape[1]),
    )


def last_add_kernel(kept_ref, came_ref, out_ref):
    out_ref[...] = (kept_ref[0].astype(F32) + came_ref[0].astype(F32)).astype(BF16)


def split_store(out_ref, start, value):
    rows = value.shape[0]
    coarse = value.astype(BF16)
    out_ref[start : start + rows] = coarse
    out_ref[start + rows : start + 2 * rows] = (value - coarse.astype(F32)).astype(BF16)


def last_add_sums_kernel(kept_ref, came_ref, *refs):
    out_ref = refs[4]
    rows = kept_ref.shape[1]
    out_ref[:rows] = (kept_ref[0].astype(F32) + came_ref[0].astype(F32)).astype(BF16)
    sums = jnp.concatenate([refs[0][...] + refs[1][...], refs[2][...] + refs[3][...]], axis=0)
    split_store(out_ref, rows, sums)


def split_sum(refs, start, stop):
    rows = (stop - start) // 2
    return sum(
        ref[start : start + rows].astype(F32) + ref[start + rows : stop].astype(F32)
        for ref in refs
    )


def stack_kernel(own_ref, came_ref, out_ref, *, sums):
    rows = own_ref.shape[0] - sums
    out_ref[:rows] = own_ref[:rows]
    out_ref[rows : 2 * rows] = came_ref[:rows]
    if sums:
        split_store(out_ref, 2 * rows, split_sum((own_ref, came_ref), rows, rows + sums))


def place_rows(where_ref, digits, at):
    bits = 2 * (digits - 1)
    return where_ref[2] ^ sum(((at >> bit) & 1) << (bits - 1 - bit) for bit in range(bits))


def each_piece(where_ref, refs, digits, rows, use, steps=range(4)):
    owners = 4 ** (digits - 1)
    for step in steps:
        column = where_ref[1] ^ step
        for at in range(owners):
            owner = place_rows(where_ref, digits, at)
            first = at * 2 * rows

            def load(low, high, first=first, step=step):
                if step < 3:
                    return refs[step][first + low : first + high]
                middle = refs[3].shape[0]
                start, stop = first + low, first + high
                if stop <= middle:
                    return refs[3][start:stop]
                if start >= middle:
                    return refs[4][start - middle : stop - middle]
                return jnp.concatenate([refs[3][start:middle], refs[4][: stop - middle]], axis=0)

            use(column, owner, load)


def out_value_pieces(where_ref, refs, digits, steps, value_ref, value_column, out_ref, out_first):
    width = value_ref.shape[1]
    rows = width // 4 ** (digits - 1)
    few = rows * 128 // width

    def use(column, owner, load):
        start = pl.multiple_of(out_first(column) + owner * few, few)
        out_ref[pl.ds(start, few), :] = jnp.concatenate(
            [load(at, at + few).astype(F32) for at in range(0, rows, few)], axis=1
        )
        lanes = pl.ds(pl.multiple_of(value_column(column), 128), 128)
        value_ref[0, pl.ds(pl.multiple_of(owner * rows, rows), rows), lanes] = load(
            rows, 2 * rows
        ).astype(F32)

    each_piece(where_ref, refs, digits, rows, use, steps)


def finish_out_value_near_kernel(where_ref, *refs, digits):
    value_ref, out_ref = refs[3:]

    def place(column):
        return column * 128

    out_value_pieces(where_ref, refs[:3], digits, range(3), value_ref, place, out_ref, place)


def finish_out_value_far_kernel(where_ref, *refs, digits):
    halves, (_, _, value_far, out_far, value_ref, out_ref, sems) = refs[:2], refs[2:]
    out_value_pieces(
        where_ref, (None, None, None, *halves), digits, range(3, 4),
        value_ref, lambda column: 0, out_ref, lambda column: 0,
    )
    first = pl.ds(pl.multiple_of((where_ref[1] ^ 3) * 128, 128), 128)
    leaving = [
        started(value_ref, value_far.at[pl.ds(2, 1), :, first], sems.at[0]),
        started(out_ref, out_far.at[first], sems.at[1]),
    ]
    for copy in leaving:
        copy.wait()


def finish_near_kernel(where_ref, *refs, digits, sums):
    qkv_ref, sums_ref = refs[4:]
    width = qkv_ref.shape[1]
    owners = 4 ** (digits - 1)
    rows = width // owners
    for step in range(3):
        lanes = pl.ds(pl.multiple_of((where_ref[1] ^ step) * 128, 128), 128)
        for at in range(owners):
            owner = place_rows(where_ref, digits, at)
            down = pl.ds(pl.multiple_of(owner * rows, rows), rows)
            start = pl.multiple_of((2 * at + 1 - pl.program_id(0)) * rows, rows)
            qkv_ref[0, down, lanes] = refs[step][pl.ds(start, rows), :].astype(F32)
    total = refs[0].shape[0]
    sums_ref[...] = split_sum(refs[:3], total - sums, total)


def finish_far_kernel(where_ref, *refs, digits, sums):
    halves, near_sums_ref, _, qkv_far, *sums_refs, total_ref, sem = refs[:2], *refs[2:]
    width = total_ref.shape[1]
    rows = width // 4 ** (digits - 1)

    def use(column, owner, load):
        down = pl.ds(pl.multiple_of(owner * rows, rows), rows)
        total_ref[1, down, :] = load(0, rows).astype(F32)
        total_ref[0, down, :] = load(rows, 2 * rows).astype(F32)

    each_piece(where_ref, (None, None, None, *halves), digits, rows, use, range(3, 4))
    lanes = pl.ds(pl.multiple_of((where_ref[1] ^ 3) * 128, 128), 128)
    leaving = started(total_ref, qkv_far.at[pl.ds(0, 2), :, lanes], sem)
    half = halves[1].shape[0]
    total_sums = near_sums_ref[...] + split_sum(halves[1:], half - sums, half)
    count = total_sums.shape[0] // len(sums_refs)
    for at, sums_ref in enumerate(sums_refs):
        sums_ref[...] = total_sums[at * count : (at + 1) * count]
    leaving.wait()


def expert_grad_kernel(rows_ref, grads_ref, hidden_ref, dpre_ref, up_ref, down_ref, turned_ref):
    @pl.when(pl.program_id(0) == 0)
    def _():
        turned_ref[...] = rows_ref[...].T

    up_ref[...] = dot(turned_ref[...], dpre_ref[...])
    down_ref[...] = dot_tn(hidden_ref[...], grads_ref[...])


def branch_kernel(hidden_ref, w_down_ref, kept_ref, sent_ref, branch_ref):
    @pl.when(pl.program_id(0) == 0)
    def _():
        branch_ref[...] = jnp.zeros_like(branch_ref)

    branch_ref[...] += dot(hidden_ref[...], w_down_ref[...])

    @pl.when(pl.program_id(0) == pl.num_programs(0) - 1)
    def _():
        count = kept_ref.shape[0]
        kept_ref[...] = branch_ref[:count].astype(BF16)
        sent_ref[...] = branch_ref[count:].astype(BF16)


def norm1_back_kernel(packed_ref, x_ref, dresid_ref, gain_ref, out_ref, sums_ref, *, cap):
    count, width = x_ref.shape
    dh1 = unpack(packed_ref, slots_down(count), cap, width)
    normed, inverse = normalise(x_ref[...].astype(F32))
    out_ref[...] = dresid_ref[...] + norm_back(dh1, normed, inverse, gain_ref[...])
    store_sums(sums_ref, dh1, normed)


VMEM = pl.BlockSpec(memory_space=pltpu.VMEM)
SMEM = pl.BlockSpec(memory_space=pltpu.SMEM)


def after(value, *others):
    return lax.optimization_barrier((value, *others))[0]


def far(value):
    return pltpu.with_memory_space_constraint(value, pltpu.HBM)


def call(kernel, name, outs, args, flops, scalars=0, scratch=(), limit=16, away=(), out_away=(), raw=(), out_raw=()):
    shapes = [
        pltpu.HBM(shape, kind)
        if at in out_away or at in out_raw
        else jax.ShapeDtypeStruct(shape, kind)
        for at, (shape, kind) in enumerate(outs)
    ]

    def spec(at, away, raw):
        if at in raw:
            return pl.BlockSpec(memory_space=pltpu.HBM)
        return pl.BlockSpec() if at in away else VMEM

    size = sum(math.prod(a.shape) * a.dtype.itemsize for a in (*args, *shapes))
    return pl.pallas_call(
        kernel,
        name=name,
        out_shape=shapes,
        in_specs=[
            SMEM if at < scalars else spec(at, away, raw) for at in range(len(args))
        ],
        out_specs=[spec(at, out_away, out_raw) for at in range(len(outs))],
        scratch_shapes=list(scratch),
        cost_estimate=pl.CostEstimate(flops=flops, bytes_accessed=size, transcendentals=0),
        compiler_params=pltpu.CompilerParams(vmem_limit_bytes=limit * MIB),
    )(*[far(value) if at in away or at in raw else value for at, value in enumerate(args)])


def expert(h2, h2_other, upstream, upstream_other, w_up, w_down):
    count, width = h2.shape
    units = w_up.shape[1]
    tile = min(512, units)
    shapes = [
        ((2 * count, units), BF16),
        ((2 * count, units), BF16),
        ((count, width), F32),
        ((count, width), BF16),
        ((2 * count, width), BF16),
        ((2 * count, width), BF16),
    ]
    stay = (2, 3)
    both = pl.BlockSpec((2 * count, width), lambda j: (0, 0))
    rows = pl.BlockSpec((count, width), lambda j: (0, 0))
    by_unit = pl.BlockSpec((2 * count, tile), lambda j: (0, j))
    return pl.pallas_call(
        expert_kernel,
        name="expert",
        grid=(units // tile,),
        out_shape=[
            jax.ShapeDtypeStruct(shape, kind) if at in stay else pltpu.HBM(shape, kind)
            for at, (shape, kind) in enumerate(shapes)
        ],
        in_specs=[rows] * 4
        + [
            pl.BlockSpec((width, tile), lambda j: (0, j)),
            pl.BlockSpec((tile, width), lambda j: (j, 0)),
        ],
        out_specs=[by_unit, by_unit, rows, rows, both, both],
        scratch_shapes=[
            pltpu.VMEM((2 * count, width), F32),
        ],
        cost_estimate=pl.CostEstimate(
            flops=12 * count * width * units, bytes_accessed=16 * MIB, transcendentals=0
        ),
        compiler_params=pltpu.CompilerParams(vmem_limit_bytes=40 * MIB),
    )(h2, h2_other, upstream, upstream_other, w_up, w_down)


def expert_grads(rows, grads, hidden, dpre):
    count, width = rows.shape
    units = hidden.shape[1]
    tile = min(512, units)
    whole = pl.BlockSpec((count, width), lambda j: (0, 0))
    by_unit = pl.BlockSpec((count, tile), lambda j: (0, j))
    return pl.pallas_call(
        expert_grad_kernel,
        name="expert_grads",
        grid=(units // tile,),
        out_shape=[pltpu.HBM((width, units), F32), pltpu.HBM((units, width), F32)],
        in_specs=[whole] * 2 + [by_unit] * 2,
        out_specs=[
            pl.BlockSpec((width, tile), lambda j: (0, j)),
            pl.BlockSpec((tile, width), lambda j: (j, 0)),
        ],
        scratch_shapes=[pltpu.VMEM((width, count), BF16)],
        cost_estimate=pl.CostEstimate(
            flops=4 * count * width * units, bytes_accessed=24 * MIB, transcendentals=0
        ),
        compiler_params=pltpu.CompilerParams(vmem_limit_bytes=40 * MIB),
    )(far(rows), far(grads), far(hidden), far(dpre))


def expert_branch(hidden, w_down):
    count, units = hidden.shape
    width = w_down.shape[1]
    tile = min(512, units)
    half = pl.BlockSpec((count // 2, width), lambda j: (0, 0))
    return pl.pallas_call(
        branch_kernel,
        name="expert_branch",
        grid=(units // tile,),
        out_shape=[pltpu.HBM((count // 2, width), BF16)] * 2,
        in_specs=[
            pl.BlockSpec((count, tile), lambda j: (0, j)),
            pl.BlockSpec((tile, width), lambda j: (j, 0)),
        ],
        out_specs=[half, half],
        scratch_shapes=[pltpu.VMEM((count, width), F32)],
        cost_estimate=pl.CostEstimate(
            flops=2 * count * width * units, bytes_accessed=8 * MIB, transcendentals=0
        ),
        compiler_params=pltpu.CompilerParams(vmem_limit_bytes=20 * MIB),
    )(far(hidden), far(w_down))


def flip(value, axis, bit):
    size = lax.axis_size(axis)
    return lax.ppermute(value, axis, [(i, i ^ bit) for i in range(size)])


def to_others(values, digit):
    return [
        flip(values[m] if isinstance(values, (list, tuple)) else values, "exp", m << (2 * digit))
        for m in range(1, 4)
    ]


def after_all(values, *others):
    return list(lax.optimization_barrier((*values, *others))[: len(values)])


def sum_and_spread(first, second, where, digits, sums, extra, finish_near, finish_far, first_wait, filler):
    bits = 2 * (digits - 1)

    def across(value, bit):
        return flip(value, "exp", 4 << bit)

    def add(halves, came, bit, sums=None):
        owners, rows, columns = came.shape
        if bit + 1 < bits:
            return call(
                functools.partial(add_kernel, bit=bit + 1), "add",
                [((owners // 2, rows, columns), BF16)] * 2, [where, halves[0], came], 0, scalars=1,
            )
        if sums is None:
            return call(
                last_add_kernel, "last_add", [((rows, columns), BF16)], [halves[0], came], 0,
            )
        return call(
            last_add_sums_kernel, "last_add_sums", [((rows + extra, columns), BF16)],
            [halves[0], came, *sums], 0,
        )

    def stack(own, came, sums):
        rows, columns = own.shape
        return call(
            functools.partial(stack_kernel, sums=sums), "stack",
            [((2 * rows - sums, columns), BF16)], [own, came], 0,
        )[0]

    def steps(halves, sums, extra):
        for bit in range(bits):
            came = yield halves[1], [across(halves[1], bit)]
            halves = add(halves, came[0], bit, sums)
        total = halves[0]
        for bit in reversed(range(bits)):
            came = yield total, [across(total, bit)]
            total = stack(total, came[0], extra)
        by_x, by_y = yield total, [flip(total, "exp", 1), flip(total, "exp", 2)]
        if extra == 0:
            near.extend(finish_near(total, by_x, by_y))
        middle = total.shape[0] // 2
        sent = [by_y[:middle], by_x[middle:]]
        halves = yield sent[0], [flip(sent[0], "exp", 1), flip(sent[1], "exp", 2)]
        yield None, [total, by_x, by_y, *halves]

    near = []
    lines, states, last, finished = [steps(first, None, 0), None], [None, None], first_wait, None
    states[0] = next(lines[0])
    for at, line in enumerate([0] + [0, 1] * (2 * bits + 1) + [1]):
        if at == 1:
            pieces = second(last)
            lines[1], last = steps(pieces, sums, extra), pieces[1]
            states[1] = next(lines[1])
        ahead = [*near[1:], filler] if line == 0 and near else []
        states[line] = lines[line].send(after_all(states[line][1], last, *ahead))
        last = states[line][0]
        if line == 0 and last is None:
            finished = finish_far(*states[0][1][3:], *near)
            last = states[0][1][3]
        elif finished is not None:
            last = finished[1]
    return finished, states[1][1]


def on_device(
    block_input,
    dispatch,
    lengths,
    ln1_gain,
    ln1_bias,
    ln2_gain,
    ln2_bias,
    w_qkv,
    w_out,
    w_up,
    w_down,
    grad_output,
):
    slots, width = block_input.shape
    seq_rows = dispatch.shape[0]
    n_exp = lax.axis_size("exp")
    devices = n_exp * lax.axis_size("head")
    cap = slots // devices
    span = 2 * seq_rows
    columns = w_qkv.shape[2]
    scale = 1.0 / math.sqrt(HEAD_DIM)
    digits = (n_exp.bit_length() - 1) // 2
    place = lax.axis_index("exp")
    where = jnp.stack(
        [lax.axis_index("head"), place & 3, place >> 2]
    ).astype(jnp.int32)
    step = 128
    reach = 3 * seq_rows // 4
    packed = ((devices * 8, cap * 128), BF16)
    moving = 2 * devices * 8 * max(slots, seq_rows) * width * 3
    gain1, bias1 = ln1_gain.reshape(1, width), ln1_bias.reshape(1, width)
    gain2, bias2 = ln2_gain.reshape(1, width), ln2_bias.reshape(1, width)
    along = dispatch.reshape(1, seq_rows)

    def exchange(value):
        value = value.reshape(devices, 8, cap * 128)
        value = lax.all_to_all(value, ("exp", "head"), split_axis=0, concat_axis=0, tiled=True)
        return value.reshape(devices * 8, cap * 128)

    def cross(value):
        return flip(value, "head", 1)

    (h1,) = call(
        functools.partial(norm1_kernel, cap=cap), "norm1", [packed],
        [block_input, gain1, bias1], moving, away=(0, 1, 2),
    )
    arrived = exchange(h1)
    (own,) = call(
        functools.partial(gather_kernel, cap=cap), "gather1", [((seq_rows, width), BF16)],
        [arrived, along], moving,
    )
    other = cross(own)
    own_copy, inputs, qkv, context, logsum, attn_kept, attn_sent = call(
        functools.partial(attend_kernel, step=step, reach=reach, scale=scale),
        "attend",
        [
            ((seq_rows, width), BF16),
            ((span, width), BF16),
            ((3, span, columns), BF16),
            ((span, columns), BF16),
            ((128, span), F32),
            ((seq_rows, width), F32),
            ((seq_rows, width), BF16),
        ],
        [where, lengths, own, other, w_qkv, w_out],
        2 * span * width * columns * 4 + 16 * span * span * columns,
        scalars=2,
        limit=24,
        raw=(4, 5),
        out_raw=range(5),
        scratch=[
            pltpu.VMEM((3, width, columns), BF16),
            pltpu.VMEM((columns, width), BF16),
            pltpu.VMEM((span, width), BF16),
            pltpu.VMEM((3, span, columns), BF16),
            pltpu.VMEM((span, columns), BF16),
            pltpu.VMEM((128, span), F32),
            pltpu.SemaphoreType.DMA((9,)),
        ],
    )
    (sent,) = call(
        functools.partial(scatter_kernel, cap=cap, fill=True), "scatter1", [packed],
        [attn_kept, cross(attn_sent), along], moving,
    )
    attn_back = exchange(sent)
    by_xy = flip(after(own_copy, attn_back), "exp", 3)
    resid, h2, upstream, valid = call(
        functools.partial(norm2_kernel, cap=cap),
        "norm2",
        [((slots, width), F32), ((slots, width), BF16), ((slots, width), BF16), ((slots, 128), F32)],
        [attn_back, block_input, grad_output, gain2, bias2],
        moving,
    )
    h2_other, upstream_other = cross(h2), cross(upstream)
    hidden, dpre, dh2_kept, dh2_sent, rows_all, grads_all = expert(
        h2, h2_other, upstream, upstream_other, w_up[0], w_down[0]
    )
    dh2_sent = after(dh2_sent, by_xy)
    dresid, sent, sums2 = call(
        functools.partial(norm2_back_kernel, cap=cap),
        "norm2_back",
        [((slots, width), F32), packed, ((width // 64, 128), F32)],
        [dh2_kept, cross(dh2_sent), resid, grad_output, gain2],
        moving,
        out_raw=(0,),
        scratch=[pltpu.VMEM((slots, width), F32), pltpu.SemaphoreType.DMA],
    )
    arrived = exchange(sent)
    near_own, hidden, far_own = after_all([own_copy, hidden, by_xy], sent)
    by_x, by_y = flip(near_own, "exp", 1), flip(near_own, "exp", 2)
    far_other = cross(far_own)
    grad_up, grad_down = expert_grads(rows_all, grads_all, hidden, dpre)
    arrived, grad_up, grad_down, by_x, by_y, far_other = lax.optimization_barrier(
        (arrived, grad_up, grad_down, by_x, by_y, far_other)
    )
    plane_own = [by_x, by_y, far_own]
    plane_other = [cross(by_x), cross(by_y), far_other]
    (own,) = call(
        functools.partial(gather_kernel, cap=cap), "gather2", [((seq_rows, width), BF16)],
        [arrived, along], moving,
    )
    other = cross(own)
    piece = 4 * width // n_exp
    dattn, *out_pieces = call(
        out_grad_kernel,
        "out_grad",
        [((span, width), BF16), *[((n_exp // 4, piece, 128), BF16)] * 4],
        [where, own, other, context],
        2 * span * width * columns,
        scalars=1,
        scratch=[
            pltpu.VMEM((span, columns), BF16),
            pltpu.VMEM((columns, width), F32),
            pltpu.VMEM((n_exp // 4, piece, 128), BF16),
            pltpu.SemaphoreType.DMA((2,)),
        ],
        raw=(3,),
        out_raw=(1,),
    )
    out_parts = [out_pieces[0], *to_others(out_pieces, 0)]
    du_kept, du_sent, *parts = call(
        functools.partial(attend_back_kernel, step=step, reach=reach, scale=scale),
        "attend_back",
        [
            ((seq_rows, width), F32),
            ((seq_rows, width), BF16),
            *[((span, 128), BF16)] * 4,
            *[((2, span, 128), BF16)] * 4,
        ],
        [where, lengths, dattn, qkv, context, logsum, w_qkv, w_out],
        2 * span * width * columns * 4 + 40 * span * span * columns,
        scalars=2,
        limit=24,
        raw=range(3, 8),
        out_raw=range(2, 10),
        scratch=[
            pltpu.VMEM((span, columns), BF16),
            pltpu.VMEM((16, span), F32),
            pltpu.VMEM((span, columns), F32),
            pltpu.VMEM((3, span, columns), BF16),
            pltpu.VMEM((3, span, columns), BF16),
            pltpu.VMEM((span, columns), BF16),
            pltpu.VMEM((128, span), F32),
            pltpu.VMEM((3, width, columns), BF16),
            pltpu.VMEM((columns, width), BF16),
            pltpu.SemaphoreType.DMA((17,)),
        ],
    )
    du_sent, *parts = after_all([du_sent, *parts], *out_parts[1:], *plane_other)
    value_parts = [parts[0], *to_others(parts[:4], 0)]
    key_query_parts = [parts[4], *to_others(after_all(parts[4:], *value_parts[1:]), 0)]
    (sent,) = call(
        functools.partial(scatter_kernel, cap=cap, fill=False), "scatter2", [packed],
        [du_kept, cross(du_sent), along], moving,
    )
    arrived = exchange(after(sent, *value_parts[1:]))
    input_grad, sums1 = call(
        functools.partial(norm1_back_kernel, cap=cap),
        "norm1_back",
        [((slots, width), F32), ((width // 64, 128), F32)],
        [arrived, block_input, dresid, gain1],
        moving,
        away=(1, 2, 3),
        out_away=(0,),
    )
    tokens = [inputs, *after_all([*plane_own, *plane_other], du_sent)]
    split = [((n_exp // 8, 2 * piece, 128), BF16)] * 2
    product = 8 * span * width * 128
    out_value = call(
        value_grad_kernel, "value_grad", split, [where, *value_parts, *tokens, *out_parts],
        product, scalars=1, scratch=[pltpu.VMEM((width, 128), F32)], away=(1, *range(5, 13)),
    )
    branch_kept, branch_sent = expert_branch(after(hidden, out_value[1]), w_down[0])
    branch_came = cross(branch_sent)
    branch = branch_kept.astype(F32) + branch_came.astype(F32)
    result = (resid + valid[:, :1] * branch).astype(BF16)

    def key_query(last):
        came = after_all(key_query_parts[1:], last)
        return call(
            key_query_grad_kernel, "key_query_grad", split,
            [where, key_query_parts[0], *came, *tokens], 2 * product, scalars=1,
            scratch=[pltpu.VMEM((width, 128), F32)], away=(1, *range(5, 12)),
        )

    sums = [sums1, cross(sums1), sums2, cross(sums2)]
    extra = 4 * sums1.shape[0]
    whole_qkv = pltpu.HBM((3, width, columns), F32)
    whole_out = pltpu.HBM((columns, width), F32)
    in_place = pl.BlockSpec(memory_space=pltpu.HBM)
    finish_near = pl.pallas_call(
        functools.partial(finish_out_value_near_kernel, digits=digits),
        name="finish_out_value_near",
        grid=(1,),
        out_shape=[whole_qkv, whole_out],
        in_specs=[SMEM] + [VMEM] * 3,
        out_specs=[
            pl.BlockSpec((1, width, columns), lambda i: (2, 0, 0)),
            pl.BlockSpec((columns, width), lambda i: (0, 0)),
        ],
        cost_estimate=pl.CostEstimate(flops=0, bytes_accessed=6 * MIB, transcendentals=0),
        compiler_params=pltpu.CompilerParams(vmem_limit_bytes=20 * MIB),
    )
    finish_far = pl.pallas_call(
        functools.partial(finish_out_value_far_kernel, digits=digits),
        name="finish_out_value_far",
        out_shape=[whole_qkv, whole_out],
        in_specs=[SMEM] + [VMEM] * 2 + [in_place] * 2,
        out_specs=[in_place] * 2,
        scratch_shapes=[
            pltpu.VMEM((1, width, 128), F32),
            pltpu.VMEM((128, width), F32),
            pltpu.SemaphoreType.DMA((2,)),
        ],
        input_output_aliases={3: 0, 4: 1},
        cost_estimate=pl.CostEstimate(flops=0, bytes_accessed=2 * MIB, transcendentals=0),
        compiler_params=pltpu.CompilerParams(vmem_limit_bytes=16 * MIB),
    )
    (grad_qkv, grad_out), key_query = sum_and_spread(
        out_value, key_query, where, digits, sums, extra, functools.partial(finish_near, where),
        functools.partial(finish_far, where), branch_sent, result,
    )
    sums_shape = jax.ShapeDtypeStruct((extra // 2, 128), F32)
    grad_qkv, sums = pl.pallas_call(
        functools.partial(finish_near_kernel, digits=digits, sums=extra),
        name="finish_near",
        grid=(2,),
        out_shape=[whole_qkv, sums_shape],
        in_specs=[SMEM] + [VMEM] * 3 + [in_place],
        out_specs=[
            pl.BlockSpec((1, width, columns), lambda i: (i, 0, 0)),
            pl.BlockSpec((extra // 2, 128), lambda i: (0, 0)),
        ],
        input_output_aliases={4: 0},
        cost_estimate=pl.CostEstimate(flops=0, bytes_accessed=6 * MIB, transcendentals=0),
        compiler_params=pltpu.CompilerParams(vmem_limit_bytes=20 * MIB),
    )(where, *key_query[:3], grad_qkv)
    halves = after_all(key_query[3:], sums)
    grad_qkv, *sums = pl.pallas_call(
        functools.partial(finish_far_kernel, digits=digits, sums=extra),
        name="finish_far",
        out_shape=[whole_qkv, *[jax.ShapeDtypeStruct((width // 128, 128), F32)] * 4],
        in_specs=[SMEM] + [VMEM] * 3 + [in_place],
        out_specs=[in_place, *[VMEM] * 4],
        scratch_shapes=[pltpu.VMEM((2, width, 128), F32), pltpu.SemaphoreType.DMA],
        input_output_aliases={4: 0},
        cost_estimate=pl.CostEstimate(flops=0, bytes_accessed=2 * MIB, transcendentals=0),
        compiler_params=pltpu.CompilerParams(vmem_limit_bytes=16 * MIB),
    )(where, *halves, sums, grad_qkv)
    sums = [total.reshape(width) for total in sums]
    return (
        result,
        input_grad,
        sums[0],
        sums[1],
        sums[2],
        sums[3],
        grad_qkv,
        grad_out,
        grad_up[None],
        grad_down[None],
    )


def solution(mesh):
    placed = (
        P(("exp", "head"), None),
        P(("exp", "head")),
        P("exp", None),
        P(),
        P(),
        P(),
        P(),
        P(None, None, "head"),
        P("head", None),
        P("exp", None, "head"),
        P("exp", "head", None),
        P(("exp", "head"), None),
    )
    return jax.shard_map(
        on_device,
        mesh=mesh,
        in_specs=placed,
        out_specs=(
            P(("exp", "head"), None),
            P(("exp", "head"), None),
            P(),
            P(),
            P(),
            P(),
            P(None, None, "head"),
            P("head", None),
            P("exp", None, "head"),
            P("exp", "head", None),
        ),
        check_vma=False,
    )
```
